32 devices in a mesh: row: 4 (over z), col: 8 (over y, x, core).
Axes of the slice: x: 2, y: 2, z: 4, core: 2. Of those that a mesh axis runs over, the one named last changes fastest.
Arguments:
- query_tokens: bfloat16 [128, 32, 128], P('row'), may hold values from -14 to 14
- query_lengths: int32 [128], P('row'), may hold values from 8 to 32
- passage_tokens: bfloat16 [1024, 176, 128], P(('col', 'row')), may hold values from -8 to 8
- passage_lengths: int32 [1024], P(('col', 'row')), may hold values from 44 to 176
- student_queries: bfloat16 [128, 768], P('row', 'col'), may hold values from -28 to 28
- student_passages: bfloat16 [1024, 768], P('col', 'row'), may hold values from -0.21875 to 0.21875
- positives: int32 [128], P('row'), may hold values from 0 to 1023
Outputs:
- query_grads: float32 [128, 768], P('row', 'col')
- passage_grads: float32 [1024, 768], P('col', 'row')
- loss: float32 [], replicated
The draws below stay inside these ranges and needn't reach their ends.
All inputs are finite; a program needn't handle non-finite values.
Results may differ from the reference program's by a relative error of at most 0.00045.
Values may be sent and summed in bfloat16 or wider, within the bound.
No kernel may reach another device: no remote copies, remote signals or barrier semaphores. Data moves between devices by JAX's collectives and lax.ppermute only.
A program may use at most 64 MiB of HBM per device.

```python
import math
import jax
import jax.numpy as jnp
from jax import lax

LQ = 32
LP = 176
E = 128
DS = 768
Q = 128
P_SIZE = 1024


def token_base(key, scale_span):
    normal_key = jax.random.fold_in(key, 0)
    scale_key = jax.random.fold_in(key, 2)
    normal_values = jnp.clip(jax.random.normal(normal_key, (Q, LQ, E), jnp.float32), -6.0, 6.0)
    values = normal_values
    scales = jnp.exp(jax.random.uniform(scale_key, (Q, 1, 1), jnp.float32, 0.0, math.log(scale_span)))
    return (values, scales)


def draw_query_tokens(key, part):
    values, scales = token_base(key, 1.0)
    return (values * scales).astype(jnp.bfloat16)


def draw_passage_tokens(key, part):
    values, scales = token_base(key, 1.0)
    low_level = 0.8
    high_level = 1.25
    key = jax.random.fold_in(key, 37)
    noise_key, level_key, owner_key, source_key, target_key, strength_key = jax.random.split(key, 6)
    background = jnp.clip(jax.random.normal(noise_key, (P_SIZE, LP, E), jnp.float32), -6.0, 6.0) / math.sqrt(E)
    levels = jnp.exp(jax.random.uniform(level_key, (P_SIZE, 1, 1), jnp.float32, math.log(low_level), math.log(high_level)))
    owner_query = jax.random.randint(owner_key, (P_SIZE,), 0, Q)
    owner_slot = jax.random.randint(source_key, (P_SIZE,), 0, max(LQ // 4, 1))
    passage_slot = jax.random.randint(target_key, (P_SIZE,), 0, max(LP // 4, 1))
    strength = jnp.exp(jax.random.uniform(strength_key, (P_SIZE, 1), jnp.float32, math.log(1.5), math.log(5.0)))
    planted = values[owner_query, owner_slot] * strength / math.sqrt(E)
    planted_slot = (jnp.arange(LP)[None, :] == passage_slot[:, None])[:, :, None]
    tokens = jnp.where(planted_slot, planted[:, None, :], background * levels)
    return tokens.astype(jnp.bfloat16)


def draw_student_queries(key, part):
    key = jax.random.fold_in(key, 23)
    values = jax.random.normal(key, (Q, DS), jnp.float32)
    return jnp.clip(values, -6.0, 6.0).astype(jnp.bfloat16)


def touch_ends(values, rng, low, high):
    extent = values.shape
    place = [jax.random.randint(jax.random.fold_in(rng, axis), (), 0, extent[axis]) for axis in range(len(extent))]
    values = values.at[tuple(place)].set(low)
    longest = extent.index(max(extent))
    place[longest] = (place[longest] + 1) % extent[longest]
    return values.at[tuple(place)].set(high)


def block_scale(own_key, extent, shards, least, high):
    def one(axis_at, shards_of):
        heights = jax.random.uniform(jax.random.fold_in(jax.random.fold_in(own_key, 6), axis_at), (shards_of,), jnp.float32, least / len(shards), high / len(shards))
        return jnp.repeat(jnp.exp(heights), extent[axis_at] // shards_of).reshape((-1,) + (1,) * (len(extent) - axis_at - 1))

    factor_of = one(*shards[0])
    for cut in shards[1:]:
        factor_of = factor_of * one(*cut)
    return factor_of


def noise(key, dims, width, reach, cuts=(), kind=jnp.bfloat16):
    drawn = width * jax.random.normal(key, dims, jnp.float32)
    if cuts:
        drawn = drawn * block_scale(key, dims, cuts, -0.22, 0.18)
    return jnp.clip(drawn, -reach, reach).astype(kind)


def setup_inputs(seed: int = 0) -> dict:
    arg_keys = jax.random.split(jax.random.key(seed), 8)
    query_tokens = draw_query_tokens(jax.random.fold_in(arg_keys[7], 71), 0)
    query_lengths = touch_ends(jax.random.randint(arg_keys[1], (Q,), max(LQ // 4, 1), LQ + 1), jax.random.fold_in(arg_keys[1], 1), max(LQ // 4, 1), LQ).astype(jnp.int32)
    passage_tokens = draw_passage_tokens(jax.random.fold_in(arg_keys[7], 71), 0)
    passage_lengths = touch_ends(jax.random.randint(arg_keys[3], (P_SIZE,), max(LP // 4, 1), LP + 1), jax.random.fold_in(arg_keys[3], 1), max(LP // 4, 1), LP).astype(jnp.int32)
    student_queries = draw_student_queries(jax.random.fold_in(arg_keys[7], 71), 0)
    student_passages = noise(arg_keys[5], (P_SIZE, DS), DS ** -0.5, 0.21875, ((0, 8), (1, 4)))
    positives = touch_ends(jax.random.randint(arg_keys[6], (Q,), 0, P_SIZE), jax.random.fold_in(arg_keys[6], 1), 0, P_SIZE - 1).astype(jnp.int32)
    return {"query_tokens": query_tokens, "query_lengths": query_lengths, "passage_tokens": passage_tokens, "passage_lengths": passage_lengths, "student_queries": student_queries, "student_passages": student_passages, "positives": positives}


NEG = -1e30
SCALE = 4.0


def reference(query_tokens, query_lengths, passage_tokens, passage_lengths, student_queries, student_passages, positives):
    query_mask = (jnp.arange(LQ)[None, :] < query_lengths[:, None]).astype(jnp.float32)
    passage_valid = jnp.arange(LP)[None, :] < passage_lengths[:, None]
    passage_flat = passage_tokens.astype(jnp.float32).reshape(P_SIZE * LP, E)
    blocks = query_tokens.astype(jnp.float32).reshape(Q // 4, 4 * LQ, E)
    masks = query_mask.reshape(Q // 4, 4, LQ)

    def one_block(items):
        block, mask_rows = items
        sims = jnp.dot(block, passage_flat.T, precision=lax.Precision.HIGHEST).reshape(4 * LQ, P_SIZE, LP)
        sims = jnp.where(passage_valid[None], sims, NEG)
        maxima = jnp.max(sims, axis=2).reshape(4, LQ, P_SIZE)
        return jnp.sum(maxima * mask_rows[:, :, None], axis=1)

    teacher = lax.map(one_block, (blocks, masks)).reshape(Q, P_SIZE)
    student = SCALE * jnp.dot(student_queries, student_passages.T, preferred_element_type=jnp.float32)
    teacher_max = jnp.max(teacher, axis=1, keepdims=True)
    student_max = jnp.max(student, axis=1, keepdims=True)
    teacher_exp = jnp.exp(teacher - teacher_max)
    student_exp = jnp.exp(student - student_max)
    teacher_sum = jnp.sum(teacher_exp, axis=1, keepdims=True)
    student_sum = jnp.sum(student_exp, axis=1, keepdims=True)
    cross = jnp.sum(teacher_exp * (teacher - student), axis=1, keepdims=True)
    onehot = (jnp.arange(P_SIZE)[None, :] == positives[:, None])
    positive_score = jnp.sum(jnp.where(onehot, student, 0.0), axis=1, keepdims=True)
    teacher_lse = teacher_max + jnp.log(teacher_sum)
    student_lse = student_max + jnp.log(student_sum)
    per_query = cross / teacher_sum - teacher_lse + 2.0 * student_lse - positive_score
    loss = jnp.sum(per_query) / Q
    teacher_probs = teacher_exp / teacher_sum
    student_probs = student_exp / student_sum
    slope = (2.0 * student_probs - teacher_probs - onehot.astype(jnp.float32)) / Q
    query_grads = SCALE * jnp.dot(slope, student_passages.astype(jnp.float32), precision=lax.Precision.HIGHEST)
    passage_grads = SCALE * jnp.dot(slope.T, student_queries.astype(jnp.float32), precision=lax.Precision.HIGHEST)
    return query_grads, passage_grads, loss
```

```python
import functools

import jax
import jax.numpy as jnp
from jax import lax
from jax.experimental import pallas as pl
from jax.experimental.pallas import tpu as pltpu
from jax.sharding import PartitionSpec as P

NEG = -1e30
SCALE = 4.0
VMEM_LIMIT = 56 * 1024 * 1024


def params():
    return pltpu.CompilerParams(vmem_limit_bytes=VMEM_LIMIT)


def vmem():
    return pl.BlockSpec(memory_space=pltpu.VMEM)


def smem():
    return pl.BlockSpec(memory_space=pltpu.SMEM)


def split(x, parts):
    out = []
    for _ in range(parts):
        piece = x.astype(jnp.bfloat16)
        out.append(piece)
        x = x - piece.astype(jnp.float32)
    return out


def mxu(a, b, dims=((1,), (0,))):
    return lax.dot_general(a, b, (dims, ((), ())), preferred_element_type=jnp.float32)


def teacher_kernel(offsets, slots, first, *refs):
    count = len(offsets)
    query_refs = refs[:count]
    tokens_ref, lengths_ref = refs[count : count + 2]
    rest = refs[count + 2 :]
    prior_ref = None if first else rest[0]
    out_ref, best = rest[-2:]
    passages, span, width = tokens_ref.shape
    queries = out_ref.shape[1]
    r, c = lax.axis_index("row"), lax.axis_index("col")
    total = jnp.zeros(out_ref.shape, jnp.float32) if first else prior_ref[...]
    for query_ref, offset in zip(query_refs, offsets):
        rows = query_ref.shape[0]
        tile = min(256, rows)

        def passage(p, carry, query_ref=query_ref, rows=rows, tile=tile):
            block = tokens_ref[p]
            live = lax.broadcasted_iota(jnp.int32, (span, tile), 0) < lengths_ref[p]
            for n in range(0, rows, tile):
                sims = mxu(block, query_ref[n : n + tile, :], ((1,), (1,)))
                sims = jnp.where(live, sims, NEG)
                best[pl.ds(p, 1), n : n + tile] = jnp.max(sims, axis=0, keepdims=True)
            return carry

        lax.fori_loop(0, passages, passage, 0)
        start = offset(r, c)
        owner = lax.broadcasted_iota(jnp.int32, (rows, queries), 0) // slots + start
        member = (owner == lax.broadcasted_iota(jnp.int32, (rows, queries), 1)).astype(jnp.bfloat16)
        for piece in split(best[:, :rows], 3):
            total = total + mxu(piece, member)
    out_ref[...] = total


def teacher_block(blocks, offsets, slots, tokens, lengths, prior, queries):
    passages = tokens.shape[0]
    operands = list(blocks) + [tokens, lengths]
    specs = [vmem()] * len(blocks) + [vmem(), smem()]
    if prior is not None:
        operands.append(prior)
        specs.append(vmem())
    rows = max(b.shape[0] for b in blocks)
    flops = 2 * sum(b.shape[0] for b in blocks) * tokens.size
    return pl.pallas_call(
        functools.partial(teacher_kernel, offsets, slots, prior is None),
        out_shape=jax.ShapeDtypeStruct((passages, queries), jnp.float32),
        in_specs=specs,
        out_specs=vmem(),
        scratch_shapes=[pltpu.VMEM((passages, rows), jnp.float32)],
        compiler_params=params(),
        cost_estimate=pl.CostEstimate(flops=flops, bytes_accessed=2 * tokens.size, transcendentals=0),
    )(*operands)


def student_kernel(R, C, *refs):
    sq_refs = refs[:C]
    sp_refs = refs[C : C + R]
    score_ref, vectors_ref, pos_ref, held = refs[C + R :]
    per = C // R
    r, c = lax.axis_index("row"), lax.axis_index("col")
    block = sq_refs[0].shape[1]
    wide = sp_refs[0].shape[0] // per
    queries = R * block
    for kc in range(C):
        for kr in range(R):
            held[c ^ kc, r ^ kr] = sq_refs[kc][kr]
    total = jnp.zeros((queries, sp_refs[0].shape[1]), jnp.float32)
    for k in range(R):
        pieces = [
            held[(r ^ k) * per + h].reshape(queries, held.shape[3]).astype(jnp.float32)[:, :wide] for h in range(per)
        ]
        vectors = jnp.concatenate(pieces, axis=1).astype(jnp.bfloat16)
        if k == 0:
            vectors_ref[...] = vectors
        total = total + mxu(vectors, sp_refs[k][...])
    score_ref[...] = (SCALE * total).T
    meta = held[c].reshape(queries, held.shape[3]).astype(jnp.float32)
    where = meta[:, wide : wide + 1] * 64.0 + meta[:, wide + 1 : wide + 2]
    diag = lax.broadcasted_iota(jnp.int32, (queries, queries), 0) == lax.broadcasted_iota(
        jnp.int32, (queries, queries), 1
    )
    pos_ref[...] = jnp.sum(jnp.where(diag, where, 0.0), axis=0, keepdims=True)


def student_scores(sq, sp, R, C):
    block, lanes = sq[0].shape[1:]
    queries, depth, passages = R * block, sp[0].shape[0], sp[0].shape[1]
    return pl.pallas_call(
        functools.partial(student_kernel, R, C),
        out_shape=(
            jax.ShapeDtypeStruct((passages, queries), jnp.float32),
            jax.ShapeDtypeStruct((queries, depth), jnp.bfloat16),
            jax.ShapeDtypeStruct((1, queries), jnp.float32),
        ),
        in_specs=[vmem()] * (C + R),
        out_specs=(vmem(),) * 3,
        scratch_shapes=[pltpu.VMEM((C, R, block, lanes), jnp.bfloat16)],
        compiler_params=params(),
    )(*sq, *sp)


def finish_kernel(R, C, block, *refs):
    t_refs, s_refs, d_refs = refs[:C], refs[C : 2 * C], refs[2 * C : 3 * C]
    vectors_ref, pos_ref, query_ref, passage_ref, loss_ref, teach, stud = refs[3 * C :]
    r, c = lax.axis_index("row"), lax.axis_index("col")
    per = C // R
    queries = pos_ref.shape[1]
    wide = d_refs[0].shape[0]
    span = s_refs[0].shape[0]
    shape = (span, queries)
    for kc in range(C):
        for kr in range(R):
            teach[c ^ kc, r ^ kr] = t_refs[kc][kr]
        stud[c ^ kc] = s_refs[kc][...]

    def rows(op, x):
        return op(x, axis=0, keepdims=True)

    def peak(i, carry):
        t_max, s_max = carry
        return jnp.maximum(t_max, teach[i].reshape(shape)), jnp.maximum(s_max, stud[i])

    low = jnp.full(shape, -jnp.inf, jnp.float32)
    t_max, s_max = lax.fori_loop(0, C, peak, (low, low))
    t_max, s_max = rows(jnp.max, t_max), rows(jnp.max, s_max)
    place = pos_ref[...].astype(jnp.int32)
    index = lax.broadcasted_iota(jnp.int32, shape, 0)

    def totals(i, carry):
        t_sum, s_sum, cross, score = carry
        t, s = teach[i].reshape(shape), stud[i]
        t_exp, s_exp = jnp.exp(t - t_max), jnp.exp(s - s_max)
        hot = index + i * span == place
        teach[i] = t_exp.reshape(R, span // R, queries)
        stud[i] = s_exp
        return (
            t_sum + rows(jnp.sum, t_exp),
            s_sum + rows(jnp.sum, s_exp),
            cross + rows(jnp.sum, t_exp * (t - s)),
            score + rows(jnp.sum, jnp.where(hot, s, 0.0)),
        )

    zero = jnp.zeros((1, queries), jnp.float32)
    t_sum, s_sum, cross, score = lax.fori_loop(0, C, totals, (zero,) * 4)
    t_lse = t_max + jnp.log(t_sum)
    s_lse = s_max + jnp.log(s_sum)
    each = cross / t_sum - t_lse + 2.0 * s_lse - score
    loss_ref[...] = jnp.sum(each, axis=1, keepdims=True) / queries
    factor = SCALE / queries
    t_factor, s_factor = factor / t_sum, 2.0 * factor / s_sum

    def slope(i):
        hot = index + i * span == place
        gap = stud[i] * s_factor - teach[i].reshape(shape) * t_factor
        return split(gap - jnp.where(hot, factor, 0.0), 2)

    total = jnp.zeros((wide, queries), jnp.float32)
    group = r * per + c % per
    for k in range(C):
        for piece in slope(group ^ k):
            total = total + mxu(d_refs[k][...], piece)
    flat = total.T
    query_ref[...] = functools.reduce(
        jnp.add, [jnp.where(r == i, flat[i * block : (i + 1) * block, :], 0.0) for i in range(R)]
    )
    grads = sum(mxu(piece, vectors_ref[...]) for piece in slope(c))
    passage_ref[...] = grads.T


def finish(t, s, d, vectors, pos, R, C, block):
    queries = pos.shape[1]
    span = s[0].shape[0]
    return pl.pallas_call(
        functools.partial(finish_kernel, R, C, block),
        out_shape=(
            jax.ShapeDtypeStruct((block, d[0].shape[0]), jnp.float32),
            jax.ShapeDtypeStruct((vectors.shape[1], span), jnp.float32),
            jax.ShapeDtypeStruct((1, 1), jnp.float32),
        ),
        in_specs=[vmem()] * (3 * C + 2),
        out_specs=(vmem(),) * 3,
        scratch_shapes=[
            pltpu.VMEM((C, R, span // R, queries), jnp.float32),
            pltpu.VMEM((C, span, queries), jnp.float32),
        ],
        compiler_params=params(),
    )(*t, *s, *d, vectors, pos)


def shards(query_tokens, query_lengths, passage_tokens, passage_lengths, student_queries, student_passages, positives):
    R, C = lax.axis_size("row"), lax.axis_size("col")
    r, c = lax.axis_index("row"), lax.axis_index("col")
    block, slots, width = query_tokens.shape
    queries = block * R
    local = passage_tokens.shape[0]
    per = C // R

    def over_row(x, k):
        return lax.ppermute(x, "row", [(i, i ^ k) for i in range(R)])

    def over_col(x, k):
        return lax.ppermute(x, "col", [(i, i ^ k) for i in range(C)])

    live = jnp.arange(slots)[None, :] < query_lengths[:, None]
    tokens = jnp.where(live[:, :, None], query_tokens, 0).reshape(block * slots, width)
    half = block // 2
    mine = lax.dynamic_slice_in_dim(tokens, (c % 2) * half * slots, half * slots, 0)
    near = [over_row(mine, k) for k in range(1, R)]
    far = [over_col(x, 1) for x in near]

    wide = student_queries.shape[1]
    meta = jnp.stack([positives // 64, positives % 64], axis=1).astype(jnp.bfloat16)
    sent = jnp.pad(jnp.concatenate([student_queries, meta], axis=1), ((0, 0), (0, -(wide + 2) % 128)))
    sq_row = jnp.stack([sent] + [over_row(sent, k) for k in range(1, R)])
    sq = [sq_row] + [over_col(sq_row, k) for k in range(1, C)]
    flipped = student_passages.T
    sp = [flipped] + [over_row(flipped, k) for k in range(1, R)]
    parts = flipped.reshape(per, flipped.shape[0] // per, flipped.shape[1])
    chosen = [lax.dynamic_index_in_dim(parts, (c % per) ^ j, 0, keepdims=False) for j in range(per)]
    d = []
    for k in range(C):
        pairs = []
        for row in range(R):
            for col in range(C):
                group = col ^ k
                pairs.append((row * C + col, (group // per) * C + row * per + group % per))
        d.append(lax.ppermute(chosen[k % per], ("row", "col"), pairs))

    score = teacher_block(
        [tokens], [lambda r, c: r * block], slots, passage_tokens, passage_lengths, None, queries
    )
    own, vectors, pos = student_scores(sq, sp, R, C)

    def spread(x):
        pieces, bit = [x], C // 2
        while bit:
            pieces = pieces + [over_col(p, bit) for p in pieces]
            bit //= 2
        order, bit = [0], C // 2
        while bit:
            order = order + [o ^ bit for o in order]
            bit //= 2
        return [pieces[order.index(k)] for k in range(C)]

    s = spread(own)
    for k in range(1, R):
        offsets = [
            lambda r, c, k=k: (r ^ k) * block + (c % 2) * half,
            lambda r, c, k=k: (r ^ k) * block + (1 - c % 2) * half,
        ]
        score = teacher_block(
            [near[k - 1], far[k - 1]], offsets, slots, passage_tokens, passage_lengths, score, queries
        )
    stacked = jnp.stack([score] + [over_row(score, k) for k in range(1, R)])
    t = spread(stacked)
    query_grads, passage_grads, loss = finish(t, s, d, vectors, pos, R, C, block)
    return (query_grads, passage_grads.T, loss[0, 0])


def solution(mesh):
    return jax.shard_map(
        shards,
        mesh=mesh,
        in_specs=(
            P("row", None, None),
            P("row"),
            P(("col", "row"), None, None),
            P(("col", "row")),
            P("row", "col"),
            P("col", "row"),
            P("row"),
        ),
        out_specs=(P("row", "col"), P("col", "row"), P()),
        check_vma=False,
    )
```

```python
import functools

import jax
import jax.numpy as jnp
from jax import lax
from jax.experimental import pallas as pl
from jax.experimental.pallas import tpu as pltpu
from jax.sharding import PartitionSpec as P

NEG = -1e30
SCALE = 4.0
TILE = 16
GROUP = 32
LANES = 128


def params(megabytes):
    return pltpu.CompilerParams(vmem_limit_bytes=megabytes * 1024 * 1024)


def vmem():
    return pl.BlockSpec(memory_space=pltpu.VMEM)


def smem():
    return pl.BlockSpec(memory_space=pltpu.SMEM)


def split(x, parts):
    out = []
    for _ in range(parts):
        piece = x.astype(jnp.bfloat16)
        out.append(piece)
        x = x - piece.astype(jnp.float32)
    return out


def mxu(a, b, dims=((1,), (0,))):
    return lax.dot_general(a, b, (dims, ((), ())), preferred_element_type=jnp.float32)


def live_blocks(lengths_ref, blocks_ref, passages, per):
    def one(p, at):
        for b in range(per):
            blocks_ref[at + b] = p * TILE + b
        return at + (lengths_ref[p] + TILE - 1) // TILE

    count = lax.fori_loop(0, passages, one, 0)
    for i in range(GROUP):
        blocks_ref[count + i] = (passages - 1) * TILE
    return count


def teacher_kernel(slots, shift, sides, first, *refs):
    query_ref = refs[0]
    token_refs = refs[1 : 1 + len(sides)]
    length_refs = refs[1 + len(sides) : 1 + 2 * len(sides)]
    prior_ref = None if first else refs[1 + 2 * len(sides)]
    out_ref, flipped, best, blocks_ref = refs[-4:]
    passages, lanes = out_ref.shape
    rows = query_ref.shape[0]
    tile = min(256, rows)
    r, c = lax.axis_index("row"), lax.axis_index("col")
    flipped[...] = query_ref[...].astype(jnp.float32).T.astype(jnp.bfloat16)
    total = jnp.zeros(out_ref.shape, jnp.float32) if first else prior_ref[...]
    sub = lax.broadcasted_iota(jnp.int32, (8, tile), 0)
    for side, tokens_ref, lengths_ref in zip(sides, token_refs, length_refs):
        per = tokens_ref.shape[0] // passages
        count = live_blocks(lengths_ref, blocks_ref, passages, per)
        best[...] = jnp.full(best.shape, NEG, jnp.float32)

        def step(i, carry, tokens_ref=tokens_ref, lengths_ref=lengths_ref, per=per):
            owner, begin, values = [], [], []
            for g in range(GROUP):
                entry = blocks_ref[i * GROUP + g]
                p, b = entry // TILE, entry % TILE
                owner.append(pl.multiple_of(p * 8, 8))
                begin.append(lengths_ref[p] - b * TILE)
                values.append(tokens_ref[p * per + b])
            block = jnp.concatenate(values, axis=0)
            for n in range(0, rows, tile):
                sims = mxu(block, flipped[:, n : n + tile])
                for g in range(GROUP):
                    top = jnp.where(sub < begin[g], sims[g * TILE : g * TILE + 8], NEG)
                    low = jnp.where(sub < begin[g] - 8, sims[g * TILE + 8 : g * TILE + 16], NEG)
                    peak = jnp.maximum(top, low)
                    for l in range(0, tile, LANES):
                        at = ((n + l) // LANES, pl.ds(owner[g], 8))
                        best[at] = jnp.maximum(best[at], peak[:, l : l + LANES])
            return carry

        lax.fori_loop(0, (count + GROUP - 1) // GROUP, step, 0)
        found = []
        for l in range(rows // LANES):
            peak = best[l, pl.ds(0, passages, stride=8), :]
            for s in range(1, 8):
                peak = jnp.maximum(peak, best[l, pl.ds(s, passages, stride=8), :])
            found.append(peak)
        found = jnp.concatenate(found, axis=1)
        parity = c % 2 if side == 0 else 1 - c % 2
        start = parity * (lanes // 2) + (r ^ shift) * (rows // slots)
        owner = lax.broadcasted_iota(jnp.int32, (rows, lanes), 0) // slots + start
        member = (owner == lax.broadcasted_iota(jnp.int32, (rows, lanes), 1)).astype(jnp.bfloat16)
        for piece in split(found, 3):
            total = total + mxu(piece, member)
    out_ref[...] = total


def teacher_block(query, slots, shift, sides, tokens, lengths, prior, queries, passages):
    tokens = [tokens[side] for side in sides]
    operands = [query] + tokens + [lengths[side] for side in sides]
    specs = [vmem()] * (1 + len(sides)) + [smem()] * len(sides)
    if prior is not None:
        operands.append(prior)
        specs.append(vmem())
    rows, width = query.shape
    return pl.pallas_call(
        functools.partial(teacher_kernel, slots, shift, sides, prior is None),
        out_shape=jax.ShapeDtypeStruct((passages, queries), jnp.float32),
        in_specs=specs,
        out_specs=vmem(),
        scratch_shapes=[
            pltpu.VMEM((width, rows), jnp.bfloat16),
            pltpu.VMEM((rows // LANES, passages * 8, LANES), jnp.float32),
            pltpu.SMEM((tokens[0].shape[0] + TILE + GROUP,), jnp.int32),
        ],
        compiler_params=params(16),
        cost_estimate=pl.CostEstimate(
            flops=2 * rows * sum(t.size for t in tokens),
            bytes_accessed=2 * sum(t.size for t in tokens),
            transcendentals=0,
        ),
    )(*operands)


def student_kernel(R, C, wide, sq_ref, *refs):
    sp_refs, cut_refs = refs[:R], refs[R:-4]
    sent_ref, vectors_ref, pos_ref, held = refs[-4:]
    per = C // R
    r, c = lax.axis_index("row"), lax.axis_index("col")
    lanes = sq_ref.shape[2]
    half = sq_ref.shape[1] // 2
    queries = 2 * R * half
    span = sp_refs[0].shape[1]

    def columns(index):
        for i in range(R):
            for h in range(2):
                held[h, i] = sq_ref[i * C + index, h * half : (h + 1) * half]
        return held[...].reshape(queries, lanes).astype(jnp.float32)

    total = jnp.zeros((queries, span), jnp.float32)
    for k in range(R):
        pieces = [columns((r ^ k) * per + h)[:, :wide] for h in range(per)]
        vectors = jnp.concatenate(pieces, axis=1).astype(jnp.bfloat16)
        if k == 0:
            vectors_ref[...] = vectors
        total = total + mxu(vectors, sp_refs[k][...])
    scores = split((SCALE * total).T, 3)
    pad = sent_ref.shape[1] - 3 * span * (queries // LANES)
    for i in range(C):
        at = pad
        for piece in scores:
            for n in range(0, queries, LANES):
                sent_ref[i, at : at + span] = piece[:, n : n + LANES]
                at += span
    for k in range(R):
        for h in range(per):
            cut = cut_refs[0][k, h] if cut_refs else sp_refs[k][h * wide : (h + 1) * wide]
            sent_ref[(r ^ k) * per + h, :pad] = cut
    meta = columns(c)
    where = meta[:, wide : wide + 1] * 64.0 + meta[:, wide + 1 : wide + 2]
    diag = lax.broadcasted_iota(jnp.int32, (queries, queries), 0) == lax.broadcasted_iota(
        jnp.int32, (queries, queries), 1
    )
    pos_ref[...] = jnp.sum(jnp.where(diag, where, 0.0), axis=0, keepdims=True)


def student_scores(sq, sp, R, C, wide):
    block, lanes = sq.shape[1:]
    queries, depth, span = R * block, sp[0].shape[0], sp[0].shape[1]
    per = C // R
    pad = wide + -wide % TILE
    cut = []
    if pad > wide:
        cut = [jnp.pad(jnp.stack(sp).reshape(R, per, wide, span), ((0, 0), (0, 0), (0, pad - wide), (0, 0)))]
    return pl.pallas_call(
        functools.partial(student_kernel, R, C, wide),
        out_shape=(
            jax.ShapeDtypeStruct((C, pad + 3 * span * (queries // LANES), LANES), jnp.bfloat16),
            jax.ShapeDtypeStruct((queries, depth), jnp.bfloat16),
            jax.ShapeDtypeStruct((1, queries), jnp.float32),
        ),
        in_specs=[vmem()] * (1 + R + len(cut)),
        out_specs=(vmem(),) * 3,
        scratch_shapes=[pltpu.VMEM((2, R, block // 2, lanes), jnp.bfloat16)],
        compiler_params=params(40),
    )(sq, *sp, *cut)


def finish_kernel(R, C, block, wide, t_ref, s_ref, vectors_ref, pos_ref, query_ref, passage_ref, loss_ref, teach, stud):
    r, c = lax.axis_index("row"), lax.axis_index("col")
    queries = pos_ref.shape[1]
    span = passage_ref.shape[1]
    pad = s_ref.shape[1] - 3 * span * (queries // LANES)
    half = queries // 2
    shape = (span, queries)

    def rows(op, x):
        return op(x, axis=0, keepdims=True)

    def peak(j, carry):
        t_max, s_max = carry
        pair = [t_ref[2 * j + h].reshape(span, queries) for h in range(2)]
        for b in range(2):
            t = jnp.concatenate([x[:, b * half : (b + 1) * half] for x in pair], axis=1)
            teach[2 * j + b] = t
            t_max = jnp.maximum(t_max, t)
            pieces, at = [], pad
            for _ in range(3):
                cells = []
                for _ in range(0, queries, LANES):
                    cells.append(s_ref[2 * j + b, at : at + span].astype(jnp.float32))
                    at += span
                pieces.append(jnp.concatenate(cells, axis=1))
            s = pieces[0] + (pieces[1] + pieces[2])
            stud[2 * j + b] = s
            s_max = jnp.maximum(s_max, s)
        return t_max, s_max

    low = jnp.full(shape, -jnp.inf, jnp.float32)
    t_max, s_max = lax.fori_loop(0, C // 2, peak, (low, low))
    t_max, s_max = rows(jnp.max, t_max), rows(jnp.max, s_max)
    place = pos_ref[...].astype(jnp.int32)
    index = lax.broadcasted_iota(jnp.int32, shape, 0)

    def totals(i, carry):
        t_sum, s_sum, cross, score = carry
        t, s = teach[i], stud[i]
        t_exp, s_exp = jnp.exp(t - t_max), jnp.exp(s - s_max)
        hot = index + i * span == place
        teach[i] = t_exp
        stud[i] = s_exp
        return (
            t_sum + rows(jnp.sum, t_exp),
            s_sum + rows(jnp.sum, s_exp),
            cross + rows(jnp.sum, t_exp * (t - s)),
            score + rows(jnp.sum, jnp.where(hot, s, 0.0)),
        )

    zero = jnp.zeros((1, queries), jnp.float32)
    t_sum, s_sum, cross, score = lax.fori_loop(0, C, totals, (zero,) * 4)
    t_lse = t_max + jnp.log(t_sum)
    s_lse = s_max + jnp.log(s_sum)
    each = cross / t_sum - t_lse + 2.0 * s_lse - score
    loss_ref[...] = jnp.sum(each, axis=1, keepdims=True) / queries
    factor = SCALE / queries
    t_factor, s_factor = factor / t_sum, 2.0 * factor / s_sum

    def slope(i):
        hot = index + i * span == place
        gap = stud[i] * s_factor - teach[i] * t_factor
        return split(gap - jnp.where(hot, factor, 0.0), 2)

    def gradient(i, total):
        for piece in slope(i):
            total = total + mxu(s_ref[i, :pad], piece)
        return total

    flat = lax.fori_loop(0, C, gradient, jnp.zeros((pad, queries), jnp.float32)).T[:, :wide]
    sub = block // 2
    for h in range(2):
        query_ref[h * sub : (h + 1) * sub, :] = functools.reduce(
            jnp.add,
            [jnp.where(r == i, flat[h * half + i * sub : h * half + (i + 1) * sub], 0.0) for i in range(R)],
        )
    grads = sum(mxu(piece, vectors_ref[...]) for piece in slope(c))
    passage_ref[...] = grads.T


def finish(t, s, vectors, pos, R, C, block, wide, span):
    queries = pos.shape[1]
    held = pltpu.VMEM((C, span, queries), jnp.float32)
    return pl.pallas_call(
        functools.partial(finish_kernel, R, C, block, wide),
        out_shape=(
            jax.ShapeDtypeStruct((block, wide), jnp.float32),
            jax.ShapeDtypeStruct((vectors.shape[1], span), jnp.float32),
            jax.ShapeDtypeStruct((1, 1), jnp.float32),
        ),
        in_specs=[vmem()] * 4,
        out_specs=(vmem(),) * 3,
        scratch_shapes=[held, held],
        compiler_params=params(48),
    )(t, s, vectors, pos)


def shards(query_tokens, query_lengths, passage_tokens, passage_lengths, student_queries, student_passages, positives):
    R, C = lax.axis_size("row"), lax.axis_size("col")
    r, c = lax.axis_index("row"), lax.axis_index("col")
    block, slots, width = query_tokens.shape
    queries = block * R
    local, count = passage_tokens.shape[:2]
    half = block // 2

    def over_row(x, k):
        return lax.ppermute(x, "row", [(i, i ^ k) for i in range(R)])

    def over_col(x, k):
        return lax.ppermute(x, "col", [(i, i ^ k) for i in range(C)])

    part = lax.dynamic_slice_in_dim(query_tokens, (c % 2) * half, half, 0)
    lives = lax.dynamic_slice_in_dim(query_lengths, (c % 2) * half, half, 0)
    live = jnp.arange(slots)[None, :] < lives[:, None]
    mine = jnp.where(live[:, :, None], part, 0).reshape(half * slots, width)
    near = [mine] + [over_row(mine, k) for k in range(1, R)]
    cells = passage_tokens.reshape(local * count // TILE, TILE, width)
    tokens = [cells, over_col(cells, 1)]
    lengths = [passage_lengths, over_col(passage_lengths, 1)]

    wide = student_queries.shape[1]
    meta = jnp.stack([positives // 64, positives % 64], axis=1).astype(jnp.bfloat16)
    sent = jnp.pad(jnp.concatenate([student_queries, meta], axis=1), ((0, 0), (0, -(wide + 2) % LANES)))
    sq = lax.all_to_all(jnp.broadcast_to(sent[None], (R * C,) + sent.shape), ("row", "col"), 0, 0, tiled=True)
    flipped = student_passages.T
    sp = [flipped] + [over_row(flipped, k) for k in range(1, R)]

    common = dict(slots=slots, tokens=tokens, lengths=lengths, queries=queries, passages=local)
    score = teacher_block(near[0], shift=0, sides=(0,), prior=None, **common)
    score = teacher_block(near[0], shift=0, sides=(1,), prior=score, **common)
    out, vectors, pos = student_scores(sq, sp, R, C, wide)
    s = lax.all_to_all(out, "col", 0, 0, tiled=True)
    for k in range(1, R):
        score = teacher_block(near[k], shift=k, sides=(0, 1), prior=score, **common)
    t = lax.all_gather(score, ("col", "row"), axis=0, tiled=True).reshape(C, R * local, queries)
    span = R * local
    query_grads, passage_grads, loss = finish(t, s, vectors, pos, R, C, block, wide, span)
    return (query_grads, passage_grads.T, loss[0, 0])


def solution(mesh):
    return jax.shard_map(
        shards,
        mesh=mesh,
        in_specs=(
            P("row", None, None),
            P("row"),
            P(("col", "row"), None, None),
            P(("col", "row")),
            P("row", "col"),
            P("col", "row"),
            P("row"),
        ),
        out_specs=(P("row", "col"), P("col", "row"), P()),
        check_vma=False,
    )
```

```python
import functools

import jax
import jax.numpy as jnp
from jax import lax
from jax.experimental import pallas as pl
from jax.experimental.pallas import tpu as pltpu
from jax.sharding import PartitionSpec as P

NEG = -1e30
SCALE = 4.0
TILE = 16
GROUP = 32
LANES = 128


def params(megabytes):
    return pltpu.CompilerParams(vmem_limit_bytes=megabytes * 1024 * 1024)


def vmem():
    return pl.BlockSpec(memory_space=pltpu.VMEM)


def smem():
    return pl.BlockSpec(memory_space=pltpu.SMEM)


def split(x, parts):
    out = []
    for _ in range(parts):
        piece = x.astype(jnp.bfloat16)
        out.append(piece)
        x = x - piece.astype(jnp.float32)
    return out


def mxu(a, b, dims=((1,), (0,))):
    return lax.dot_general(a, b, (dims, ((), ())), preferred_element_type=jnp.float32)


def prepare_kernel(slots, tokens_ref, lives_ref, cells_ref, lengths_ref, sq_ref, sp_ref, pos_ref, mine_ref, out_ref, sent_ref):
    c = lax.axis_index("col")
    half = tokens_ref.shape[0] // 2
    width = tokens_ref.shape[2]
    slot = lax.broadcasted_iota(jnp.int32, (slots, width), 0)
    for q in range(half):
        at = (c % 2) * half + q
        value = tokens_ref[at].astype(jnp.float32)
        value = jnp.where(slot < lives_ref[at], value, 0.0)
        mine_ref[q * slots : (q + 1) * slots, :] = value.astype(jnp.bfloat16)
    out_ref[...] = cells_ref[...]
    passages = lengths_ref.shape[0]
    per = cells_ref.shape[0] // passages
    row = lax.broadcasted_iota(jnp.int32, (TILE, width), 0)

    def trim(p, carry):
        last = (lengths_ref[p] + TILE - 1) // TILE - 1
        value = cells_ref[p * per + last].astype(jnp.float32)
        value = jnp.where(row < lengths_ref[p] - last * TILE, value, value[0:1, :])
        out_ref[p * per + last] = value.astype(jnp.bfloat16)
        return carry

    lax.fori_loop(0, passages, trim, 0)
    block, wide = sq_ref.shape
    depth = sp_ref.shape[0]
    vectors = jnp.concatenate([sq_ref[...].astype(jnp.float32), jnp.zeros((block, LANES - wide), jnp.float32)], axis=1)
    line = lax.broadcasted_iota(jnp.int32, (block, LANES), 0)
    lane = lax.broadcasted_iota(jnp.int32, (block, LANES), 1)
    place = jnp.zeros((block, LANES), jnp.int32)
    for q in range(block):
        place = jnp.where(line == q, pos_ref[q], place)
    high, low = place // 64, place % 64
    vectors = jnp.where(lane == wide, high.astype(jnp.float32), vectors)
    vectors = jnp.where(lane == wide + 1, low.astype(jnp.float32), vectors).astype(jnp.bfloat16)
    for i in range(sent_ref.shape[0]):
        sent_ref[i, :depth] = sp_ref[...]
        sent_ref[i, depth:] = vectors


def prepare(tokens, lives, cells, lengths, sq, sp, pos, R):
    block, slots, width = tokens.shape
    return pl.pallas_call(
        functools.partial(prepare_kernel, slots),
        out_shape=(
            jax.ShapeDtypeStruct((block // 2 * slots, width), jnp.bfloat16),
            jax.ShapeDtypeStruct(cells.shape, jnp.bfloat16),
            jax.ShapeDtypeStruct((R, sp.shape[0] + block, LANES), jnp.bfloat16),
        ),
        in_specs=[vmem(), smem(), vmem(), smem(), vmem(), vmem(), smem()],
        out_specs=(vmem(),) * 3,
        compiler_params=params(16),
    )(tokens, lives, cells, lengths, sq, sp, pos)


def live_blocks(lengths_ref, blocks_ref, passages, per):
    def one(p, at):
        for b in range(per):
            blocks_ref[at + b] = p * TILE + b
        return at + (lengths_ref[p] + TILE - 1) // TILE

    count = lax.fori_loop(0, passages, one, 0)
    last = (passages - 1) * TILE + (lengths_ref[passages - 1] + TILE - 1) // TILE - 1
    for i in range(GROUP):
        blocks_ref[count + i] = last
    return count


def teacher_kernel(slots, shift, sides, first, copies, *refs):
    query_ref = refs[0]
    token_refs = refs[1 : 1 + len(sides)]
    length_refs = refs[1 + len(sides) : 1 + 2 * len(sides)]
    prior_ref = None if first else refs[1 + 2 * len(sides)]
    out_ref, flipped, best, blocks_ref = refs[-4:]
    passages, lanes = out_ref.shape[-2:]
    rows = query_ref.shape[0]
    tile = min(256, rows)
    r, c = lax.axis_index("row"), lax.axis_index("col")
    flipped[...] = query_ref[...].astype(jnp.float32).T.astype(jnp.bfloat16)
    total = jnp.zeros((passages, lanes), jnp.float32) if first else prior_ref[...]
    for side, tokens_ref, lengths_ref in zip(sides, token_refs, length_refs):
        per = tokens_ref.shape[0] // passages
        count = live_blocks(lengths_ref, blocks_ref, passages, per)

        def step(i, carry, tokens_ref=tokens_ref, per=per):
            carry = list(carry)
            owner, fresh, values = [], [], []
            for g in range(GROUP):
                entry = blocks_ref[i * GROUP + g]
                p, b = lax.shift_right_logical(entry, 4), entry & (TILE - 1)
                owner.append(pl.multiple_of(p * 8, 8))
                fresh.append(b == 0)
                values.append(tokens_ref[p * per + b])
            block = jnp.concatenate(values, axis=0)
            for n in range(0, rows, tile):
                sims = mxu(block, flipped[:, n : n + tile])
                for g in range(GROUP):
                    for l in range(0, tile, LANES):
                        j = (n + l) // LANES
                        top = sims[g * TILE : g * TILE + 8, l : l + LANES]
                        low = sims[g * TILE + 8 : g * TILE + 16, l : l + LANES]
                        kept = jnp.where(fresh[g], NEG, carry[j])
                        carry[j] = jnp.maximum(kept, jnp.maximum(top, low))
                        best[j, pl.ds(owner[g], 8), :] = carry[j]
            return tuple(carry)

        lax.fori_loop(
            0,
            (count + GROUP - 1) // GROUP,
            step,
            tuple(jnp.full((8, LANES), NEG, jnp.float32) for _ in range(rows // LANES)),
        )
        found = []
        for l in range(rows // LANES):
            peak = best[l, pl.ds(0, passages, stride=8), :]
            for s in range(1, 8):
                peak = jnp.maximum(peak, best[l, pl.ds(s, passages, stride=8), :])
            found.append(peak)
        found = jnp.concatenate(found, axis=1)
        parity = c % 2 if side == 0 else 1 - c % 2
        start = parity * (lanes // 2) + (r ^ shift) * (rows // slots)
        owner = lax.broadcasted_iota(jnp.int32, (rows, lanes), 0) // slots + start
        member = (owner == lax.broadcasted_iota(jnp.int32, (rows, lanes), 1)).astype(jnp.bfloat16)
        for piece in split(found, 3):
            total = total + mxu(piece, member)
    if copies:
        for i in range(copies):
            out_ref[i] = total
    else:
        out_ref[...] = total


def teacher_block(query, slots, shift, sides, tokens, lengths, prior, queries, passages, copies=0):
    tokens = [tokens[side] for side in sides]
    operands = [query] + tokens + [lengths[side] for side in sides]
    specs = [vmem()] * (1 + len(sides)) + [smem()] * len(sides)
    if prior is not None:
        operands.append(prior)
        specs.append(vmem())
    rows, width = query.shape
    shape = (passages, queries)
    return pl.pallas_call(
        functools.partial(teacher_kernel, slots, shift, sides, prior is None, copies),
        out_shape=jax.ShapeDtypeStruct(((copies,) if copies else ()) + shape, jnp.float32),
        in_specs=specs,
        out_specs=vmem(),
        scratch_shapes=[
            pltpu.VMEM((width, rows), jnp.bfloat16),
            pltpu.VMEM((rows // LANES, passages * 8, LANES), jnp.float32),
            pltpu.SMEM((tokens[0].shape[0] + TILE + GROUP,), jnp.int32),
        ],
        compiler_params=params(16),
        cost_estimate=pl.CostEstimate(
            flops=2 * rows * sum(t.size for t in tokens),
            bytes_accessed=2 * sum(t.size for t in tokens),
            transcendentals=0,
        ),
    )(*operands)


def student_kernel(wide, raw_ref, score_ref, vectors_ref, stats_ref, held, flat):
    C, R, rows, span = raw_ref.shape
    r, c = lax.axis_index("row"), lax.axis_index("col")
    queries = score_ref.shape[2]
    block = queries // R
    half = block // 2
    depth = rows - block
    per = depth // wide
    for i in range(R):
        pieces = []
        for h in range(per):
            for j in range(R):
                for x in range(2):
                    held[x, j] = raw_ref[i * per + h, j, depth + x * half : depth + (x + 1) * half]
            pieces.append(held[...].reshape(queries, span).astype(jnp.float32)[:, :wide])
        flat[i] = jnp.concatenate(pieces, axis=1).astype(jnp.bfloat16)
    vectors_ref[...] = flat[r]
    for j in range(R):
        for x in range(2):
            held[x, j] = raw_ref[c, j, depth + x * half : depth + (x + 1) * half]
    meta = held[...].reshape(queries, span).astype(jnp.float32)
    where = meta[:, wide : wide + 1] * 64.0 + meta[:, wide + 1 : wide + 2]
    diag = lax.broadcasted_iota(jnp.int32, (queries, queries), 0) == lax.broadcasted_iota(
        jnp.int32, (queries, queries), 1
    )
    where = jnp.sum(jnp.where(diag, where, 0.0), axis=0, keepdims=True)
    place = where.astype(jnp.int32)
    index = lax.broadcasted_iota(jnp.int32, (span, queries), 0)

    def scores(i, carry):
        peak, score = carry
        total = jnp.zeros((queries, span), jnp.float32)
        for k in range(R):
            total = total + mxu(flat[k], raw_ref[i, k, :depth])
        s = (SCALE * total).T
        score_ref[i] = s
        hot = index + i * span == place
        return jnp.maximum(peak, s), score + jnp.where(hot, s, 0.0)

    low = jnp.full((span, queries), -jnp.inf, jnp.float32)
    peak, score = lax.fori_loop(0, C, scores, (low, jnp.zeros((span, queries), jnp.float32)))
    peak = jnp.max(peak, axis=0, keepdims=True)
    score = jnp.sum(score, axis=0, keepdims=True)
    total = lax.fori_loop(
        0, C, lambda i, t: t + jnp.exp(score_ref[i] - peak), jnp.zeros((span, queries), jnp.float32)
    )
    total = jnp.sum(total, axis=0, keepdims=True)
    stats_ref[0:1, :] = where
    stats_ref[1:2, :] = peak
    stats_ref[2:3, :] = total
    stats_ref[3:4, :] = score
    stats_ref[4:8, :] = jnp.zeros((4, queries), jnp.float32)


def student_scores(raw, queries, wide):
    C, R, rows, span = raw.shape
    depth = rows - queries // R
    return pl.pallas_call(
        functools.partial(student_kernel, wide),
        out_shape=(
            jax.ShapeDtypeStruct((C, span, queries), jnp.float32),
            jax.ShapeDtypeStruct((queries, depth), jnp.bfloat16),
            jax.ShapeDtypeStruct((8, queries), jnp.float32),
        ),
        in_specs=[vmem()],
        out_specs=(vmem(),) * 3,
        scratch_shapes=[
            pltpu.VMEM((2, R, queries // R // 2, span), jnp.bfloat16),
            pltpu.VMEM((R, queries, depth), jnp.bfloat16),
        ],
        compiler_params=params(40),
    )(raw)


def finish_kernel(wide, t_ref, s_ref, raw_ref, vectors_ref, stats_ref, query_ref, passage_ref, loss_ref, teach):
    C, R, rows, span = raw_ref.shape
    r, c = lax.axis_index("row"), lax.axis_index("col")
    queries = vectors_ref.shape[0]
    depth = vectors_ref.shape[1]
    per = depth // wide
    block = queries // R
    half = queries // 2
    shape = (span, queries)
    where, s_max, s_sum, score = [stats_ref[i : i + 1, :] for i in range(4)]

    def peak(j, t_max):
        pair = [[t_ref[k, 2 * j + h] for k in range(R)] for h in range(2)]
        pair = [jnp.concatenate(x, axis=0) for x in pair]
        for b in range(2):
            t = jnp.concatenate([x[:, b * half : (b + 1) * half] for x in pair], axis=1)
            teach[2 * j + b] = t
            t_max = jnp.maximum(t_max, t)
        return t_max

    t_max = lax.fori_loop(0, C // 2, peak, jnp.full(shape, -jnp.inf, jnp.float32))
    t_max = jnp.max(t_max, axis=0, keepdims=True)

    def totals(i, carry):
        t_sum, cross = carry
        t = teach[i]
        t_exp = jnp.exp(t - t_max)
        teach[i] = t_exp
        return t_sum + t_exp, cross + t_exp * (t - s_ref[i])

    zero = jnp.zeros(shape, jnp.float32)
    t_sum, cross = lax.fori_loop(0, C, totals, (zero, zero))
    t_sum = jnp.sum(t_sum, axis=0, keepdims=True)
    cross = jnp.sum(cross, axis=0, keepdims=True)
    t_lse = t_max + jnp.log(t_sum)
    s_lse = s_max + jnp.log(s_sum)
    each = cross / t_sum - t_lse + 2.0 * s_lse - score
    loss_ref[...] = jnp.sum(each, axis=1, keepdims=True) / queries
    factor = SCALE / queries
    t_factor, s_factor = factor / t_sum, 2.0 * factor / s_sum
    place = where.astype(jnp.int32)
    index = lax.broadcasted_iota(jnp.int32, shape, 0)

    def slope(i):
        hot = index + i * span == place
        gap = jnp.exp(s_ref[i] - s_max) * s_factor - teach[i] * t_factor
        return split(gap - jnp.where(hot, factor, 0.0), 2)

    def gradient(i, total):
        for piece in slope(i):
            total = total + mxu(raw_ref[i, c // per, :depth], piece)
        return total

    flat = lax.fori_loop(0, C, gradient, jnp.zeros((depth, queries), jnp.float32)).T
    sub = block // 2
    for h in range(2):
        lines = functools.reduce(
            jnp.add,
            [jnp.where(r == i, flat[h * half + i * sub : h * half + (i + 1) * sub], 0.0) for i in range(R)],
        )
        query_ref[h * sub : (h + 1) * sub, :] = functools.reduce(
            jnp.add, [jnp.where(c % per == i, lines[:, i * wide : (i + 1) * wide], 0.0) for i in range(per)]
        )
    grads = sum(mxu(piece, vectors_ref[...]) for piece in slope(c))
    passage_ref[...] = grads.T


def finish(t, s, raw, vectors, stats, wide):
    C, R, rows, span = raw.shape
    queries, depth = vectors.shape
    return pl.pallas_call(
        functools.partial(finish_kernel, wide),
        out_shape=(
            jax.ShapeDtypeStruct((queries // R, wide), jnp.float32),
            jax.ShapeDtypeStruct((depth, span), jnp.float32),
            jax.ShapeDtypeStruct((1, 1), jnp.float32),
        ),
        in_specs=[vmem()] * 5,
        out_specs=(vmem(),) * 3,
        scratch_shapes=[pltpu.VMEM((C, span, queries), jnp.float32)],
        compiler_params=params(48),
    )(t, s, raw, vectors, stats)


def shards(query_tokens, query_lengths, passage_tokens, passage_lengths, student_queries, student_passages, positives):
    R, C = lax.axis_size("row"), lax.axis_size("col")
    block, slots, width = query_tokens.shape
    queries = block * R
    local, count = passage_tokens.shape[:2]
    wide = student_queries.shape[1]

    def over_row(x, k):
        return lax.ppermute(x, "row", [(i, i ^ k) for i in range(R)])

    def over_col(x, k):
        return lax.ppermute(x, "col", [(i, i ^ k) for i in range(C)])

    cells = passage_tokens.reshape(local * count // TILE, TILE, width)
    mine, cells, sent = prepare(
        query_tokens, query_lengths, cells, passage_lengths, student_queries, student_passages.T, positives, R
    )
    tokens = [cells, over_col(cells, 1)]
    lengths = [passage_lengths, over_col(passage_lengths, 1)]
    rows = lax.all_to_all(sent, "row", 0, 0, tiled=True)
    near = [mine] + [over_row(mine, k) for k in range(1, R)]
    common = dict(slots=slots, tokens=tokens, lengths=lengths, queries=queries, passages=local)
    score = teacher_block(near[0], shift=0, sides=(0,), prior=None, **common)
    score = teacher_block(near[0], shift=0, sides=(1,), prior=score, **common)
    rows, score = lax.optimization_barrier((rows, score))
    raw = lax.all_to_all(jnp.broadcast_to(rows[None], (C,) + rows.shape), "col", 0, 0, tiled=True)
    for k in range(1, R):
        copies = R * C if k == R - 1 else 0
        score = teacher_block(near[k], shift=k, sides=(0, 1), prior=score, copies=copies, **common)
    raw, score = lax.optimization_barrier((raw, score))
    t = lax.all_to_all(score, ("row", "col"), 0, 0, tiled=True).reshape(R, C, local, queries)
    s, vectors, stats = student_scores(raw, queries, wide)
    query_grads, passage_grads, loss = finish(t, s, raw, vectors, stats, wide)
    return (query_grads, passage_grads.T, loss[0, 0])


def solution(mesh):
    return jax.shard_map(
        shards,
        mesh=mesh,
        in_specs=(
            P("row", None, None),
            P("row"),
            P(("col", "row"), None, None),
            P(("col", "row")),
            P("row", "col"),
            P("col", "row"),
            P("row"),
        ),
        out_specs=(P("row", "col"), P("col", "row"), P()),
        check_vma=False,
    )
```

```python
import functools

import jax
import jax.numpy as jnp
from jax import lax
from jax.experimental import pallas as pl
from jax.experimental.pallas import tpu as pltpu
from jax.sharding import PartitionSpec as P

NEG = -1e30
SCALE = 4.0
TILE = 16
GROUP = 32
LANES = 128


def params(megabytes):
    return pltpu.CompilerParams(vmem_limit_bytes=megabytes * 1024 * 1024)


def vmem():
    return pl.BlockSpec(memory_space=pltpu.VMEM)


def place():
    return pl.BlockSpec(memory_space=pl.ANY)


def smem():
    return pl.BlockSpec(memory_space=pltpu.SMEM)


def split(x, parts):
    out = []
    for _ in range(parts):
        piece = x.astype(jnp.bfloat16)
        out.append(piece)
        x = x - piece.astype(jnp.float32)
    return out


def mxu(a, b, dims=((1,), (0,))):
    return lax.dot_general(a, b, (dims, ((), ())), preferred_element_type=jnp.float32)


def prepare_kernel(
    slots, tokens_ref, lives_ref, cells_ref, lengths_ref, sq_ref, sp_ref, pos_ref, sent_ref, out_ref, blocks_ref
):
    c = lax.axis_index("col")
    half = tokens_ref.shape[0] // 2
    width = tokens_ref.shape[2]
    slot = lax.broadcasted_iota(jnp.int32, (slots, width), 0)
    some = LANES // slots
    for j in range(half // some):
        values = []
        for q in range(some):
            at = (c % 2) * half + j * some + q
            value = tokens_ref[at].astype(jnp.float32)
            values.append(jnp.where(slot < lives_ref[at], value, 0.0))
        flipped = jnp.concatenate(values, axis=0).T
        sent_ref[j * width : (j + 1) * width, :] = flipped.astype(jnp.bfloat16)
    out_ref[...] = cells_ref[...]
    passages = lengths_ref.shape[0]
    per = cells_ref.shape[0] // passages
    row = lax.broadcasted_iota(jnp.int32, (TILE, width), 0)

    def trim(p, at):
        last = lax.shift_right_logical(lengths_ref[p] + TILE - 1, 4) - 1
        value = cells_ref[p * per + last].astype(jnp.float32)
        value = jnp.where(row < lengths_ref[p] - last * TILE, value, value[0:1, :])
        out_ref[p * per + last] = value.astype(jnp.bfloat16)
        for b in range(per):
            blocks_ref[at + b] = p * TILE + b
        return at + last + 1

    count = lax.fori_loop(0, passages, trim, 0)
    final = (passages - 1) * TILE + lax.shift_right_logical(lengths_ref[passages - 1] + TILE - 1, 4) - 1
    for i in range(GROUP):
        blocks_ref[count + i] = final
    blocks_ref[blocks_ref.shape[0] - 1] = count
    block, wide = sq_ref.shape
    base = half // some * width
    depth = sp_ref.shape[0]
    vectors = jnp.concatenate([sq_ref[...].astype(jnp.float32), jnp.zeros((block, LANES - wide), jnp.float32)], axis=1)
    line = lax.broadcasted_iota(jnp.int32, (block, LANES), 0)
    lane = lax.broadcasted_iota(jnp.int32, (block, LANES), 1)
    place = jnp.zeros((block, LANES), jnp.int32)
    for q in range(block):
        place = jnp.where(line == q, pos_ref[q], place)
    high, low = lax.shift_right_logical(place, 6), place & 63
    vectors = jnp.where(lane == wide, high.astype(jnp.float32), vectors)
    vectors = jnp.where(lane == wide + 1, low.astype(jnp.float32), vectors).astype(jnp.bfloat16)
    sent_ref[base : base + depth] = sp_ref[...]
    sent_ref[base + depth :] = vectors


def prepare(tokens, lives, cells, lengths, sq, sp, pos):
    block, slots, width = tokens.shape
    base = block // 2 * slots // LANES * width
    return pl.pallas_call(
        functools.partial(prepare_kernel, slots),
        out_shape=(
            jax.ShapeDtypeStruct((base + sp.shape[0] + block, LANES), jnp.bfloat16),
            jax.ShapeDtypeStruct(cells.shape, jnp.bfloat16),
            jax.ShapeDtypeStruct((cells.shape[0] + TILE + GROUP + 1,), jnp.int32),
        ),
        in_specs=[vmem(), smem(), vmem(), smem(), vmem(), vmem(), smem()],
        out_specs=(vmem(), vmem(), smem()),
        compiler_params=params(56),
    )(tokens, lives, cells, lengths, sq, sp, pos)


def teacher_kernel(slots, tasks, shifts, sides, priors, *refs):
    query_refs = dict(zip(shifts, refs))
    refs = refs[len(shifts) :]
    token_refs = dict(zip(sides, refs))
    list_refs = dict(zip(sides, refs[len(sides) :]))
    prior_refs = refs[2 * len(sides) : 2 * len(sides) + priors]
    out_ref, best = refs[-2:]
    passages, lanes = out_ref.shape
    width = token_refs[sides[0]].shape[2]
    r, c = lax.axis_index("row"), lax.axis_index("col")
    rows = lanes // 2 // lax.axis_size("row") * slots
    total = sum([ref[...] for ref in prior_refs], jnp.zeros((passages, lanes), jnp.float32))
    for side, used in tasks:
        tokens_ref, blocks_ref = token_refs[side], list_refs[side]
        per = tokens_ref.shape[0] // passages
        count = blocks_ref[blocks_ref.shape[0] - 1]
        cells = [(query_refs[k], j) for k in used for j in range(rows // LANES)]

        def step(i, carry, tokens_ref=tokens_ref, blocks_ref=blocks_ref, per=per, cells=cells):
            carry = list(carry)
            owner, fresh, values = [], [], []
            for g in range(GROUP):
                entry = blocks_ref[i * GROUP + g]
                p, b = lax.shift_right_logical(entry, 4), entry & (TILE - 1)
                owner.append(pl.multiple_of(p * 8, 8))
                fresh.append(b == 0)
                values.append(tokens_ref[p * per + b])
            block = jnp.concatenate(values, axis=0)
            for n in range(0, len(cells), 2):
                pair = [ref[j * width : (j + 1) * width, :] for ref, j in cells[n : n + 2]]
                sims = mxu(block, jnp.concatenate(pair, axis=1))
                for g in range(GROUP):
                    for l in range(2):
                        top = sims[g * TILE : g * TILE + 8, l * LANES : (l + 1) * LANES]
                        low = sims[g * TILE + 8 : g * TILE + 16, l * LANES : (l + 1) * LANES]
                        kept = jnp.where(fresh[g], NEG, carry[n + l])
                        carry[n + l] = jnp.maximum(kept, jnp.maximum(top, low))
                        best[n + l, pl.ds(owner[g], 8), :] = carry[n + l]
            return tuple(carry)

        lax.fori_loop(
            0,
            lax.shift_right_logical(count + GROUP - 1, GROUP.bit_length() - 1),
            step,
            tuple(jnp.full((8, LANES), NEG, jnp.float32) for _ in cells),
        )
        found = []
        for l in range(len(cells)):
            peak = best[l, pl.ds(0, passages, stride=8), :]
            for s in range(1, 8):
                peak = jnp.maximum(peak, best[l, pl.ds(s, passages, stride=8), :])
            found.append(peak)
        parity = c % 2 if side == 0 else 1 - c % 2
        for n, k in enumerate(used):
            some = rows // LANES
            peaks = jnp.concatenate(found[n * some : (n + 1) * some], axis=1)
            start = parity * (lanes // 2) + (r ^ k) * (rows // slots)
            owner = lax.broadcasted_iota(jnp.int32, (rows, lanes), 0) // slots + start
            member = (owner == lax.broadcasted_iota(jnp.int32, (rows, lanes), 1)).astype(jnp.bfloat16)
            for piece in split(peaks, 3):
                total = total + mxu(piece, member)
    out_ref[...] = total


def teacher(slots, tasks, near, tokens, lists, queries, passages, priors=(), after=(), megabytes=16):
    shifts = sorted({k for _, used in tasks for k in used})
    sides = sorted({side for side, _ in tasks})
    operands = [near[k] for k in shifts] + [tokens[i] for i in sides] + [lists[i] for i in sides]
    specs = [vmem()] * (len(shifts) + len(sides)) + [smem()] * len(sides)
    operands += list(priors) + list(after)
    specs += [vmem()] * len(priors)
    specs += [place()] * len(after)
    most = max(len(used) for _, used in tasks)
    size = tokens[0].size
    rows = queries // 2 // lax.axis_size("row") * slots
    return pl.pallas_call(
        functools.partial(teacher_kernel, slots, tasks, shifts, sides, len(priors)),
        out_shape=jax.ShapeDtypeStruct((passages, queries), jnp.float32),
        in_specs=specs,
        out_specs=vmem(),
        scratch_shapes=[pltpu.VMEM((most * rows // LANES, passages * 8, LANES), jnp.float32)],
        compiler_params=params(megabytes),
        cost_estimate=pl.CostEstimate(
            flops=sum(4 * rows * len(used) * size for _, used in tasks),
            bytes_accessed=2 * size * len(sides),
            transcendentals=0,
        ),
    )(*operands)


def pack_kernel(first, count, pieces, *refs):
    out_ref = refs[-1]
    r = lax.axis_index("row")
    for i in range(out_ref.shape[0]):
        for k, ref in enumerate(refs[:pieces]):
            out_ref[i, r ^ k] = ref[first : first + count, :]


def pack(pieces, first, count, C, after):
    shape = (C, len(pieces), count, pieces[0].shape[1])
    return pl.pallas_call(
        functools.partial(pack_kernel, first, count, len(pieces)),
        out_shape=jax.ShapeDtypeStruct(shape, pieces[0].dtype),
        in_specs=[vmem()] * len(pieces) + [place()],
        out_specs=vmem(),
        compiler_params=params(24),
    )(*pieces, after)


def student_kernel(wide, raw_ref, after_ref, score_ref, vectors_ref, stats_ref, held, flat):
    C, R, rows, span = raw_ref.shape
    r, c = lax.axis_index("row"), lax.axis_index("col")
    queries = score_ref.shape[2]
    block = queries // R
    half = block // 2
    depth = rows - block
    per = depth // wide
    for i in range(R):
        pieces = []
        for h in range(per):
            for j in range(R):
                for x in range(2):
                    held[x, j] = raw_ref[i * per + h, j, depth + x * half : depth + (x + 1) * half]
            pieces.append(held[...].reshape(queries, span).astype(jnp.float32)[:, :wide])
        flat[i] = jnp.concatenate(pieces, axis=1).astype(jnp.bfloat16)
    vectors_ref[...] = flat[r]
    for j in range(R):
        for x in range(2):
            held[x, j] = raw_ref[c, j, depth + x * half : depth + (x + 1) * half]
    meta = held[...].reshape(queries, span).astype(jnp.float32)
    where = meta[:, wide : wide + 1] * 64.0 + meta[:, wide + 1 : wide + 2]
    diag = lax.broadcasted_iota(jnp.int32, (queries, queries), 0) == lax.broadcasted_iota(
        jnp.int32, (queries, queries), 1
    )
    where = jnp.sum(jnp.where(diag, where, 0.0), axis=0, keepdims=True)
    place = where.astype(jnp.int32)
    index = lax.broadcasted_iota(jnp.int32, (span, queries), 0)

    def scores(i, carry):
        peak, score = carry
        total = jnp.zeros((queries, span), jnp.float32)
        for k in range(R):
            total = total + mxu(flat[k], raw_ref[i, k, :depth])
        s = (SCALE * total).T
        score_ref[i] = s
        hot = index + i * span == place
        return jnp.maximum(peak, s), score + jnp.where(hot, s, 0.0)

    low = jnp.full((span, queries), -jnp.inf, jnp.float32)
    peak, score = lax.fori_loop(0, C, scores, (low, jnp.zeros((span, queries), jnp.float32)))
    peak = jnp.max(peak, axis=0, keepdims=True)
    score = jnp.sum(score, axis=0, keepdims=True)
    total = lax.fori_loop(
        0, C, lambda i, t: t + jnp.exp(score_ref[i] - peak), jnp.zeros((span, queries), jnp.float32)
    )
    total = jnp.sum(total, axis=0, keepdims=True)
    stats_ref[0:1, :] = where
    stats_ref[1:2, :] = peak
    stats_ref[2:3, :] = total
    stats_ref[3:4, :] = score
    stats_ref[4:8, :] = jnp.zeros((4, queries), jnp.float32)


def student_scores(raw, after, queries, wide):
    C, R, rows, span = raw.shape
    depth = rows - queries // R
    return pl.pallas_call(
        functools.partial(student_kernel, wide),
        out_shape=(
            jax.ShapeDtypeStruct((C, span, queries), jnp.float32),
            jax.ShapeDtypeStruct((queries, depth), jnp.bfloat16),
            jax.ShapeDtypeStruct((8, queries), jnp.float32),
        ),
        in_specs=[vmem(), place()],
        out_specs=(vmem(),) * 3,
        scratch_shapes=[
            pltpu.VMEM((2, R, queries // R // 2, span), jnp.bfloat16),
            pltpu.VMEM((R, queries, depth), jnp.bfloat16),
        ],
        compiler_params=params(40),
    )(raw, after)


def finish_kernel(wide, t_ref, s_ref, raw_ref, vectors_ref, stats_ref, query_ref, passage_ref, loss_ref, teach):
    C, R, rows, span = raw_ref.shape
    r, c = lax.axis_index("row"), lax.axis_index("col")
    queries = vectors_ref.shape[0]
    depth = vectors_ref.shape[1]
    per = depth // wide
    block = queries // R
    half = queries // 2
    shape = (span, queries)
    where, s_max, s_sum, score = [stats_ref[i : i + 1, :] for i in range(4)]

    def peak(j, t_max):
        pair = [t_ref[2 * j + h].reshape(shape) for h in range(2)]
        for b in range(2):
            t = jnp.concatenate([x[:, b * half : (b + 1) * half] for x in pair], axis=1)
            teach[2 * j + b] = t
            t_max = jnp.maximum(t_max, t)
        return t_max

    t_max = lax.fori_loop(0, C // 2, peak, jnp.full(shape, -jnp.inf, jnp.float32))
    t_max = jnp.max(t_max, axis=0, keepdims=True)

    def totals(i, carry):
        t_sum, cross = carry
        t = teach[i]
        t_exp = jnp.exp(t - t_max)
        teach[i] = t_exp
        return t_sum + t_exp, cross + t_exp * (t - s_ref[i])

    zero = jnp.zeros(shape, jnp.float32)
    t_sum, cross = lax.fori_loop(0, C, totals, (zero, zero))
    t_sum = jnp.sum(t_sum, axis=0, keepdims=True)
    cross = jnp.sum(cross, axis=0, keepdims=True)
    t_lse = t_max + jnp.log(t_sum)
    s_lse = s_max + jnp.log(s_sum)
    each = cross / t_sum - t_lse + 2.0 * s_lse - score
    loss_ref[...] = jnp.sum(each, axis=1, keepdims=True) / queries
    factor = SCALE / queries
    t_factor, s_factor = factor / t_sum, 2.0 * factor / s_sum
    place = where.astype(jnp.int32)
    index = lax.broadcasted_iota(jnp.int32, shape, 0)

    def slope(i):
        hot = index + i * span == place
        gap = jnp.exp(s_ref[i] - s_max) * s_factor - teach[i] * t_factor
        return split(gap - jnp.where(hot, factor, 0.0), 2)

    def gradient(i, total):
        for piece in slope(i):
            total = total + mxu(raw_ref[i, c // per, :depth], piece)
        return total

    flat = lax.fori_loop(0, C, gradient, jnp.zeros((depth, queries), jnp.float32)).T
    sub = block // 2
    for h in range(2):
        lines = functools.reduce(
            jnp.add,
            [jnp.where(r == i, flat[h * half + i * sub : h * half + (i + 1) * sub], 0.0) for i in range(R)],
        )
        query_ref[h * sub : (h + 1) * sub, :] = functools.reduce(
            jnp.add, [jnp.where(c % per == i, lines[:, i * wide : (i + 1) * wide], 0.0) for i in range(per)]
        )
    grads = sum(mxu(piece, vectors_ref[...]) for piece in slope(c))
    passage_ref[...] = grads.T


def finish(t, s, raw, vectors, stats, wide):
    C, R, rows, span = raw.shape
    queries, depth = vectors.shape
    return pl.pallas_call(
        functools.partial(finish_kernel, wide),
        out_shape=(
            jax.ShapeDtypeStruct((queries // R, wide), jnp.float32),
            jax.ShapeDtypeStruct((depth, span), jnp.float32),
            jax.ShapeDtypeStruct((1, 1), jnp.float32),
        ),
        in_specs=[vmem()] * 5,
        out_specs=(vmem(),) * 3,
        scratch_shapes=[pltpu.VMEM((C, span, queries), jnp.float32)],
        compiler_params=params(48),
    )(t, s, raw, vectors, stats)


def shards(query_tokens, query_lengths, passage_tokens, passage_lengths, student_queries, student_passages, positives):
    R, C = lax.axis_size("row"), lax.axis_size("col")
    block, slots, width = query_tokens.shape
    queries = block * R
    local, count = passage_tokens.shape[:2]
    wide = student_queries.shape[1]

    def over_row(x, k):
        return lax.ppermute(x, "row", [(i, i ^ k) for i in range(R)])

    def over_col(x, k):
        return lax.ppermute(x, "col", [(i, i ^ k) for i in range(C)])

    cells = passage_tokens.reshape(local * count // TILE, TILE, width)
    sent, cells, blocks = prepare(
        query_tokens, query_lengths, cells, passage_lengths, student_queries, student_passages.T, positives
    )
    tokens = [cells, over_col(cells, 1)]
    lists = [blocks, over_col(blocks, 1)]
    near = [sent] + [over_row(sent, k) for k in range(1, R)]
    common = dict(near=near, tokens=tokens, lists=lists, queries=queries, passages=local)
    begun = teacher(slots, ((0, (0,)),), megabytes=56, **common)
    score = teacher(slots, ((1, (0, 1)), (0, (1,))), **common)
    base = sent.shape[0] - student_passages.shape[1] - block
    vectors = pack(near, base, sent.shape[0] - base, C, score)
    raw = lax.all_to_all(vectors, "col", 0, 0, tiled=True)
    score = [begun, score]
    for k in range(2, R, 2):
        score = [teacher(slots, ((0, (k, k + 1)), (1, (k, k + 1))), priors=score, after=(vectors,), **common)]
    score = score[0]
    stacked = pack([score] + [over_row(score, k) for k in range(1, R)], 0, local, C, score)
    t = lax.all_to_all(stacked, "col", 0, 0, tiled=True)
    s, vectors, stats = student_scores(raw, stacked, queries, wide)
    query_grads, passage_grads, loss = finish(t, s, raw, vectors, stats, wide)
    return (query_grads, passage_grads.T, loss[0, 0])


def solution(mesh):
    return jax.shard_map(
        shards,
        mesh=mesh,
        in_specs=(
            P("row", None, None),
            P("row"),
            P(("col", "row"), None, None),
            P(("col", "row")),
            P("row", "col"),
            P("col", "row"),
            P("row"),
        ),
        out_specs=(P("row", "col"), P("col", "row"), P()),
        check_vma=False,
    )
```

```python
import functools

import jax
import jax.numpy as jnp
from jax import lax
from jax.experimental import pallas as pl
from jax.experimental.pallas import tpu as pltpu
from jax.sharding import PartitionSpec as P

NEG = -1e30
SCALE = 4.0
TILE = 16
GROUP = 32
LANES = 128


def params(megabytes):
    return pltpu.CompilerParams(vmem_limit_bytes=megabytes * 1024 * 1024)


def vmem():
    return pl.BlockSpec(memory_space=pltpu.VMEM)


def place():
    return pl.BlockSpec(memory_space=pl.ANY)


def smem():
    return pl.BlockSpec(memory_space=pltpu.SMEM)


def split(x, parts):
    out = []
    for _ in range(parts):
        piece = x.astype(jnp.bfloat16)
        out.append(piece)
        x = x - piece.astype(jnp.float32)
    return out


def mxu(a, b, dims=((1,), (0,))):
    return lax.dot_general(a, b, (dims, ((), ())), preferred_element_type=jnp.float32)


def prepare_kernel(
    slots, per, tokens_ref, lives_ref, lengths_ref, sq_ref, sp_ref, pos_ref, sent_ref, blocks_ref
):
    c = lax.axis_index("col")
    half = tokens_ref.shape[0] // 2
    width = tokens_ref.shape[2]
    slot = lax.broadcasted_iota(jnp.int32, (slots, width), 0)
    some = LANES // slots
    for j in range(half // some):
        values = []
        for q in range(some):
            at = (c % 2) * half + j * some + q
            value = tokens_ref[at].astype(jnp.float32)
            values.append(jnp.where(slot < lives_ref[at], value, 0.0))
        flipped = jnp.concatenate(values, axis=0).T
        sent_ref[j * width : (j + 1) * width, :] = flipped.astype(jnp.bfloat16)
    passages = lengths_ref.shape[0]

    def entries(p, at):
        for b in range(per):
            live = jnp.minimum(lengths_ref[p] - b * TILE, TILE) - 1
            blocks_ref[at + b] = p * TILE * TILE + b * TILE + live
        return at + lax.shift_right_logical(lengths_ref[p] + TILE - 1, 4)

    count = lax.fori_loop(0, passages, entries, 0)
    final = blocks_ref[count - 1]
    for i in range(GROUP):
        blocks_ref[count + i] = final
    blocks_ref[blocks_ref.shape[0] - 1] = count
    block, wide = sq_ref.shape
    base = half // some * width
    depth = sp_ref.shape[0]
    vectors = jnp.concatenate([sq_ref[...].astype(jnp.float32), jnp.zeros((block, LANES - wide), jnp.float32)], axis=1)
    line = lax.broadcasted_iota(jnp.int32, (block, LANES), 0)
    lane = lax.broadcasted_iota(jnp.int32, (block, LANES), 1)
    place = jnp.zeros((block, LANES), jnp.int32)
    for q in range(block):
        place = jnp.where(line == q, pos_ref[q], place)
    high, low = lax.shift_right_logical(place, 6), place & 63
    vectors = jnp.where(lane == wide, high.astype(jnp.float32), vectors)
    vectors = jnp.where(lane == wide + 1, low.astype(jnp.float32), vectors).astype(jnp.bfloat16)
    sent_ref[base : base + depth] = sp_ref[...]
    sent_ref[base + depth :] = vectors


def prepare(tokens, lives, cells, lengths, sq, sp, pos):
    per = cells.shape[0] // lengths.shape[0]
    block, slots, width = tokens.shape
    base = block // 2 * slots // LANES * width
    return pl.pallas_call(
        functools.partial(prepare_kernel, slots, per),
        out_shape=(
            jax.ShapeDtypeStruct((base + sp.shape[0] + block, LANES), jnp.bfloat16),
            jax.ShapeDtypeStruct((cells.shape[0] + TILE + GROUP + 1,), jnp.int32),
        ),
        in_specs=[vmem(), smem(), smem(), vmem(), vmem(), smem()],
        out_specs=(vmem(), smem()),
        compiler_params=params(56),
    )(tokens, lives, lengths, sq, sp, pos)


def teacher_kernel(slots, tasks, shifts, sides, priors, *refs):
    query_refs = dict(zip(shifts, refs))
    refs = refs[len(shifts) :]
    token_refs = dict(zip(sides, refs))
    list_refs = dict(zip(sides, refs[len(sides) :]))
    prior_refs = refs[2 * len(sides) : 2 * len(sides) + priors]
    out_ref, best = refs[-2:]
    passages, lanes = out_ref.shape
    width = token_refs[sides[0]].shape[2]
    r, c = lax.axis_index("row"), lax.axis_index("col")
    rows = lanes // 2 // lax.axis_size("row") * slots
    total = sum([ref[...] for ref in prior_refs], jnp.zeros((passages, lanes), jnp.float32))
    line = lax.broadcasted_iota(jnp.int32, (TILE, width), 0)
    for side, used in tasks:
        tokens_ref, blocks_ref = token_refs[side], list_refs[side]
        per = tokens_ref.shape[0] // passages
        count = blocks_ref[blocks_ref.shape[0] - 1]
        cells = [(query_refs[k], j) for k in used for j in range(rows // LANES)]

        def step(i, carry, tokens_ref=tokens_ref, blocks_ref=blocks_ref, per=per, cells=cells):
            carry = list(carry)
            owner, fresh, values = [], [], []
            for g in range(GROUP):
                entry = blocks_ref[i * GROUP + g]
                p, b = lax.shift_right_logical(entry, 8), lax.shift_right_logical(entry, 4) & (TILE - 1)
                owner.append(pl.multiple_of(p * 8, 8))
                fresh.append(b == 0)
                value = tokens_ref[p * per + b].astype(jnp.float32)
                value = jnp.where(line <= (entry & (TILE - 1)), value, value[0:1, :])
                values.append(value.astype(jnp.bfloat16))
            block = jnp.concatenate(values, axis=0)
            for n in range(0, len(cells), 2):
                pair = [ref[j * width : (j + 1) * width, :] for ref, j in cells[n : n + 2]]
                sims = mxu(block, jnp.concatenate(pair, axis=1))
                for g in range(GROUP):
                    for l in range(2):
                        top = sims[g * TILE : g * TILE + 8, l * LANES : (l + 1) * LANES]
                        low = sims[g * TILE + 8 : g * TILE + 16, l * LANES : (l + 1) * LANES]
                        kept = jnp.where(fresh[g], NEG, carry[n + l])
                        carry[n + l] = jnp.maximum(kept, jnp.maximum(top, low))
                        best[n + l, pl.ds(owner[g], 8), :] = carry[n + l]
            return tuple(carry)

        lax.fori_loop(
            0,
            lax.shift_right_logical(count + GROUP - 1, GROUP.bit_length() - 1),
            step,
            tuple(jnp.full((8, LANES), NEG, jnp.float32) for _ in cells),
        )
        found = []
        for l in range(len(cells)):
            peak = best[l, pl.ds(0, passages, stride=8), :]
            for s in range(1, 8):
                peak = jnp.maximum(peak, best[l, pl.ds(s, passages, stride=8), :])
            found.append(peak)
        parity = c % 2 if side == 0 else 1 - c % 2
        for n, k in enumerate(used):
            some = rows // LANES
            peaks = jnp.concatenate(found[n * some : (n + 1) * some], axis=1)
            start = parity * (lanes // 2) + (r ^ k) * (rows // slots)
            owner = lax.broadcasted_iota(jnp.int32, (rows, lanes), 0) // slots + start
            member = (owner == lax.broadcasted_iota(jnp.int32, (rows, lanes), 1)).astype(jnp.bfloat16)
            for piece in split(peaks, 3):
                total = total + mxu(piece, member)
    out_ref[...] = total


def teacher(slots, tasks, near, tokens, lists, queries, passages, priors=(), after=(), megabytes=16):
    shifts = sorted({k for _, used in tasks for k in used})
    sides = sorted({side for side, _ in tasks})
    operands = [near[k] for k in shifts] + [tokens[i] for i in sides] + [lists[i] for i in sides]
    specs = [vmem()] * (len(shifts) + len(sides)) + [smem()] * len(sides)
    operands += list(priors) + list(after)
    specs += [vmem()] * len(priors)
    specs += [place()] * len(after)
    most = max(len(used) for _, used in tasks)
    size = tokens[0].size
    rows = queries // 2 // lax.axis_size("row") * slots
    return pl.pallas_call(
        functools.partial(teacher_kernel, slots, tasks, shifts, sides, len(priors)),
        out_shape=jax.ShapeDtypeStruct((passages, queries), jnp.float32),
        in_specs=specs,
        out_specs=vmem(),
        scratch_shapes=[pltpu.VMEM((most * rows // LANES, passages * 8, LANES), jnp.float32)],
        compiler_params=params(megabytes),
        cost_estimate=pl.CostEstimate(
            flops=sum(4 * rows * len(used) * size for _, used in tasks),
            bytes_accessed=2 * size * len(sides),
            transcendentals=0,
        ),
    )(*operands)


def pack_kernel(axis, first, count, pieces, *refs):
    out_ref, token_ref = refs[-2:]
    me = lax.axis_index("row") if axis == "row" else lax.axis_index("col") // 2
    for k, ref in enumerate(refs[:pieces]):
        out_ref[me ^ k] = ref[first : first + count]
    token_ref[...] = jnp.zeros(token_ref.shape, jnp.float32)


def pack(axis, pieces, first, count, after):
    shape = (len(pieces), count) + pieces[0].shape[1:]
    return pl.pallas_call(
        functools.partial(pack_kernel, axis, first, count, len(pieces)),
        out_shape=(jax.ShapeDtypeStruct(shape, pieces[0].dtype), jax.ShapeDtypeStruct((8, LANES), jnp.float32)),
        in_specs=[vmem()] * len(pieces) + [place()] * len(after),
        out_specs=(vmem(), vmem()),
        compiler_params=params(24),
    )(*pieces, *after)


def loop(count, body, init):
    if count > 4:
        return lax.fori_loop(0, count, body, init)
    for i in range(count):
        init = body(i, init)
    return init


def student_kernel(
    wide, mine_ref, other_ref, after_ref, score_ref, slope_ref, vectors_ref, stats_ref, held, flat
):
    pairs, R, rows, span = mine_ref.shape
    C = 2 * pairs
    r, c = lax.axis_index("row"), lax.axis_index("col")
    queries = score_ref.shape[2]
    block = queries // R
    half = block // 2
    depth = rows - block
    per = depth // wide
    sides = ((mine_ref, c % 2), (other_ref, 1 - c % 2))
    for j in range(pairs):
        for ref, odd in sides:
            for i in range(R):
                for x in range(2):
                    held[2 * j + odd, x, i] = ref[j, i, depth + x * half : depth + (x + 1) * half]

    def columns(index):
        return held[index].reshape(queries, span).astype(jnp.float32)

    for i in range(R):
        pieces = [columns(i * per + h)[:, :wide] for h in range(per)]
        flat[i] = jnp.concatenate(pieces, axis=1).astype(jnp.bfloat16)
    vectors_ref[...] = flat[r]
    meta = columns(c)
    where = meta[:, wide : wide + 1] * 64.0 + meta[:, wide + 1 : wide + 2]
    diag = lax.broadcasted_iota(jnp.int32, (queries, queries), 0) == lax.broadcasted_iota(
        jnp.int32, (queries, queries), 1
    )
    spot = jnp.sum(jnp.where(diag, where, 0.0), axis=0, keepdims=True).astype(jnp.int32)
    index = lax.broadcasted_iota(jnp.int32, (span, queries), 0)

    def scores(j, carry):
        peak, score = carry
        for ref, odd in sides:
            total = jnp.zeros((queries, span), jnp.float32)
            for k in range(R):
                total = total + mxu(flat[k], ref[j, k, :depth])
            s = (SCALE * total).T
            i = 2 * j + odd
            score_ref[i] = s
            hot = index + i * span == spot
            peak, score = jnp.maximum(peak, s), score + jnp.where(hot, s, 0.0)
        return peak, score

    low = jnp.full((span, queries), -jnp.inf, jnp.float32)
    zero = jnp.zeros((span, queries), jnp.float32)
    peak, score = loop(pairs, scores, (low, zero))
    peak = jnp.max(peak, axis=0, keepdims=True)
    score = jnp.sum(score, axis=0, keepdims=True)

    def powers(j, total):
        for i in (2 * j, 2 * j + 1):
            power = jnp.exp(score_ref[i] - peak)
            slope_ref[i] = power
            total = total + power
        return total

    total = jnp.sum(loop(pairs, powers, zero), axis=0, keepdims=True)
    stats_ref[0:1, :] = peak + jnp.log(total)
    stats_ref[1:2, :] = score
    stats_ref[2:8, :] = jnp.zeros((6, queries), jnp.float32)
    factor = SCALE / queries
    scale = 2.0 * factor / total

    def slopes(j, carry):
        for i in (2 * j, 2 * j + 1):
            hot = index + i * span == spot
            slope_ref[i] = slope_ref[i] * scale - jnp.where(hot, factor, 0.0)
        return carry

    loop(pairs, slopes, 0)


def student_scores(mine, other, after, queries, wide):
    pairs, R, rows, span = mine.shape
    depth = rows - queries // R
    C = 2 * pairs
    return pl.pallas_call(
        functools.partial(student_kernel, wide),
        out_shape=(
            jax.ShapeDtypeStruct((C, span, queries), jnp.float32),
            jax.ShapeDtypeStruct((C, span, queries), jnp.float32),
            jax.ShapeDtypeStruct((queries, depth), jnp.bfloat16),
            jax.ShapeDtypeStruct((8, queries), jnp.float32),
        ),
        in_specs=[vmem(), vmem(), place()],
        out_specs=(vmem(),) * 4,
        scratch_shapes=[
            pltpu.VMEM((C, 2, R, queries // R // 2, span), jnp.bfloat16),
            pltpu.VMEM((R, queries, depth), jnp.bfloat16),
        ],
        compiler_params=params(40),
    )(mine, other, after)


def finish_kernel(
    wide,
    t_mine,
    t_other,
    s_ref,
    slope_ref,
    mine_ref,
    other_ref,
    vectors_ref,
    stats_ref,
    query_ref,
    passage_ref,
    loss_ref,
    teach,
):
    pairs, R, rows, span = mine_ref.shape
    r, c = lax.axis_index("row"), lax.axis_index("col")
    queries = vectors_ref.shape[0]
    depth = vectors_ref.shape[1]
    per = depth // wide
    block = queries // R
    half = queries // 2
    shape = (span, queries)
    odd = c % 2
    s_lse, score = stats_ref[0:1, :], stats_ref[1:2, :]

    def peak(j, t_max):
        a, b = t_mine[j].reshape(shape), t_other[j].reshape(shape)
        pair = [jnp.where(odd == 0, a, b), jnp.where(odd == 0, b, a)]
        for x in range(2):
            t = jnp.concatenate([v[:, x * half : (x + 1) * half] for v in pair], axis=1)
            teach[2 * j + x] = t
            t_max = jnp.maximum(t_max, t)
        return t_max

    t_max = loop(pairs, peak, jnp.full(shape, -jnp.inf, jnp.float32))
    t_max = jnp.max(t_max, axis=0, keepdims=True)

    def totals(j, carry):
        t_sum, cross = carry
        for i in (2 * j, 2 * j + 1):
            t = teach[i]
            t_exp = jnp.exp(t - t_max)
            teach[i] = t_exp
            t_sum, cross = t_sum + t_exp, cross + t_exp * (t - s_ref[i])
        return t_sum, cross

    zero = jnp.zeros(shape, jnp.float32)
    t_sum, cross = loop(pairs, totals, (zero, zero))
    t_sum = jnp.sum(t_sum, axis=0, keepdims=True)
    cross = jnp.sum(cross, axis=0, keepdims=True)
    each = cross / t_sum - (t_max + jnp.log(t_sum)) + 2.0 * s_lse - score
    loss_ref[...] = jnp.sum(each, axis=1, keepdims=True) / queries
    t_factor = SCALE / queries / t_sum

    def slope(i):
        return split(slope_ref[i] - teach[i] * t_factor, 2)

    def gradient(j, total):
        for ref, side in ((mine_ref, odd), (other_ref, 1 - odd)):
            vectors = ref[j, c // per, :depth]
            for piece in slope(2 * j + side):
                total = total + mxu(vectors, piece)
        return total

    flat = loop(pairs, gradient, jnp.zeros((depth, queries), jnp.float32)).T
    sub = block // 2
    for h in range(2):
        lines = functools.reduce(
            jnp.add,
            [jnp.where(r == i, flat[h * half + i * sub : h * half + (i + 1) * sub], 0.0) for i in range(R)],
        )
        query_ref[h * sub : (h + 1) * sub, :] = functools.reduce(
            jnp.add, [jnp.where(c % per == i, lines[:, i * wide : (i + 1) * wide], 0.0) for i in range(per)]
        )
    grads = sum(mxu(piece, vectors_ref[...]) for piece in slope(c))
    passage_ref[...] = grads.T


def finish(t_mine, t_other, s, slope, mine, other, vectors, stats, wide):
    pairs, R, rows, span = mine.shape
    queries, depth = vectors.shape
    return pl.pallas_call(
        functools.partial(finish_kernel, wide),
        out_shape=(
            jax.ShapeDtypeStruct((queries // R, wide), jnp.float32),
            jax.ShapeDtypeStruct((depth, span), jnp.float32),
            jax.ShapeDtypeStruct((1, 1), jnp.float32),
        ),
        in_specs=[vmem()] * 8,
        out_specs=(vmem(),) * 3,
        scratch_shapes=[pltpu.VMEM((2 * pairs, span, queries), jnp.float32)],
        compiler_params=params(48),
    )(t_mine, t_other, s, slope, mine, other, vectors, stats)


def shards(query_tokens, query_lengths, passage_tokens, passage_lengths, student_queries, student_passages, positives):
    R, C = lax.axis_size("row"), lax.axis_size("col")
    block, slots, width = query_tokens.shape
    queries = block * R
    local, count = passage_tokens.shape[:2]
    wide = student_queries.shape[1]

    def over_row(x, k):
        return lax.ppermute(x, "row", [(i, i ^ k) for i in range(R)])

    def over_col(x, k):
        return lax.ppermute(x, "col", [(i, i ^ k) for i in range(C)])

    def spread(stack, after):
        parts = [stack] + [over_col(stack, k) for k in range(2, C, 2)]
        mine, _ = pack("col", parts, 0, stack.shape[0], after)
        return mine, over_col(mine, 1)

    cells = passage_tokens.reshape(local * count // TILE, TILE, width)
    tokens = [cells, over_col(cells, 1)]
    sent, blocks = prepare(
        query_tokens, query_lengths, cells, passage_lengths, student_queries, student_passages.T, positives
    )
    lists = [blocks, over_col(blocks, 1)]
    near = [sent] + [over_row(sent, k) for k in range(1, R)]
    common = dict(near=near, tokens=tokens, lists=lists, queries=queries, passages=local)
    score = teacher(slots, ((0, (0,)),), **common)
    score = teacher(slots, ((1, (0, 1)), (0, (1,))), priors=(score,), **common)
    for k in range(2, R - 2, 2):
        score = teacher(slots, ((0, (k, k + 1)), (1, (k, k + 1))), priors=(score,), **common)
    score = teacher(slots, ((0, (R - 2,)), (1, (R - 2,))), priors=(score,), **common)
    base = sent.shape[0] - student_passages.shape[1] - block
    vectors, token = pack("row", near, base, sent.shape[0] - base, (score,))
    score = teacher(slots, ((0, (R - 1,)), (1, (R - 1,))), priors=(score,), after=(token,), **common)
    scores = [score] + [over_row(score, k) for k in range(1, R)]
    mine, other = spread(vectors, (scores[1],))
    stack, token = pack("row", scores, 0, local, ())
    s, slope, vectors, stats = student_scores(mine, other, token, queries, wide)
    t_mine, t_other = spread(stack, ())
    query_grads, passage_grads, loss = finish(t_mine, t_other, s, slope, mine, other, vectors, stats, wide)
    return (query_grads, passage_grads.T, loss[0, 0])


def solution(mesh):
    return jax.shard_map(
        shards,
        mesh=mesh,
        in_specs=(
            P("row", None, None),
            P("row"),
            P(("col", "row"), None, None),
            P(("col", "row")),
            P("row", "col"),
            P("col", "row"),
            P("row"),
        ),
        out_specs=(P("row", "col"), P("col", "row"), P()),
        check_vma=False,
    )
```

```python
import functools

import jax
import jax.numpy as jnp
from jax import lax
from jax.experimental import pallas as pl
from jax.experimental.pallas import tpu as pltpu
from jax.sharding import PartitionSpec as P

NEG = -1e30
SCALE = 4.0
TILE = 16
GROUP = 32
LANES = 128


def params(megabytes):
    return pltpu.CompilerParams(vmem_limit_bytes=megabytes * 1024 * 1024)


def vmem():
    return pl.BlockSpec(memory_space=pltpu.VMEM)


def place():
    return pl.BlockSpec(memory_space=pl.ANY)


def smem():
    return pl.BlockSpec(memory_space=pltpu.SMEM)


def split(x, parts):
    out = []
    for _ in range(parts):
        piece = x.astype(jnp.bfloat16)
        out.append(piece)
        x = x - piece.astype(jnp.float32)
    return out


def mxu(a, b, dims=((1,), (0,))):
    return lax.dot_general(a, b, (dims, ((), ())), preferred_element_type=jnp.float32)


def prepare_kernel(
    slots, per, tokens_ref, lives_ref, lengths_ref, sq_ref, sp_ref, pos_ref, sent_ref, blocks_ref
):
    c = lax.axis_index("col")
    half = tokens_ref.shape[0] // 2
    width = tokens_ref.shape[2]
    slot = lax.broadcasted_iota(jnp.int32, (slots, width), 0)
    some = LANES // slots
    for j in range(half // some):
        values = []
        for q in range(some):
            at = (c % 2) * half + j * some + q
            value = tokens_ref[at].astype(jnp.float32)
            values.append(jnp.where(slot < lives_ref[at], value, 0.0))
        flipped = jnp.concatenate(values, axis=0).T
        sent_ref[j * width : (j + 1) * width, :] = flipped.astype(jnp.bfloat16)
    passages = lengths_ref.shape[0]

    def entries(p, at):
        for b in range(per):
            live = jnp.minimum(lengths_ref[p] - b * TILE, TILE) - 1
            blocks_ref[at + b] = p * TILE * TILE + b * TILE + live
        return at + lax.shift_right_logical(lengths_ref[p] + TILE - 1, 4)

    count = lax.fori_loop(0, passages, entries, 0)
    final = blocks_ref[count - 1]
    for i in range(2 * GROUP):
        blocks_ref[count + i] = final
    blocks_ref[blocks_ref.shape[0] - 1] = count
    block, wide = sq_ref.shape
    base = half // some * width
    depth = sp_ref.shape[0]
    vectors = jnp.concatenate([sq_ref[...].astype(jnp.float32), jnp.zeros((block, LANES - wide), jnp.float32)], axis=1)
    line = lax.broadcasted_iota(jnp.int32, (block, LANES), 0)
    lane = lax.broadcasted_iota(jnp.int32, (block, LANES), 1)
    place = jnp.zeros((block, LANES), jnp.int32)
    for q in range(block):
        place = jnp.where(line == q, pos_ref[q], place)
    high, low = lax.shift_right_logical(place, 6), place & 63
    vectors = jnp.where(lane == wide, high.astype(jnp.float32), vectors)
    vectors = jnp.where(lane == wide + 1, low.astype(jnp.float32), vectors).astype(jnp.bfloat16)
    sent_ref[base : base + depth] = sp_ref[...]
    sent_ref[base + depth :] = vectors


def prepare(tokens, lives, cells, lengths, sq, sp, pos):
    per = cells.shape[0] // lengths.shape[0]
    block, slots, width = tokens.shape
    base = block // 2 * slots // LANES * width
    return pl.pallas_call(
        functools.partial(prepare_kernel, slots, per),
        out_shape=(
            jax.ShapeDtypeStruct((base + sp.shape[0] + block, LANES), jnp.bfloat16),
            jax.ShapeDtypeStruct((cells.shape[0] + 2 * GROUP + 1,), jnp.int32),
        ),
        in_specs=[vmem(), smem(), smem(), vmem(), vmem(), smem()],
        out_specs=(vmem(), smem()),
        compiler_params=params(56),
    )(tokens, lives, lengths, sq, sp, pos)


def teacher_kernel(slots, tasks, shifts, sides, priors, *refs):
    query_refs = dict(zip(shifts, refs))
    refs = refs[len(shifts) :]
    token_refs = dict(zip(sides, refs))
    list_refs = dict(zip(sides, refs[len(sides) :]))
    prior_refs = refs[2 * len(sides) : 2 * len(sides) + priors]
    out_ref, best, ahead = refs[-3:]
    passages, lanes = out_ref.shape
    width = token_refs[sides[0]].shape[2]
    r, c = lax.axis_index("row"), lax.axis_index("col")
    rows = lanes // 2 // lax.axis_size("row") * slots
    total = sum([ref[...] for ref in prior_refs], jnp.zeros((passages, lanes), jnp.float32))
    line = lax.broadcasted_iota(jnp.int32, (TILE, width), 0)
    for side, used in tasks:
        tokens_ref, blocks_ref = token_refs[side], list_refs[side]
        per = tokens_ref.shape[0] // passages
        count = blocks_ref[blocks_ref.shape[0] - 1]
        cells = [(query_refs[k], j) for k in used for j in range(rows // LANES)]

        def gather(i, tokens_ref=tokens_ref, blocks_ref=blocks_ref, per=per):
            for g in range(GROUP):
                entry = blocks_ref[i * GROUP + g]
                p, b = lax.shift_right_logical(entry, 8), lax.shift_right_logical(entry, 4) & (TILE - 1)
                value = tokens_ref[p * per + b].astype(jnp.float32)
                value = jnp.where(line <= (entry & (TILE - 1)), value, value[0:1, :])
                ahead[g * TILE : (g + 1) * TILE, :] = value.astype(jnp.bfloat16)

        def step(i, carry, blocks_ref=blocks_ref, cells=cells, gather=gather):
            carry = list(carry)
            block = ahead[...]
            gather(i + 1)
            owner, fresh = [], []
            for g in range(GROUP):
                entry = blocks_ref[i * GROUP + g]
                owner.append(pl.multiple_of(lax.shift_right_logical(entry, 8) * 8, 8))
                fresh.append((entry & (TILE * TILE - TILE)) == 0)
            for n in range(0, len(cells), 2):
                pair = [ref[j * width : (j + 1) * width, :] for ref, j in cells[n : n + 2]]
                sims = mxu(block, jnp.concatenate(pair, axis=1))
                for g in range(GROUP):
                    for l in range(2):
                        top = sims[g * TILE : g * TILE + 8, l * LANES : (l + 1) * LANES]
                        low = sims[g * TILE + 8 : g * TILE + 16, l * LANES : (l + 1) * LANES]
                        kept = jnp.where(fresh[g], NEG, carry[n + l])
                        carry[n + l] = jnp.maximum(kept, jnp.maximum(top, low))
                        best[n + l, pl.ds(owner[g], 8), :] = carry[n + l]
            return tuple(carry)

        gather(0)
        lax.fori_loop(
            0,
            lax.shift_right_logical(count + GROUP - 1, GROUP.bit_length() - 1),
            step,
            tuple(jnp.full((8, LANES), NEG, jnp.float32) for _ in cells),
        )
        found = []
        for l in range(len(cells)):
            peak = best[l, pl.ds(0, passages, stride=8), :]
            for s in range(1, 8):
                peak = jnp.maximum(peak, best[l, pl.ds(s, passages, stride=8), :])
            found.append(peak)
        parity = c % 2 if side == 0 else 1 - c % 2
        for n, k in enumerate(used):
            some = rows // LANES
            peaks = jnp.concatenate(found[n * some : (n + 1) * some], axis=1)
            start = parity * (lanes // 2) + (r ^ k) * (rows // slots)
            owner = lax.broadcasted_iota(jnp.int32, (rows, lanes), 0) // slots + start
            member = (owner == lax.broadcasted_iota(jnp.int32, (rows, lanes), 1)).astype(jnp.bfloat16)
            for piece in split(peaks, 3):
                total = total + mxu(piece, member)
    out_ref[...] = total


def teacher(slots, tasks, near, tokens, lists, queries, passages, priors=(), after=(), megabytes=16):
    shifts = sorted({k for _, used in tasks for k in used})
    sides = sorted({side for side, _ in tasks})
    operands = [near[k] for k in shifts] + [tokens[i] for i in sides] + [lists[i] for i in sides]
    specs = [vmem()] * (len(shifts) + len(sides)) + [smem()] * len(sides)
    operands += list(priors) + list(after)
    specs += [vmem()] * len(priors)
    specs += [place()] * len(after)
    most = max(len(used) for _, used in tasks)
    size, sent_width = tokens[0].size, tokens[0].shape[2]
    rows = queries // 2 // lax.axis_size("row") * slots
    return pl.pallas_call(
        functools.partial(teacher_kernel, slots, tasks, shifts, sides, len(priors)),
        out_shape=jax.ShapeDtypeStruct((passages, queries), jnp.float32),
        in_specs=specs,
        out_specs=vmem(),
        scratch_shapes=[
            pltpu.VMEM((most * rows // LANES, passages * 8, LANES), jnp.float32),
            pltpu.VMEM((GROUP * TILE, sent_width), jnp.bfloat16),
        ],
        compiler_params=params(megabytes),
        cost_estimate=pl.CostEstimate(
            flops=sum(4 * rows * len(used) * size for _, used in tasks),
            bytes_accessed=2 * size * len(sides),
            transcendentals=0,
        ),
    )(*operands)


def pack_kernel(axis, first, count, pieces, *refs):
    out_ref, token_ref = refs[-2:]
    me = lax.axis_index("row") if axis == "row" else lax.axis_index("col") // 2
    for k, ref in enumerate(refs[:pieces]):
        out_ref[me ^ k] = ref[first : first + count]
    token_ref[...] = jnp.zeros(token_ref.shape, jnp.float32)


def pack(axis, pieces, first, count, after):
    shape = (len(pieces), count) + pieces[0].shape[1:]
    return pl.pallas_call(
        functools.partial(pack_kernel, axis, first, count, len(pieces)),
        out_shape=(jax.ShapeDtypeStruct(shape, pieces[0].dtype), jax.ShapeDtypeStruct((8, LANES), jnp.float32)),
        in_specs=[vmem()] * len(pieces) + [place()] * len(after),
        out_specs=(vmem(), vmem()),
        compiler_params=params(24),
    )(*pieces, *after)


def loop(count, body, init):
    if count > 4:
        return lax.fori_loop(0, count, body, init)
    for i in range(count):
        init = body(i, init)
    return init


def student_kernel(
    wide, mine_ref, other_ref, after_ref, score_ref, slope_ref, vectors_ref, stats_ref, held, flat
):
    pairs, R, rows, span = mine_ref.shape
    C = 2 * pairs
    r, c = lax.axis_index("row"), lax.axis_index("col")
    queries = score_ref.shape[2]
    block = queries // R
    half = block // 2
    depth = rows - block
    per = depth // wide
    sides = ((mine_ref, c % 2), (other_ref, 1 - c % 2))
    for j in range(pairs):
        for ref, odd in sides:
            for i in range(R):
                for x in range(2):
                    held[2 * j + odd, x, i] = ref[j, i, depth + x * half : depth + (x + 1) * half]

    def columns(index):
        return held[index].reshape(queries, span).astype(jnp.float32)

    for i in range(R):
        pieces = [columns(i * per + h)[:, :wide] for h in range(per)]
        flat[i] = jnp.concatenate(pieces, axis=1).astype(jnp.bfloat16)
    vectors_ref[...] = flat[r]
    meta = columns(c)
    where = meta[:, wide : wide + 1] * 64.0 + meta[:, wide + 1 : wide + 2]
    diag = lax.broadcasted_iota(jnp.int32, (queries, queries), 0) == lax.broadcasted_iota(
        jnp.int32, (queries, queries), 1
    )
    spot = jnp.sum(jnp.where(diag, where, 0.0), axis=0, keepdims=True).astype(jnp.int32)
    index = lax.broadcasted_iota(jnp.int32, (span, queries), 0)

    def scores(j, carry):
        peak, score = carry
        for ref, odd in sides:
            total = jnp.zeros((queries, span), jnp.float32)
            for k in range(R):
                total = total + mxu(flat[k], ref[j, k, :depth])
            s = (SCALE * total).T
            i = 2 * j + odd
            score_ref[i] = s
            hot = index + i * span == spot
            peak, score = jnp.maximum(peak, s), score + jnp.where(hot, s, 0.0)
        return peak, score

    low = jnp.full((span, queries), -jnp.inf, jnp.float32)
    zero = jnp.zeros((span, queries), jnp.float32)
    peak, score = loop(pairs, scores, (low, zero))
    peak = jnp.max(peak, axis=0, keepdims=True)
    score = jnp.sum(score, axis=0, keepdims=True)

    def powers(j, total):
        for i in (2 * j, 2 * j + 1):
            power = jnp.exp(score_ref[i] - peak)
            slope_ref[i] = power
            total = total + power
        return total

    total = jnp.sum(loop(pairs, powers, zero), axis=0, keepdims=True)
    stats_ref[0:1, :] = peak + jnp.log(total)
    stats_ref[1:2, :] = score
    stats_ref[2:8, :] = jnp.zeros((6, queries), jnp.float32)
    factor = SCALE / queries
    scale = 2.0 * factor / total

    def slopes(j, carry):
        for i in (2 * j, 2 * j + 1):
            hot = index + i * span == spot
            slope_ref[i] = slope_ref[i] * scale - jnp.where(hot, factor, 0.0)
        return carry

    loop(pairs, slopes, 0)


def student_scores(mine, other, after, queries, wide):
    pairs, R, rows, span = mine.shape
    depth = rows - queries // R
    C = 2 * pairs
    return pl.pallas_call(
        functools.partial(student_kernel, wide),
        out_shape=(
            jax.ShapeDtypeStruct((C, span, queries), jnp.float32),
            jax.ShapeDtypeStruct((C, span, queries), jnp.float32),
            jax.ShapeDtypeStruct((queries, depth), jnp.bfloat16),
            jax.ShapeDtypeStruct((8, queries), jnp.float32),
        ),
        in_specs=[vmem(), vmem(), place()],
        out_specs=(vmem(),) * 4,
        scratch_shapes=[
            pltpu.VMEM((C, 2, R, queries // R // 2, span), jnp.bfloat16),
            pltpu.VMEM((R, queries, depth), jnp.bfloat16),
        ],
        compiler_params=params(40),
    )(mine, other, after)


def finish_kernel(
    wide,
    t_mine,
    t_other,
    s_ref,
    slope_ref,
    mine_ref,
    other_ref,
    vectors_ref,
    stats_ref,
    query_ref,
    passage_ref,
    loss_ref,
    teach,
):
    pairs, R, rows, span = mine_ref.shape
    r, c = lax.axis_index("row"), lax.axis_index("col")
    queries = vectors_ref.shape[0]
    depth = vectors_ref.shape[1]
    per = depth // wide
    block = queries // R
    half = queries // 2
    shape = (span, queries)
    odd = c % 2
    s_lse, score = stats_ref[0:1, :], stats_ref[1:2, :]

    def peak(j, t_max):
        a, b = t_mine[j].reshape(shape), t_other[j].reshape(shape)
        pair = [jnp.where(odd == 0, a, b), jnp.where(odd == 0, b, a)]
        for x in range(2):
            t = jnp.concatenate([v[:, x * half : (x + 1) * half] for v in pair], axis=1)
            teach[2 * j + x] = t
            t_max = jnp.maximum(t_max, t)
        return t_max

    t_max = loop(pairs, peak, jnp.full(shape, -jnp.inf, jnp.float32))
    t_max = jnp.max(t_max, axis=0, keepdims=True)

    def totals(j, carry):
        t_sum, cross = carry
        for i in (2 * j, 2 * j + 1):
            t = teach[i]
            t_exp = jnp.exp(t - t_max)
            teach[i] = t_exp
            t_sum, cross = t_sum + t_exp, cross + t_exp * (t - s_ref[i])
        return t_sum, cross

    zero = jnp.zeros(shape, jnp.float32)
    t_sum, cross = loop(pairs, totals, (zero, zero))
    t_sum = jnp.sum(t_sum, axis=0, keepdims=True)
    cross = jnp.sum(cross, axis=0, keepdims=True)
    each = cross / t_sum - (t_max + jnp.log(t_sum)) + 2.0 * s_lse - score
    loss_ref[...] = jnp.sum(each, axis=1, keepdims=True) / queries
    t_factor = SCALE / queries / t_sum

    def slope(i):
        return split(slope_ref[i] - teach[i] * t_factor, 2)

    def gradient(j, total):
        for ref, side in ((mine_ref, odd), (other_ref, 1 - odd)):
            vectors = ref[j, c // per, :depth]
            for piece in slope(2 * j + side):
                total = total + mxu(vectors, piece)
        return total

    flat = loop(pairs, gradient, jnp.zeros((depth, queries), jnp.float32)).T
    sub = block // 2
    for h in range(2):
        lines = functools.reduce(
            jnp.add,
            [jnp.where(r == i, flat[h * half + i * sub : h * half + (i + 1) * sub], 0.0) for i in range(R)],
        )
        query_ref[h * sub : (h + 1) * sub, :] = functools.reduce(
            jnp.add, [jnp.where(c % per == i, lines[:, i * wide : (i + 1) * wide], 0.0) for i in range(per)]
        )
    grads = sum(mxu(piece, vectors_ref[...]) for piece in slope(c))
    passage_ref[...] = grads.T


def finish(t_mine, t_other, s, slope, mine, other, vectors, stats, wide):
    pairs, R, rows, span = mine.shape
    queries, depth = vectors.shape
    return pl.pallas_call(
        functools.partial(finish_kernel, wide),
        out_shape=(
            jax.ShapeDtypeStruct((queries // R, wide), jnp.float32),
            jax.ShapeDtypeStruct((depth, span), jnp.float32),
            jax.ShapeDtypeStruct((1, 1), jnp.float32),
        ),
        in_specs=[vmem()] * 8,
        out_specs=(vmem(),) * 3,
        scratch_shapes=[pltpu.VMEM((2 * pairs, span, queries), jnp.float32)],
        compiler_params=params(48),
    )(t_mine, t_other, s, slope, mine, other, vectors, stats)


def shards(query_tokens, query_lengths, passage_tokens, passage_lengths, student_queries, student_passages, positives):
    R, C = lax.axis_size("row"), lax.axis_size("col")
    block, slots, width = query_tokens.shape
    queries = block * R
    local, count = passage_tokens.shape[:2]
    wide = student_queries.shape[1]

    def over_row(x, k):
        return lax.ppermute(x, "row", [(i, i ^ k) for i in range(R)])

    def over_col(x, k):
        return lax.ppermute(x, "col", [(i, i ^ k) for i in range(C)])

    def spread(stack, after):
        parts = [stack] + [over_col(stack, k) for k in range(2, C, 2)]
        mine, _ = pack("col", parts, 0, stack.shape[0], after)
        return mine, over_col(mine, 1)

    cells = passage_tokens.reshape(local * count // TILE, TILE, width)
    tokens = [cells, over_col(cells, 1)]
    sent, blocks = prepare(
        query_tokens, query_lengths, cells, passage_lengths, student_queries, student_passages.T, positives
    )
    lists = [blocks, over_col(blocks, 1)]
    near = [sent] + [over_row(sent, k) for k in range(1, R)]
    common = dict(near=near, tokens=tokens, lists=lists, queries=queries, passages=local)
    begun = teacher(slots, ((0, (0,)),), megabytes=56, **common)
    score = teacher(slots, ((1, (0, 1)), (0, (1,))), after=(begun,), **common)
    for k in range(2, R - 2, 2):
        score = teacher(slots, ((0, (k, k + 1)), (1, (k, k + 1))), priors=(score,), **common)
    score = teacher(slots, ((0, (R - 2,)), (1, (R - 2,))), priors=(score,), **common)
    base = sent.shape[0] - student_passages.shape[1] - block
    vectors, token = pack("row", near, base, sent.shape[0] - base, (score,))
    score = teacher(slots, ((0, (R - 1,)), (1, (R - 1,))), priors=(score, begun), after=(token,), **common)
    scores = [score] + [over_row(score, k) for k in range(1, R)]
    stack, token = pack("row", scores, 0, local, ())
    mine, other = spread(vectors, (token,))
    s, slope, vectors, stats = student_scores(mine, other, token, queries, wide)
    t_mine, t_other = spread(stack, ())
    query_grads, passage_grads, loss = finish(t_mine, t_other, s, slope, mine, other, vectors, stats, wide)
    return (query_grads, passage_grads.T, loss[0, 0])


def solution(mesh):
    return jax.shard_map(
        shards,
        mesh=mesh,
        in_specs=(
            P("row", None, None),
            P("row"),
            P(("col", "row"), None, None),
            P(("col", "row")),
            P("row", "col"),
            P("col", "row"),
            P("row"),
        ),
        out_specs=(P("row", "col"), P("col", "row"), P()),
        check_vma=False,
    )
```

```python
import functools

import jax
import jax.numpy as jnp
from jax import lax
from jax.experimental import pallas as pl
from jax.experimental.pallas import tpu as pltpu
from jax.sharding import PartitionSpec as P

NEG = -1e30
SCALE = 4.0
TILE = 16
GROUP = 32
LANES = 128


def params(megabytes):
    return pltpu.CompilerParams(vmem_limit_bytes=megabytes * 1024 * 1024)


def vmem():
    return pl.BlockSpec(memory_space=pltpu.VMEM)


def place():
    return pl.BlockSpec(memory_space=pl.ANY)


def smem():
    return pl.BlockSpec(memory_space=pltpu.SMEM)


def split(x, parts):
    out = []
    for _ in range(parts):
        piece = x.astype(jnp.bfloat16)
        out.append(piece)
        x = x - piece.astype(jnp.float32)
    return out


def mxu(a, b, dims=((1,), (0,))):
    return lax.dot_general(a, b, (dims, ((), ())), preferred_element_type=jnp.float32)


def prepare_kernel(
    slots, per, tokens_ref, lives_ref, lengths_ref, sq_ref, sp_ref, pos_ref, sent_ref, blocks_ref
):
    c = lax.axis_index("col")
    half = tokens_ref.shape[0] // 2
    width = tokens_ref.shape[2]
    slot = lax.broadcasted_iota(jnp.int32, (slots, width), 0)
    some = LANES // slots
    for j in range(half // some):
        values = []
        for q in range(some):
            at = (c % 2) * half + j * some + q
            value = tokens_ref[at].astype(jnp.float32)
            values.append(jnp.where(slot < lives_ref[at], value, 0.0))
        flipped = jnp.concatenate(values, axis=0).T
        sent_ref[j * width : (j + 1) * width, :] = flipped.astype(jnp.bfloat16)
    passages = lengths_ref.shape[0]

    def entries(p, at):
        for b in range(per):
            live = jnp.minimum(lengths_ref[p] - b * TILE, TILE) - 1
            blocks_ref[at + b] = p * TILE * TILE + b * TILE + live
        return at + lax.shift_right_logical(lengths_ref[p] + TILE - 1, 4)

    count = lax.fori_loop(0, passages, entries, 0)
    final = blocks_ref[count - 1]
    for i in range(GROUP):
        blocks_ref[count + i] = final
    blocks_ref[blocks_ref.shape[0] - 1] = count
    block, wide = sq_ref.shape
    base = half // some * width
    depth = sp_ref.shape[0]
    vectors = jnp.concatenate([sq_ref[...].astype(jnp.float32), jnp.zeros((block, LANES - wide), jnp.float32)], axis=1)
    line = lax.broadcasted_iota(jnp.int32, (block, LANES), 0)
    lane = lax.broadcasted_iota(jnp.int32, (block, LANES), 1)
    place = jnp.zeros((block, LANES), jnp.int32)
    for q in range(block):
        place = jnp.where(line == q, pos_ref[q], place)
    high, low = lax.shift_right_logical(place, 6), place & 63
    vectors = jnp.where(lane == wide, high.astype(jnp.float32), vectors)
    vectors = jnp.where(lane == wide + 1, low.astype(jnp.float32), vectors).astype(jnp.bfloat16)
    sent_ref[base : base + depth] = sp_ref[...]
    sent_ref[base + depth :] = vectors


def prepare(tokens, lives, cells, lengths, sq, sp, pos):
    per = cells.shape[0] // lengths.shape[0]
    block, slots, width = tokens.shape
    base = block // 2 * slots // LANES * width
    return pl.pallas_call(
        functools.partial(prepare_kernel, slots, per),
        out_shape=(
            jax.ShapeDtypeStruct((base + sp.shape[0] + block, LANES), jnp.bfloat16),
            jax.ShapeDtypeStruct((cells.shape[0] + TILE + GROUP + 1,), jnp.int32),
        ),
        in_specs=[vmem(), smem(), smem(), vmem(), vmem(), smem()],
        out_specs=(vmem(), smem()),
        compiler_params=params(56),
    )(tokens, lives, lengths, sq, sp, pos)


def teacher_kernel(slots, tasks, shifts, sides, priors, *refs):
    query_refs = dict(zip(shifts, refs))
    refs = refs[len(shifts) :]
    token_refs = dict(zip(sides, refs))
    list_refs = dict(zip(sides, refs[len(sides) :]))
    prior_refs = refs[2 * len(sides) : 2 * len(sides) + priors]
    out_ref, best = refs[-2:]
    passages, lanes = out_ref.shape
    width = token_refs[sides[0]].shape[2]
    r, c = lax.axis_index("row"), lax.axis_index("col")
    rows = lanes // 2 // lax.axis_size("row") * slots
    total = sum([ref[...] for ref in prior_refs], jnp.zeros((passages, lanes), jnp.float32))
    line = lax.broadcasted_iota(jnp.int32, (TILE, width), 0)
    for side, used in tasks:
        tokens_ref, blocks_ref = token_refs[side], list_refs[side]
        per = tokens_ref.shape[0] // passages
        count = blocks_ref[blocks_ref.shape[0] - 1]
        cells = [(query_refs[k], j) for k in used for j in range(rows // LANES)]

        def step(i, carry, tokens_ref=tokens_ref, blocks_ref=blocks_ref, per=per, cells=cells):
            carry = list(carry)
            owner, fresh, values = [], [], []
            for g in range(GROUP):
                entry = blocks_ref[i * GROUP + g]
                p, b = lax.shift_right_logical(entry, 8), lax.shift_right_logical(entry, 4) & (TILE - 1)
                owner.append(pl.multiple_of(p * 8, 8))
                fresh.append(b == 0)
                value = tokens_ref[p * per + b].astype(jnp.float32)
                value = jnp.where(line <= (entry & (TILE - 1)), value, value[0:1, :])
                values.append(value.astype(jnp.bfloat16))
            block = jnp.concatenate(values, axis=0)
            for n in range(0, len(cells), 2):
                pair = [ref[j * width : (j + 1) * width, :] for ref, j in cells[n : n + 2]]
                sims = mxu(block, jnp.concatenate(pair, axis=1))
                for g in range(GROUP):
                    for l in range(2):
                        top = sims[g * TILE : g * TILE + 8, l * LANES : (l + 1) * LANES]
                        low = sims[g * TILE + 8 : g * TILE + 16, l * LANES : (l + 1) * LANES]
                        kept = jnp.where(fresh[g], NEG, carry[n + l])
                        carry[n + l] = jnp.maximum(kept, jnp.maximum(top, low))
                        best[n + l, pl.ds(owner[g], 8), :] = carry[n + l]
            return tuple(carry)

        steps = lax.shift_right_logical(count + GROUP - 1, GROUP.bit_length() - 1)
        twice = lax.shift_right_logical(steps, 1)
        begin = tuple(jnp.full((8, LANES), NEG, jnp.float32) for _ in cells)
        begin = lax.fori_loop(0, twice, lambda i, x, step=step: step(2 * i + 1, step(2 * i, x)), begin)
        lax.fori_loop(2 * twice, steps, step, begin)
        found = []
        for l in range(len(cells)):
            peak = best[l, pl.ds(0, passages, stride=8), :]
            for s in range(1, 8):
                peak = jnp.maximum(peak, best[l, pl.ds(s, passages, stride=8), :])
            found.append(peak)
        parity = c % 2 if side == 0 else 1 - c % 2
        for n, k in enumerate(used):
            some = rows // LANES
            peaks = jnp.concatenate(found[n * some : (n + 1) * some], axis=1)
            start = parity * (lanes // 2) + (r ^ k) * (rows // slots)
            owner = lax.broadcasted_iota(jnp.int32, (rows, lanes), 0) // slots + start
            member = (owner == lax.broadcasted_iota(jnp.int32, (rows, lanes), 1)).astype(jnp.bfloat16)
            for piece in split(peaks, 3):
                total = total + mxu(piece, member)
    out_ref[...] = total


def teacher(slots, tasks, near, tokens, lists, queries, passages, priors=(), after=(), megabytes=16):
    shifts = sorted({k for _, used in tasks for k in used})
    sides = sorted({side for side, _ in tasks})
    operands = [near[k] for k in shifts] + [tokens[i] for i in sides] + [lists[i] for i in sides]
    specs = [vmem()] * (len(shifts) + len(sides)) + [smem()] * len(sides)
    operands += list(priors) + list(after)
    specs += [vmem()] * len(priors)
    specs += [place()] * len(after)
    most = max(len(used) for _, used in tasks)
    size = tokens[0].size
    rows = queries // 2 // lax.axis_size("row") * slots
    return pl.pallas_call(
        functools.partial(teacher_kernel, slots, tasks, shifts, sides, len(priors)),
        out_shape=jax.ShapeDtypeStruct((passages, queries), jnp.float32),
        in_specs=specs,
        out_specs=vmem(),
        scratch_shapes=[pltpu.VMEM((most * rows // LANES, passages * 8, LANES), jnp.float32)],
        compiler_params=params(megabytes),
        cost_estimate=pl.CostEstimate(
            flops=sum(4 * rows * len(used) * size for _, used in tasks),
            bytes_accessed=2 * size * len(sides),
            transcendentals=0,
        ),
    )(*operands)


def pack_kernel(axis, first, count, pieces, *refs):
    out_ref, token_ref = refs[-2:]
    me = lax.axis_index("row") if axis == "row" else lax.axis_index("col") // 2
    for k, ref in enumerate(refs[:pieces]):
        out_ref[me ^ k] = ref[first : first + count]
    token_ref[...] = jnp.zeros(token_ref.shape, jnp.float32)


def pack(axis, pieces, first, count, after):
    shape = (len(pieces), count) + pieces[0].shape[1:]
    return pl.pallas_call(
        functools.partial(pack_kernel, axis, first, count, len(pieces)),
        out_shape=(jax.ShapeDtypeStruct(shape, pieces[0].dtype), jax.ShapeDtypeStruct((8, LANES), jnp.float32)),
        in_specs=[vmem()] * len(pieces) + [place()] * len(after),
        out_specs=(vmem(), vmem()),
        compiler_params=params(24),
    )(*pieces, *after)


def loop(count, body, init):
    if count > 4:
        return lax.fori_loop(0, count, body, init)
    for i in range(count):
        init = body(i, init)
    return init


def student_kernel(
    wide, mine_ref, other_ref, after_ref, score_ref, slope_ref, vectors_ref, stats_ref, held, flat
):
    pairs, R, rows, span = mine_ref.shape
    C = 2 * pairs
    r, c = lax.axis_index("row"), lax.axis_index("col")
    queries = score_ref.shape[2]
    block = queries // R
    half = block // 2
    depth = rows - block
    per = depth // wide
    sides = ((mine_ref, c % 2), (other_ref, 1 - c % 2))
    for j in range(pairs):
        for ref, odd in sides:
            for i in range(R):
                for x in range(2):
                    held[2 * j + odd, x, i] = ref[j, i, depth + x * half : depth + (x + 1) * half]

    def columns(index):
        return held[index].reshape(queries, span).astype(jnp.float32)

    for i in range(R):
        pieces = [columns(i * per + h)[:, :wide] for h in range(per)]
        flat[i] = jnp.concatenate(pieces, axis=1).astype(jnp.bfloat16)
    vectors_ref[...] = flat[r]
    meta = columns(c)
    where = meta[:, wide : wide + 1] * 64.0 + meta[:, wide + 1 : wide + 2]
    diag = lax.broadcasted_iota(jnp.int32, (queries, queries), 0) == lax.broadcasted_iota(
        jnp.int32, (queries, queries), 1
    )
    spot = jnp.sum(jnp.where(diag, where, 0.0), axis=0, keepdims=True).astype(jnp.int32)
    index = lax.broadcasted_iota(jnp.int32, (span, queries), 0)

    def scores(j, carry):
        peak, score = carry
        for ref, odd in sides:
            total = jnp.zeros((queries, span), jnp.float32)
            for k in range(R):
                total = total + mxu(flat[k], ref[j, k, :depth])
            s = (SCALE * total).T
            i = 2 * j + odd
            score_ref[i] = s
            hot = index + i * span == spot
            peak, score = jnp.maximum(peak, s), score + jnp.where(hot, s, 0.0)
        return peak, score

    low = jnp.full((span, queries), -jnp.inf, jnp.float32)
    zero = jnp.zeros((span, queries), jnp.float32)
    peak, score = loop(pairs, scores, (low, zero))
    peak = jnp.max(peak, axis=0, keepdims=True)
    score = jnp.sum(score, axis=0, keepdims=True)

    def powers(j, total):
        for i in (2 * j, 2 * j + 1):
            power = jnp.exp(score_ref[i] - peak)
            slope_ref[i] = power
            total = total + power
        return total

    total = jnp.sum(loop(pairs, powers, zero), axis=0, keepdims=True)
    stats_ref[0:1, :] = peak + jnp.log(total)
    stats_ref[1:2, :] = score
    stats_ref[2:8, :] = jnp.zeros((6, queries), jnp.float32)
    factor = SCALE / queries
    scale = 2.0 * factor / total

    def slopes(j, carry):
        for i in (2 * j, 2 * j + 1):
            hot = index + i * span == spot
            slope_ref[i] = slope_ref[i] * scale - jnp.where(hot, factor, 0.0)
        return carry

    loop(pairs, slopes, 0)


def student_scores(mine, other, after, queries, wide):
    pairs, R, rows, span = mine.shape
    depth = rows - queries // R
    C = 2 * pairs
    return pl.pallas_call(
        functools.partial(student_kernel, wide),
        out_shape=(
            jax.ShapeDtypeStruct((C, span, queries), jnp.float32),
            jax.ShapeDtypeStruct((C, span, queries), jnp.float32),
            jax.ShapeDtypeStruct((queries, depth), jnp.bfloat16),
            jax.ShapeDtypeStruct((8, queries), jnp.float32),
        ),
        in_specs=[vmem(), vmem(), place()],
        out_specs=(vmem(),) * 4,
        scratch_shapes=[
            pltpu.VMEM((C, 2, R, queries // R // 2, span), jnp.bfloat16),
            pltpu.VMEM((R, queries, depth), jnp.bfloat16),
        ],
        compiler_params=params(40),
    )(mine, other, after)


def finish_kernel(
    wide,
    t_mine,
    t_other,
    s_ref,
    slope_ref,
    mine_ref,
    other_ref,
    vectors_ref,
    stats_ref,
    query_ref,
    passage_ref,
    loss_ref,
    teach,
):
    pairs, R, rows, span = mine_ref.shape
    r, c = lax.axis_index("row"), lax.axis_index("col")
    queries = vectors_ref.shape[0]
    depth = vectors_ref.shape[1]
    per = depth // wide
    block = queries // R
    half = queries // 2
    shape = (span, queries)
    odd = c % 2
    s_lse, score = stats_ref[0:1, :], stats_ref[1:2, :]

    def peak(j, t_max):
        a, b = t_mine[j].reshape(shape), t_other[j].reshape(shape)
        pair = [jnp.where(odd == 0, a, b), jnp.where(odd == 0, b, a)]
        for x in range(2):
            t = jnp.concatenate([v[:, x * half : (x + 1) * half] for v in pair], axis=1)
            teach[2 * j + x] = t
            t_max = jnp.maximum(t_max, t)
        return t_max

    t_max = loop(pairs, peak, jnp.full(shape, -jnp.inf, jnp.float32))
    t_max = jnp.max(t_max, axis=0, keepdims=True)

    def totals(j, carry):
        t_sum, cross = carry
        for i in (2 * j, 2 * j + 1):
            t = teach[i]
            t_exp = jnp.exp(t - t_max)
            teach[i] = t_exp
            t_sum, cross = t_sum + t_exp, cross + t_exp * (t - s_ref[i])
        return t_sum, cross

    zero = jnp.zeros(shape, jnp.float32)
    t_sum, cross = loop(pairs, totals, (zero, zero))
    t_sum = jnp.sum(t_sum, axis=0, keepdims=True)
    cross = jnp.sum(cross, axis=0, keepdims=True)
    each = cross / t_sum - (t_max + jnp.log(t_sum)) + 2.0 * s_lse - score
    loss_ref[...] = jnp.sum(each, axis=1, keepdims=True) / queries
    t_factor = SCALE / queries / t_sum

    def slope(i):
        return split(slope_ref[i] - teach[i] * t_factor, 2)

    def gradient(j, total):
        for ref, side in ((mine_ref, odd), (other_ref, 1 - odd)):
            vectors = ref[j, c // per, :depth]
            for piece in slope(2 * j + side):
                total = total + mxu(vectors, piece)
        return total

    flat = loop(pairs, gradient, jnp.zeros((depth, queries), jnp.float32)).T
    sub = block // 2
    for h in range(2):
        lines = functools.reduce(
            jnp.add,
            [jnp.where(r == i, flat[h * half + i * sub : h * half + (i + 1) * sub], 0.0) for i in range(R)],
        )
        query_ref[h * sub : (h + 1) * sub, :] = functools.reduce(
            jnp.add, [jnp.where(c % per == i, lines[:, i * wide : (i + 1) * wide], 0.0) for i in range(per)]
        )
    grads = sum(mxu(piece, vectors_ref[...]) for piece in slope(c))
    passage_ref[...] = grads.T


def finish(t_mine, t_other, s, slope, mine, other, vectors, stats, wide):
    pairs, R, rows, span = mine.shape
    queries, depth = vectors.shape
    return pl.pallas_call(
        functools.partial(finish_kernel, wide),
        out_shape=(
            jax.ShapeDtypeStruct((queries // R, wide), jnp.float32),
            jax.ShapeDtypeStruct((depth, span), jnp.float32),
            jax.ShapeDtypeStruct((1, 1), jnp.float32),
        ),
        in_specs=[vmem()] * 8,
        out_specs=(vmem(),) * 3,
        scratch_shapes=[pltpu.VMEM((2 * pairs, span, queries), jnp.float32)],
        compiler_params=params(48),
    )(t_mine, t_other, s, slope, mine, other, vectors, stats)


def shards(query_tokens, query_lengths, passage_tokens, passage_lengths, student_queries, student_passages, positives):
    R, C = lax.axis_size("row"), lax.axis_size("col")
    block, slots, width = query_tokens.shape
    queries = block * R
    local, count = passage_tokens.shape[:2]
    wide = student_queries.shape[1]

    def over_row(x, k):
        return lax.ppermute(x, "row", [(i, i ^ k) for i in range(R)])

    def over_col(x, k):
        return lax.ppermute(x, "col", [(i, i ^ k) for i in range(C)])

    def spread(stack, after):
        parts = [stack] + [over_col(stack, k) for k in range(2, C, 2)]
        mine, _ = pack("col", parts, 0, stack.shape[0], after)
        return mine, over_col(mine, 1)

    cells = passage_tokens.reshape(local * count // TILE, TILE, width)
    tokens = [cells, over_col(cells, 1)]
    sent, blocks = prepare(
        query_tokens, query_lengths, cells, passage_lengths, student_queries, student_passages.T, positives
    )
    lists = [blocks, over_col(blocks, 1)]
    near = [sent] + [over_row(sent, k) for k in range(1, R)]
    common = dict(near=near, tokens=tokens, lists=lists, queries=queries, passages=local)
    begun = teacher(slots, ((0, (0,)),), megabytes=56, **common)
    score = teacher(slots, ((1, (0, 1)), (0, (1,))), after=(begun,), **common)
    base = sent.shape[0] - student_passages.shape[1] - block
    vectors, token = pack("row", near, base, sent.shape[0] - base, (score,))
    priors = (score, begun)
    for k in range(2, R, 2):
        score = teacher(slots, ((0, (k, k + 1)), (1, (k, k + 1))), priors=priors, after=(token,), **common)
        priors = (score,)
    scores = [score] + [over_row(score, k) for k in range(1, R)]
    stack, token = pack("row", scores, 0, local, ())
    mine, other = spread(vectors, (token,))
    s, slope, vectors, stats = student_scores(mine, other, token, queries, wide)
    t_mine, t_other = spread(stack, ())
    query_grads, passage_grads, loss = finish(t_mine, t_other, s, slope, mine, other, vectors, stats, wide)
    return (query_grads, passage_grads.T, loss[0, 0])


def solution(mesh):
    return jax.shard_map(
        shards,
        mesh=mesh,
        in_specs=(
            P("row", None, None),
            P("row"),
            P(("col", "row"), None, None),
            P(("col", "row")),
            P("row", "col"),
            P("col", "row"),
            P("row"),
        ),
        out_specs=(P("row", "col"), P("col", "row"), P()),
        check_vma=False,
    )
```

```python
import functools

import jax
import jax.numpy as jnp
from jax import lax
from jax.experimental import pallas as pl
from jax.experimental.pallas import tpu as pltpu
from jax.sharding import PartitionSpec as P

NEG = -1e30
SCALE = 4.0
TILE = 16
GROUP = 32
LANES = 128


def params(megabytes):
    return pltpu.CompilerParams(vmem_limit_bytes=megabytes * 1024 * 1024)


def vmem():
    return pl.BlockSpec(memory_space=pltpu.VMEM)


def place():
    return pl.BlockSpec(memory_space=pl.ANY)


def smem():
    return pl.BlockSpec(memory_space=pltpu.SMEM)


def split(x, parts):
    out = []
    for _ in range(parts):
        piece = x.astype(jnp.bfloat16)
        out.append(piece)
        x = x - piece.astype(jnp.float32)
    return out


def mxu(a, b, dims=((1,), (0,))):
    return lax.dot_general(a, b, (dims, ((), ())), preferred_element_type=jnp.float32)


def prepare_kernel(
    slots, per, tokens_ref, lives_ref, lengths_ref, sq_ref, sp_ref, pos_ref, sent_ref, blocks_ref
):
    c = lax.axis_index("col")
    half = tokens_ref.shape[0] // 2
    width = tokens_ref.shape[2]
    slot = lax.broadcasted_iota(jnp.int32, (slots, width), 0)
    some = LANES // slots
    for j in range(half // some):
        values = []
        for q in range(some):
            at = (c % 2) * half + j * some + q
            value = tokens_ref[at].astype(jnp.float32)
            values.append(jnp.where(slot < lives_ref[at], value, 0.0))
        flipped = jnp.concatenate(values, axis=0).T
        sent_ref[j * width : (j + 1) * width, :] = flipped.astype(jnp.bfloat16)
    passages = lengths_ref.shape[0]

    def entries(p, at):
        for b in range(per):
            live = jnp.minimum(lengths_ref[p] - b * TILE, TILE) - 1
            blocks_ref[at + b] = p * TILE * TILE + b * TILE + live
        return at + lax.shift_right_logical(lengths_ref[p] + TILE - 1, 4)

    count = lax.fori_loop(0, passages, entries, 0)
    final = blocks_ref[count - 1]
    for i in range(GROUP):
        blocks_ref[count + i] = final
    blocks_ref[blocks_ref.shape[0] - 1] = count
    block, wide = sq_ref.shape
    base = half // some * width
    depth = sp_ref.shape[0]
    vectors = jnp.concatenate([sq_ref[...].astype(jnp.float32), jnp.zeros((block, LANES - wide), jnp.float32)], axis=1)
    line = lax.broadcasted_iota(jnp.int32, (block, LANES), 0)
    lane = lax.broadcasted_iota(jnp.int32, (block, LANES), 1)
    place = jnp.zeros((block, LANES), jnp.int32)
    for q in range(block):
        place = jnp.where(line == q, pos_ref[q], place)
    high, low = lax.shift_right_logical(place, 6), place & 63
    vectors = jnp.where(lane == wide, high.astype(jnp.float32), vectors)
    vectors = jnp.where(lane == wide + 1, low.astype(jnp.float32), vectors).astype(jnp.bfloat16)
    sent_ref[base : base + depth] = sp_ref[...]
    sent_ref[base + depth :] = vectors


def prepare(tokens, lives, cells, lengths, sq, sp, pos):
    per = cells.shape[0] // lengths.shape[0]
    block, slots, width = tokens.shape
    base = block // 2 * slots // LANES * width
    return pl.pallas_call(
        functools.partial(prepare_kernel, slots, per),
        out_shape=(
            jax.ShapeDtypeStruct((base + sp.shape[0] + block, LANES), jnp.bfloat16),
            jax.ShapeDtypeStruct((cells.shape[0] + TILE + GROUP + 1,), jnp.int32),
        ),
        in_specs=[vmem(), smem(), smem(), vmem(), vmem(), smem()],
        out_specs=(vmem(), smem()),
        compiler_params=params(56),
    )(tokens, lives, lengths, sq, sp, pos)


def teacher_kernel(slots, tasks, shifts, sides, priors, copies, *refs):
    query_refs = dict(zip(shifts, refs))
    refs = refs[len(shifts) :]
    token_refs = dict(zip(sides, refs))
    list_refs = dict(zip(sides, refs[len(sides) :]))
    prior_refs = refs[2 * len(sides) : 2 * len(sides) + priors]
    out_ref, best = refs[-2:]
    passages, lanes = out_ref.shape[-2:]
    width = token_refs[sides[0]].shape[2]
    r, c = lax.axis_index("row"), lax.axis_index("col")
    rows = lanes // 2 // lax.axis_size("row") * slots
    total = sum([ref[...] for ref in prior_refs], jnp.zeros((passages, lanes), jnp.float32))
    line = lax.broadcasted_iota(jnp.int32, (TILE, width), 0)
    for side, used in tasks:
        tokens_ref, blocks_ref = token_refs[side], list_refs[side]
        per = tokens_ref.shape[0] // passages
        count = blocks_ref[blocks_ref.shape[0] - 1]
        cells = [(query_refs[k], j) for k in used for j in range(rows // LANES)]

        def step(i, carry, tokens_ref=tokens_ref, blocks_ref=blocks_ref, per=per, cells=cells):
            carry = list(carry)
            owner, fresh, values = [], [], []
            for g in range(GROUP):
                entry = blocks_ref[i * GROUP + g]
                p, b = lax.shift_right_logical(entry, 8), lax.shift_right_logical(entry, 4) & (TILE - 1)
                owner.append(pl.multiple_of(p * 8, 8))
                fresh.append(b == 0)
                value = tokens_ref[p * per + b].astype(jnp.float32)
                value = jnp.where(line <= (entry & (TILE - 1)), value, value[0:1, :])
                values.append(value.astype(jnp.bfloat16))
            block = jnp.concatenate(values, axis=0)
            for n in range(0, len(cells), 2):
                pair = [ref[j * width : (j + 1) * width, :] for ref, j in cells[n : n + 2]]
                sims = mxu(block, jnp.concatenate(pair, axis=1))
                for g in range(GROUP):
                    for l in range(2):
                        top = sims[g * TILE : g * TILE + 8, l * LANES : (l + 1) * LANES]
                        low = sims[g * TILE + 8 : g * TILE + 16, l * LANES : (l + 1) * LANES]
                        kept = jnp.where(fresh[g], NEG, carry[n + l])
                        carry[n + l] = jnp.maximum(kept, jnp.maximum(top, low))
                        best[n + l, pl.ds(owner[g], 8), :] = carry[n + l]
            return tuple(carry)

        steps = lax.shift_right_logical(count + GROUP - 1, GROUP.bit_length() - 1)
        twice = lax.shift_right_logical(steps, 1)
        begin = tuple(jnp.full((8, LANES), NEG, jnp.float32) for _ in cells)
        begin = lax.fori_loop(0, twice, lambda i, x, step=step: step(2 * i + 1, step(2 * i, x)), begin)
        lax.fori_loop(2 * twice, steps, step, begin)
        found = []
        for l in range(len(cells)):
            peak = best[l, pl.ds(0, passages, stride=8), :]
            for s in range(1, 8):
                peak = jnp.maximum(peak, best[l, pl.ds(s, passages, stride=8), :])
            found.append(peak)
        parity = c % 2 if side == 0 else 1 - c % 2
        for n, k in enumerate(used):
            some = rows // LANES
            peaks = jnp.concatenate(found[n * some : (n + 1) * some], axis=1)
            start = parity * (lanes // 2) + (r ^ k) * (rows // slots)
            owner = lax.broadcasted_iota(jnp.int32, (rows, lanes), 0) // slots + start
            member = (owner == lax.broadcasted_iota(jnp.int32, (rows, lanes), 1)).astype(jnp.bfloat16)
            for piece in split(peaks, 3):
                total = total + mxu(piece, member)
    if copies:
        for i in range(copies):
            out_ref[i] = total
    else:
        out_ref[...] = total


def teacher(slots, tasks, near, tokens, lists, queries, passages, priors=(), after=(), megabytes=16, copies=0):
    shifts = sorted({k for _, used in tasks for k in used})
    sides = sorted({side for side, _ in tasks})
    operands = [near[k] for k in shifts] + [tokens[i] for i in sides] + [lists[i] for i in sides]
    specs = [vmem()] * (len(shifts) + len(sides)) + [smem()] * len(sides)
    operands += list(priors) + list(after)
    specs += [vmem()] * len(priors)
    specs += [place()] * len(after)
    most = max(len(used) for _, used in tasks)
    size = tokens[0].size
    rows = queries // 2 // lax.axis_size("row") * slots
    return pl.pallas_call(
        functools.partial(teacher_kernel, slots, tasks, shifts, sides, len(priors), copies),
        out_shape=jax.ShapeDtypeStruct((copies, passages, queries)[0 if copies else 1 :], jnp.float32),
        in_specs=specs,
        out_specs=vmem(),
        scratch_shapes=[pltpu.VMEM((most * rows // LANES, passages * 8, LANES), jnp.float32)],
        compiler_params=params(megabytes),
        cost_estimate=pl.CostEstimate(
            flops=sum(4 * rows * len(used) * size for _, used in tasks),
            bytes_accessed=2 * size * len(sides),
            transcendentals=0,
        ),
    )(*operands)


def pack_kernel(axis, first, count, pieces, *refs):
    out_ref, token_ref = refs[-2:]
    me = lax.axis_index("row") if axis == "row" else lax.axis_index("col") // 2
    for k, ref in enumerate(refs[:pieces]):
        for i in range(out_ref.shape[0]):
            out_ref[i, me ^ k] = ref[first : first + count]
    token_ref[...] = jnp.zeros(token_ref.shape, jnp.float32)


def pack(axis, pieces, first, count, after, copies=1):
    shape = (copies, len(pieces), count) + pieces[0].shape[1:]
    return pl.pallas_call(
        functools.partial(pack_kernel, axis, first, count, len(pieces)),
        out_shape=(jax.ShapeDtypeStruct(shape, pieces[0].dtype), jax.ShapeDtypeStruct((8, LANES), jnp.float32)),
        in_specs=[vmem()] * len(pieces) + [place()] * len(after),
        out_specs=(vmem(), vmem()),
        compiler_params=params(24),
    )(*pieces, *after)


def loop(count, body, init):
    if count > 4:
        return lax.fori_loop(0, count, body, init)
    for i in range(count):
        init = body(i, init)
    return init


def student_kernel(
    wide, mine_ref, other_ref, after_ref, score_ref, slope_ref, vectors_ref, stats_ref, held, flat
):
    pairs, R, rows, span = mine_ref.shape
    C = 2 * pairs
    r, c = lax.axis_index("row"), lax.axis_index("col")
    queries = score_ref.shape[2]
    block = queries // R
    half = block // 2
    depth = rows - block
    per = depth // wide
    sides = ((mine_ref, c % 2), (other_ref, 1 - c % 2))
    for j in range(pairs):
        for ref, odd in sides:
            for i in range(R):
                for x in range(2):
                    held[2 * j + odd, x, i] = ref[j, i, depth + x * half : depth + (x + 1) * half]

    def columns(index):
        return held[index].reshape(queries, span).astype(jnp.float32)

    for i in range(R):
        pieces = [columns(i * per + h)[:, :wide] for h in range(per)]
        flat[i] = jnp.concatenate(pieces, axis=1).astype(jnp.bfloat16)
    vectors_ref[...] = flat[r]
    meta = columns(c)
    where = meta[:, wide : wide + 1] * 64.0 + meta[:, wide + 1 : wide + 2]
    diag = lax.broadcasted_iota(jnp.int32, (queries, queries), 0) == lax.broadcasted_iota(
        jnp.int32, (queries, queries), 1
    )
    spot = jnp.sum(jnp.where(diag, where, 0.0), axis=0, keepdims=True).astype(jnp.int32)
    index = lax.broadcasted_iota(jnp.int32, (span, queries), 0)

    def scores(j, carry):
        peak, score = carry
        for ref, odd in sides:
            total = jnp.zeros((queries, span), jnp.float32)
            for k in range(R):
                total = total + mxu(flat[k], ref[j, k, :depth])
            s = (SCALE * total).T
            i = 2 * j + odd
            score_ref[i] = s
            hot = index + i * span == spot
            peak, score = jnp.maximum(peak, s), score + jnp.where(hot, s, 0.0)
        return peak, score

    low = jnp.full((span, queries), -jnp.inf, jnp.float32)
    zero = jnp.zeros((span, queries), jnp.float32)
    peak, score = loop(pairs, scores, (low, zero))
    peak = jnp.max(peak, axis=0, keepdims=True)
    score = jnp.sum(score, axis=0, keepdims=True)

    def powers(j, total):
        for i in (2 * j, 2 * j + 1):
            power = jnp.exp(score_ref[i] - peak)
            slope_ref[i] = power
            total = total + power
        return total

    total = jnp.sum(loop(pairs, powers, zero), axis=0, keepdims=True)
    stats_ref[0:1, :] = peak + jnp.log(total)
    stats_ref[1:2, :] = score
    stats_ref[2:8, :] = jnp.zeros((6, queries), jnp.float32)
    factor = SCALE / queries
    scale = 2.0 * factor / total

    def slopes(j, carry):
        for i in (2 * j, 2 * j + 1):
            hot = index + i * span == spot
            slope_ref[i] = slope_ref[i] * scale - jnp.where(hot, factor, 0.0)
        return carry

    loop(pairs, slopes, 0)


def student_scores(mine, other, after, queries, wide):
    pairs, R, rows, span = mine.shape
    depth = rows - queries // R
    C = 2 * pairs
    return pl.pallas_call(
        functools.partial(student_kernel, wide),
        out_shape=(
            jax.ShapeDtypeStruct((C, span, queries), jnp.float32),
            jax.ShapeDtypeStruct((C, span, queries), jnp.float32),
            jax.ShapeDtypeStruct((queries, depth), jnp.bfloat16),
            jax.ShapeDtypeStruct((8, queries), jnp.float32),
        ),
        in_specs=[vmem(), vmem(), place()],
        out_specs=(vmem(),) * 4,
        scratch_shapes=[
            pltpu.VMEM((C, 2, R, queries // R // 2, span), jnp.bfloat16),
            pltpu.VMEM((R, queries, depth), jnp.bfloat16),
        ],
        compiler_params=params(40),
    )(mine, other, after)


def finish_kernel(
    wide,
    t_mine,
    t_other,
    s_ref,
    slope_ref,
    mine_ref,
    other_ref,
    vectors_ref,
    stats_ref,
    query_ref,
    passage_ref,
    loss_ref,
    teach,
):
    pairs, R, rows, span = mine_ref.shape
    r, c = lax.axis_index("row"), lax.axis_index("col")
    queries = vectors_ref.shape[0]
    depth = vectors_ref.shape[1]
    per = depth // wide
    block = queries // R
    half = queries // 2
    shape = (span, queries)
    odd = c % 2
    s_lse, score = stats_ref[0:1, :], stats_ref[1:2, :]

    def peak(j, t_max):
        a, b = t_mine[j].reshape(shape), t_other[j].reshape(shape)
        pair = [jnp.where(odd == 0, a, b), jnp.where(odd == 0, b, a)]
        for x in range(2):
            t = jnp.concatenate([v[:, x * half : (x + 1) * half] for v in pair], axis=1)
            teach[2 * j + x] = t
            t_max = jnp.maximum(t_max, t)
        return t_max

    t_max = loop(pairs, peak, jnp.full(shape, -jnp.inf, jnp.float32))
    t_max = jnp.max(t_max, axis=0, keepdims=True)

    def totals(j, carry):
        t_sum, cross = carry
        for i in (2 * j, 2 * j + 1):
            t = teach[i]
            t_exp = jnp.exp(t - t_max)
            teach[i] = t_exp
            t_sum, cross = t_sum + t_exp, cross + t_exp * (t - s_ref[i])
        return t_sum, cross

    zero = jnp.zeros(shape, jnp.float32)
    t_sum, cross = loop(pairs, totals, (zero, zero))
    t_sum = jnp.sum(t_sum, axis=0, keepdims=True)
    cross = jnp.sum(cross, axis=0, keepdims=True)
    each = cross / t_sum - (t_max + jnp.log(t_sum)) + 2.0 * s_lse - score
    loss_ref[...] = jnp.sum(each, axis=1, keepdims=True) / queries
    t_factor = SCALE / queries / t_sum

    def slope(i):
        return split(slope_ref[i] - teach[i] * t_factor, 2)

    def gradient(j, total):
        for ref, side in ((mine_ref, odd), (other_ref, 1 - odd)):
            vectors = ref[j, c // per, :depth]
            for piece in slope(2 * j + side):
                total = total + mxu(vectors, piece)
        return total

    flat = loop(pairs, gradient, jnp.zeros((depth, queries), jnp.float32)).T
    sub = block // 2
    for h in range(2):
        lines = functools.reduce(
            jnp.add,
            [jnp.where(r == i, flat[h * half + i * sub : h * half + (i + 1) * sub], 0.0) for i in range(R)],
        )
        query_ref[h * sub : (h + 1) * sub, :] = functools.reduce(
            jnp.add, [jnp.where(c % per == i, lines[:, i * wide : (i + 1) * wide], 0.0) for i in range(per)]
        )
    grads = sum(mxu(piece, vectors_ref[...]) for piece in slope(c))
    passage_ref[...] = grads.T


def finish(t_mine, t_other, s, slope, mine, other, vectors, stats, wide):
    pairs, R, rows, span = mine.shape
    queries, depth = vectors.shape
    return pl.pallas_call(
        functools.partial(finish_kernel, wide),
        out_shape=(
            jax.ShapeDtypeStruct((queries // R, wide), jnp.float32),
            jax.ShapeDtypeStruct((depth, span), jnp.float32),
            jax.ShapeDtypeStruct((1, 1), jnp.float32),
        ),
        in_specs=[vmem()] * 8,
        out_specs=(vmem(),) * 3,
        scratch_shapes=[pltpu.VMEM((2 * pairs, span, queries), jnp.float32)],
        compiler_params=params(48),
    )(t_mine, t_other, s, slope, mine, other, vectors, stats)


def shards(query_tokens, query_lengths, passage_tokens, passage_lengths, student_queries, student_passages, positives):
    R, C = lax.axis_size("row"), lax.axis_size("col")
    block, slots, width = query_tokens.shape
    queries = block * R
    local, count = passage_tokens.shape[:2]
    wide = student_queries.shape[1]

    def over_row(x, k):
        return lax.ppermute(x, "row", [(i, i ^ k) for i in range(R)])

    def over_col(x, k):
        return lax.ppermute(x, "col", [(i, i ^ k) for i in range(C)])

    cells = passage_tokens.reshape(local * count // TILE, TILE, width)
    tokens = [cells, over_col(cells, 1)]
    sent, blocks = prepare(
        query_tokens, query_lengths, cells, passage_lengths, student_queries, student_passages.T, positives
    )
    lists = [blocks, over_col(blocks, 1)]
    near = [sent] + [over_row(sent, k) for k in range(1, R)]
    common = dict(near=near, tokens=tokens, lists=lists, queries=queries, passages=local)
    begun = teacher(slots, ((0, (0,)),), megabytes=56, **common)
    score = teacher(slots, ((1, (0, 1)), (0, (1,))), after=(begun,), **common)
    base = sent.shape[0] - student_passages.shape[1] - block
    same = [[i for i in range(C) if i % 2 == odd] for odd in range(2)]
    vectors, token = pack("row", near, base, sent.shape[0] - base, (score,), C // 2)
    mine = lax.all_to_all(vectors, "col", 0, 0, axis_index_groups=same, tiled=True)
    priors = (score, begun)
    for k in range(2, R, 2):
        copies = R if k == R - 2 else 0
        score = teacher(
            slots, ((0, (k, k + 1)), (1, (k, k + 1))), priors=priors, after=(token,), copies=copies, **common
        )
        priors = (score,)
    stack = lax.all_to_all(score, "row", 0, 0, tiled=True)
    mine, stack = lax.optimization_barrier((mine, stack))
    other = over_col(mine, 1)
    parts = [stack] + [over_col(stack, k) for k in range(2, C, 2)]
    t_mine, token = pack("col", parts, 0, R, ())
    t_mine = t_mine[0]
    t_other = over_col(t_mine, 1)
    s, slope, vectors, stats = student_scores(mine, other, token, queries, wide)
    query_grads, passage_grads, loss = finish(t_mine, t_other, s, slope, mine, other, vectors, stats, wide)
    return (query_grads, passage_grads.T, loss[0, 0])


def solution(mesh):
    return jax.shard_map(
        shards,
        mesh=mesh,
        in_specs=(
            P("row", None, None),
            P("row"),
            P(("col", "row"), None, None),
            P(("col", "row")),
            P("row", "col"),
            P("col", "row"),
            P("row"),
        ),
        out_specs=(P("row", "col"), P("col", "row"), P()),
        check_vma=False,
    )
```

```python
import functools

import jax
import jax.numpy as jnp
from jax import lax
from jax.experimental import pallas as pl
from jax.experimental.pallas import tpu as pltpu
from jax.sharding import PartitionSpec as P

NEG = -1e30
SCALE = 4.0
TILE = 16
GROUP = 32
LANES = 128


def params(megabytes):
    return pltpu.CompilerParams(vmem_limit_bytes=megabytes * 1024 * 1024)


def vmem():
    return pl.BlockSpec(memory_space=pltpu.VMEM)


def place():
    return pl.BlockSpec(memory_space=pl.ANY)


def smem():
    return pl.BlockSpec(memory_space=pltpu.SMEM)


def split(x, parts):
    out = []
    for _ in range(parts):
        piece = x.astype(jnp.bfloat16)
        out.append(piece)
        x = x - piece.astype(jnp.float32)
    return out


def mxu(a, b, dims=((1,), (0,))):
    return lax.dot_general(a, b, (dims, ((), ())), preferred_element_type=jnp.float32)


def prepare_kernel(
    slots, tokens_ref, lives_ref, sq_ref, sp_ref, pos_ref, sent_ref
):
    c = lax.axis_index("col")
    half = tokens_ref.shape[0] // 2
    width = tokens_ref.shape[2]
    slot = lax.broadcasted_iota(jnp.int32, (slots, width), 0)
    some = LANES // slots
    for j in range(half // some):
        values = []
        for q in range(some):
            at = (c % 2) * half + j * some + q
            value = tokens_ref[at].astype(jnp.float32)
            values.append(jnp.where(slot < lives_ref[at], value, 0.0))
        flipped = jnp.concatenate(values, axis=0).T
        sent_ref[j * width : (j + 1) * width, :] = flipped.astype(jnp.bfloat16)
    block, wide = sq_ref.shape
    base = half // some * width
    depth = sp_ref.shape[0]
    vectors = jnp.concatenate([sq_ref[...].astype(jnp.float32), jnp.zeros((block, LANES - wide), jnp.float32)], axis=1)
    line = lax.broadcasted_iota(jnp.int32, (block, LANES), 0)
    lane = lax.broadcasted_iota(jnp.int32, (block, LANES), 1)
    place = jnp.zeros((block, LANES), jnp.int32)
    for q in range(block):
        place = jnp.where(line == q, pos_ref[q], place)
    high, low = lax.shift_right_logical(place, 6), place & 63
    vectors = jnp.where(lane == wide, high.astype(jnp.float32), vectors)
    vectors = jnp.where(lane == wide + 1, low.astype(jnp.float32), vectors).astype(jnp.bfloat16)
    sent_ref[base : base + depth] = sp_ref[...]
    sent_ref[base + depth :] = vectors


def prepare(tokens, lives, sq, sp, pos):
    block, slots, width = tokens.shape
    base = block // 2 * slots // LANES * width
    return pl.pallas_call(
        functools.partial(prepare_kernel, slots),
        out_shape=jax.ShapeDtypeStruct((base + sp.shape[0] + block, LANES), jnp.bfloat16),
        in_specs=[vmem(), smem(), vmem(), vmem(), smem()],
        out_specs=vmem(),
        compiler_params=params(56),
    )(tokens, lives, sq, sp, pos)


def blocks_kernel(per, lengths_ref, after_ref, blocks_ref):
    passages = lengths_ref.shape[0]

    def entries(p, at):
        for b in range(per):
            live = jnp.minimum(lengths_ref[p] - b * TILE, TILE) - 1
            blocks_ref[at + b] = p * TILE * TILE + b * TILE + live
        return at + lax.shift_right_logical(lengths_ref[p] + TILE - 1, 4)

    count = lax.fori_loop(0, passages, entries, 0)
    final = blocks_ref[count - 1]
    for i in range(GROUP):
        blocks_ref[count + i] = final
    blocks_ref[blocks_ref.shape[0] - 1] = count


def live_blocks(lengths, per, after):
    return pl.pallas_call(
        functools.partial(blocks_kernel, per),
        out_shape=jax.ShapeDtypeStruct((lengths.shape[0] * per + TILE + GROUP + 1,), jnp.int32),
        in_specs=[smem(), place()],
        out_specs=smem(),
        compiler_params=params(56),
    )(lengths, after)


def teacher_kernel(slots, tasks, shifts, sides, priors, *refs):
    query_refs = dict(zip(shifts, refs))
    refs = refs[len(shifts) :]
    token_refs = dict(zip(sides, refs))
    list_refs = dict(zip(sides, refs[len(sides) :]))
    prior_refs = refs[2 * len(sides) : 2 * len(sides) + priors]
    out_ref, best = refs[-2:]
    passages, lanes = out_ref.shape
    width = token_refs[sides[0]].shape[2]
    r, c = lax.axis_index("row"), lax.axis_index("col")
    rows = lanes // 2 // lax.axis_size("row") * slots
    total = sum([ref[...] for ref in prior_refs], jnp.zeros((passages, lanes), jnp.float32))
    line = lax.broadcasted_iota(jnp.int32, (TILE, width), 0)
    for side, used in tasks:
        tokens_ref, blocks_ref = token_refs[side], list_refs[side]
        per = tokens_ref.shape[0] // passages
        count = blocks_ref[blocks_ref.shape[0] - 1]
        cells = [(query_refs[k], j) for k in used for j in range(rows // LANES)]

        def step(i, carry, tokens_ref=tokens_ref, blocks_ref=blocks_ref, per=per, cells=cells):
            carry = list(carry)
            owner, fresh, values = [], [], []
            for g in range(GROUP):
                entry = blocks_ref[i * GROUP + g]
                p, b = lax.shift_right_logical(entry, 8), lax.shift_right_logical(entry, 4) & (TILE - 1)
                owner.append(pl.multiple_of(p * 8, 8))
                fresh.append(b == 0)
                value = tokens_ref[p * per + b].astype(jnp.float32)
                value = jnp.where(line <= (entry & (TILE - 1)), value, value[0:1, :])
                values.append(value.astype(jnp.bfloat16))
            block = jnp.concatenate(values, axis=0)
            for n in range(0, len(cells), 2):
                pair = [ref[j * width : (j + 1) * width, :] for ref, j in cells[n : n + 2]]
                sims = mxu(block, jnp.concatenate(pair, axis=1))
                for g in range(GROUP):
                    for l in range(2):
                        top = sims[g * TILE : g * TILE + 8, l * LANES : (l + 1) * LANES]
                        low = sims[g * TILE + 8 : g * TILE + 16, l * LANES : (l + 1) * LANES]
                        kept = jnp.where(fresh[g], NEG, carry[n + l])
                        carry[n + l] = jnp.maximum(kept, jnp.maximum(top, low))
                        best[n + l, pl.ds(owner[g], 8), :] = carry[n + l]
            return tuple(carry)

        steps = lax.shift_right_logical(count + GROUP - 1, GROUP.bit_length() - 1)
        twice = lax.shift_right_logical(steps, 1)
        begin = tuple(jnp.full((8, LANES), NEG, jnp.float32) for _ in cells)
        begin = lax.fori_loop(0, twice, lambda i, x, step=step: step(2 * i + 1, step(2 * i, x)), begin)
        lax.fori_loop(2 * twice, steps, step, begin)
        found = []
        for l in range(len(cells)):
            peak = best[l, pl.ds(0, passages, stride=8), :]
            for s in range(1, 8):
                peak = jnp.maximum(peak, best[l, pl.ds(s, passages, stride=8), :])
            found.append(peak)
        parity = c % 2 if side == 0 else 1 - c % 2
        for n, k in enumerate(used):
            some = rows // LANES
            peaks = jnp.concatenate(found[n * some : (n + 1) * some], axis=1)
            start = parity * (lanes // 2) + (r ^ k) * (rows // slots)
            owner = lax.broadcasted_iota(jnp.int32, (rows, lanes), 0) // slots + start
            member = (owner == lax.broadcasted_iota(jnp.int32, (rows, lanes), 1)).astype(jnp.bfloat16)
            for piece in split(peaks, 3):
                total = total + mxu(piece, member)
    out_ref[...] = total


def teacher(slots, tasks, near, tokens, lists, queries, passages, priors=(), after=(), megabytes=16):
    shifts = sorted({k for _, used in tasks for k in used})
    sides = sorted({side for side, _ in tasks})
    operands = [near[k] for k in shifts] + [tokens[i] for i in sides] + [lists[i] for i in sides]
    specs = [vmem()] * (len(shifts) + len(sides)) + [smem()] * len(sides)
    operands += list(priors) + list(after)
    specs += [vmem()] * len(priors)
    specs += [place()] * len(after)
    most = max(len(used) for _, used in tasks)
    size = tokens[0].size
    rows = queries // 2 // lax.axis_size("row") * slots
    return pl.pallas_call(
        functools.partial(teacher_kernel, slots, tasks, shifts, sides, len(priors)),
        out_shape=jax.ShapeDtypeStruct((passages, queries), jnp.float32),
        in_specs=specs,
        out_specs=vmem(),
        scratch_shapes=[pltpu.VMEM((most * rows // LANES, passages * 8, LANES), jnp.float32)],
        compiler_params=params(megabytes),
        cost_estimate=pl.CostEstimate(
            flops=sum(4 * rows * len(used) * size for _, used in tasks),
            bytes_accessed=2 * size * len(sides),
            transcendentals=0,
        ),
    )(*operands)


def pack_kernel(axis, first, count, pieces, *refs):
    out_ref, token_ref = refs[-2:]
    me = lax.axis_index("row") if axis == "row" else lax.axis_index("col") // 2
    for k, ref in enumerate(refs[:pieces]):
        out_ref[me ^ k] = ref[first : first + count]
    token_ref[...] = jnp.zeros(token_ref.shape, jnp.float32)


def pack(axis, pieces, first, count, after):
    shape = (len(pieces), count) + pieces[0].shape[1:]
    return pl.pallas_call(
        functools.partial(pack_kernel, axis, first, count, len(pieces)),
        out_shape=(jax.ShapeDtypeStruct(shape, pieces[0].dtype), jax.ShapeDtypeStruct((8, LANES), jnp.float32)),
        in_specs=[vmem()] * len(pieces) + [place()] * len(after),
        out_specs=(vmem(), vmem()),
        compiler_params=params(24),
    )(*pieces, *after)


def loop(count, body, init):
    if count > 4:
        return lax.fori_loop(0, count, body, init)
    for i in range(count):
        init = body(i, init)
    return init


def student_kernel(
    wide, mine_ref, other_ref, after_ref, score_ref, slope_ref, vectors_ref, stats_ref, held, flat
):
    pairs, R, rows, span = mine_ref.shape
    C = 2 * pairs
    r, c = lax.axis_index("row"), lax.axis_index("col")
    queries = score_ref.shape[2]
    block = queries // R
    half = block // 2
    depth = rows - block
    per = depth // wide
    sides = ((mine_ref, c % 2), (other_ref, 1 - c % 2))
    for j in range(pairs):
        for ref, odd in sides:
            for i in range(R):
                for x in range(2):
                    held[2 * j + odd, x, i] = ref[j, i, depth + x * half : depth + (x + 1) * half]

    def columns(index):
        return held[index].reshape(queries, span).astype(jnp.float32)

    for i in range(R):
        pieces = [columns(i * per + h)[:, :wide] for h in range(per)]
        flat[i] = jnp.concatenate(pieces, axis=1).astype(jnp.bfloat16)
    vectors_ref[...] = flat[r]
    meta = columns(c)
    where = meta[:, wide : wide + 1] * 64.0 + meta[:, wide + 1 : wide + 2]
    diag = lax.broadcasted_iota(jnp.int32, (queries, queries), 0) == lax.broadcasted_iota(
        jnp.int32, (queries, queries), 1
    )
    spot = jnp.sum(jnp.where(diag, where, 0.0), axis=0, keepdims=True).astype(jnp.int32)
    index = lax.broadcasted_iota(jnp.int32, (span, queries), 0)

    def scores(j, carry):
        peak, score = carry
        for ref, odd in sides:
            total = jnp.zeros((queries, span), jnp.float32)
            for k in range(R):
                total = total + mxu(flat[k], ref[j, k, :depth])
            s = (SCALE * total).T
            i = 2 * j + odd
            score_ref[i] = s
            hot = index + i * span == spot
            peak, score = jnp.maximum(peak, s), score + jnp.where(hot, s, 0.0)
        return peak, score

    low = jnp.full((span, queries), -jnp.inf, jnp.float32)
    zero = jnp.zeros((span, queries), jnp.float32)
    peak, score = loop(pairs, scores, (low, zero))
    peak = jnp.max(peak, axis=0, keepdims=True)
    score = jnp.sum(score, axis=0, keepdims=True)

    def powers(j, total):
        for i in (2 * j, 2 * j + 1):
            power = jnp.exp(score_ref[i] - peak)
            slope_ref[i] = power
            total = total + power
        return total

    total = jnp.sum(loop(pairs, powers, zero), axis=0, keepdims=True)
    stats_ref[0:1, :] = peak + jnp.log(total)
    stats_ref[1:2, :] = score
    stats_ref[2:8, :] = jnp.zeros((6, queries), jnp.float32)
    factor = SCALE / queries
    scale = 2.0 * factor / total

    def slopes(j, carry):
        for i in (2 * j, 2 * j + 1):
            hot = index + i * span == spot
            slope_ref[i] = slope_ref[i] * scale - jnp.where(hot, factor, 0.0)
        return carry

    loop(pairs, slopes, 0)


def student_scores(mine, other, after, queries, wide):
    pairs, R, rows, span = mine.shape
    depth = rows - queries // R
    C = 2 * pairs
    return pl.pallas_call(
        functools.partial(student_kernel, wide),
        out_shape=(
            jax.ShapeDtypeStruct((C, span, queries), jnp.float32),
            jax.ShapeDtypeStruct((C, span, queries), jnp.float32),
            jax.ShapeDtypeStruct((queries, depth), jnp.bfloat16),
            jax.ShapeDtypeStruct((8, queries), jnp.float32),
        ),
        in_specs=[vmem(), vmem(), place()],
        out_specs=(vmem(),) * 4,
        scratch_shapes=[
            pltpu.VMEM((C, 2, R, queries // R // 2, span), jnp.bfloat16),
            pltpu.VMEM((R, queries, depth), jnp.bfloat16),
        ],
        compiler_params=params(40),
    )(mine, other, after)


def finish_kernel(
    wide,
    t_mine,
    t_other,
    s_ref,
    slope_ref,
    mine_ref,
    other_ref,
    vectors_ref,
    stats_ref,
    query_ref,
    passage_ref,
    loss_ref,
    teach,
):
    pairs, R, rows, span = mine_ref.shape
    r, c = lax.axis_index("row"), lax.axis_index("col")
    queries = vectors_ref.shape[0]
    depth = vectors_ref.shape[1]
    per = depth // wide
    block = queries // R
    half = queries // 2
    shape = (span, queries)
    odd = c % 2
    s_lse, score = stats_ref[0:1, :], stats_ref[1:2, :]

    def peak(j, t_max):
        a, b = t_mine[j].reshape(shape), t_other[j].reshape(shape)
        pair = [jnp.where(odd == 0, a, b), jnp.where(odd == 0, b, a)]
        for x in range(2):
            t = jnp.concatenate([v[:, x * half : (x + 1) * half] for v in pair], axis=1)
            teach[2 * j + x] = t
            t_max = jnp.maximum(t_max, t)
        return t_max

    t_max = loop(pairs, peak, jnp.full(shape, -jnp.inf, jnp.float32))
    t_max = jnp.max(t_max, axis=0, keepdims=True)

    def totals(j, carry):
        t_sum, cross = carry
        for i in (2 * j, 2 * j + 1):
            t = teach[i]
            t_exp = jnp.exp(t - t_max)
            teach[i] = t_exp
            t_sum, cross = t_sum + t_exp, cross + t_exp * (t - s_ref[i])
        return t_sum, cross

    zero = jnp.zeros(shape, jnp.float32)
    t_sum, cross = loop(pairs, totals, (zero, zero))
    t_sum = jnp.sum(t_sum, axis=0, keepdims=True)
    cross = jnp.sum(cross, axis=0, keepdims=True)
    each = cross / t_sum - (t_max + jnp.log(t_sum)) + 2.0 * s_lse - score
    loss_ref[...] = jnp.sum(each, axis=1, keepdims=True) / queries
    t_factor = SCALE / queries / t_sum

    def slope(i):
        return split(slope_ref[i] - teach[i] * t_factor, 2)

    def gradient(j, total):
        for ref, side in ((mine_ref, odd), (other_ref, 1 - odd)):
            vectors = ref[j, c // per, :depth]
            for piece in slope(2 * j + side):
                total = total + mxu(vectors, piece)
        return total

    flat = loop(pairs, gradient, jnp.zeros((depth, queries), jnp.float32)).T
    sub = block // 2
    for h in range(2):
        lines = functools.reduce(
            jnp.add,
            [jnp.where(r == i, flat[h * half + i * sub : h * half + (i + 1) * sub], 0.0) for i in range(R)],
        )
        query_ref[h * sub : (h + 1) * sub, :] = functools.reduce(
            jnp.add, [jnp.where(c % per == i, lines[:, i * wide : (i + 1) * wide], 0.0) for i in range(per)]
        )
    grads = sum(mxu(piece, vectors_ref[...]) for piece in slope(c))
    passage_ref[...] = grads.T


def finish(t_mine, t_other, s, slope, mine, other, vectors, stats, wide):
    pairs, R, rows, span = mine.shape
    queries, depth = vectors.shape
    return pl.pallas_call(
        functools.partial(finish_kernel, wide),
        out_shape=(
            jax.ShapeDtypeStruct((queries // R, wide), jnp.float32),
            jax.ShapeDtypeStruct((depth, span), jnp.float32),
            jax.ShapeDtypeStruct((1, 1), jnp.float32),
        ),
        in_specs=[vmem()] * 8,
        out_specs=(vmem(),) * 3,
        scratch_shapes=[pltpu.VMEM((2 * pairs, span, queries), jnp.float32)],
        compiler_params=params(48),
    )(t_mine, t_other, s, slope, mine, other, vectors, stats)


def shards(query_tokens, query_lengths, passage_tokens, passage_lengths, student_queries, student_passages, positives):
    R, C = lax.axis_size("row"), lax.axis_size("col")
    block, slots, width = query_tokens.shape
    queries = block * R
    local, count = passage_tokens.shape[:2]
    wide = student_queries.shape[1]

    def over_row(x, k):
        return lax.ppermute(x, "row", [(i, i ^ k) for i in range(R)])

    def over_col(x, k):
        return lax.ppermute(x, "col", [(i, i ^ k) for i in range(C)])

    cells = passage_tokens.reshape(local * count // TILE, TILE, width)
    tokens = [cells, over_col(cells, 1)]
    sent = prepare(query_tokens, query_lengths, student_queries, student_passages.T, positives)
    near = [sent] + [over_row(sent, k) for k in range(1, R)]
    blocks = live_blocks(passage_lengths, count // TILE, sent)
    lists = [blocks, over_col(blocks, 1)]
    common = dict(tokens=tokens, lists=lists, queries=queries, passages=local)
    begun = teacher(slots, ((0, (0,)),), near=near, megabytes=56, **common)
    near[1], begun = lax.optimization_barrier((near[1], begun))
    common["near"] = near
    score = teacher(slots, ((1, (0, 1)), (0, (1,))), **common)
    base = sent.shape[0] - student_passages.shape[1] - block
    vectors, token = pack("row", near, base, sent.shape[0] - base, (score,))
    parts = {0: vectors}
    for k in range(2, C, 2):
        if k & (k - 1) == 0:
            parts[k] = over_col(vectors, k)
    priors = (score, begun)
    for k in range(2, R, 2):
        score = teacher(slots, ((0, (k, k + 1)), (1, (k, k + 1))), priors=priors, after=(token,), **common)
        priors = (score,)
    parts, score = lax.optimization_barrier((parts, score))
    for k in range(2, C, 2):
        if k not in parts:
            parts[k] = over_col(parts[k & (k - 1)], k & -k)
    stack, token = pack("row", [score] + [over_row(score, k) for k in range(1, R)], 0, local, ())
    mine, _ = pack("col", [parts[k] for k in range(0, C, 2)], 0, R, (token,))
    other = over_col(mine, 1)
    t_mine, token = pack("col", [stack] + [over_col(stack, k) for k in range(2, C, 2)], 0, R, ())
    t_other = over_col(t_mine, 1)
    s, slope, vectors, stats = student_scores(mine, other, token, queries, wide)
    query_grads, passage_grads, loss = finish(t_mine, t_other, s, slope, mine, other, vectors, stats, wide)
    return (query_grads, passage_grads.T, loss[0, 0])


def solution(mesh):
    return jax.shard_map(
        shards,
        mesh=mesh,
        in_specs=(
            P("row", None, None),
            P("row"),
            P(("col", "row"), None, None),
            P(("col", "row")),
            P("row", "col"),
            P("col", "row"),
            P("row"),
        ),
        out_specs=(P("row", "col"), P("col", "row"), P()),
        check_vma=False,
    )
```

```python
import functools

import jax
import jax.numpy as jnp
from jax import lax
from jax.experimental import pallas as pl
from jax.experimental.pallas import tpu as pltpu
from jax.sharding import PartitionSpec as P

NEG = -1e30
SCALE = 4.0
TILE = 16
GROUP = 32
LANES = 128


def params(megabytes):
    return pltpu.CompilerParams(vmem_limit_bytes=megabytes * 1024 * 1024)


def vmem():
    return pl.BlockSpec(memory_space=pltpu.VMEM)


def place():
    return pl.BlockSpec(memory_space=pl.ANY)


def smem():
    return pl.BlockSpec(memory_space=pltpu.SMEM)


def split(x, parts):
    out = []
    for _ in range(parts):
        piece = x.astype(jnp.bfloat16)
        out.append(piece)
        x = x - piece.astype(jnp.float32)
    return out


def mxu(a, b, dims=((1,), (0,))):
    return lax.dot_general(a, b, (dims, ((), ())), preferred_element_type=jnp.float32)


def prepare_kernel(
    slots, tokens_ref, lives_ref, sq_ref, sp_ref, pos_ref, sent_ref
):
    c = lax.axis_index("col")
    half = tokens_ref.shape[0] // 2
    width = tokens_ref.shape[2]
    slot = lax.broadcasted_iota(jnp.int32, (slots, width), 0)
    some = LANES // slots
    for j in range(half // some):
        values = []
        for q in range(some):
            at = (c % 2) * half + j * some + q
            value = tokens_ref[at].astype(jnp.float32)
            values.append(jnp.where(slot < lives_ref[at], value, 0.0))
        flipped = jnp.concatenate(values, axis=0).T
        sent_ref[j * width : (j + 1) * width, :] = flipped.astype(jnp.bfloat16)
    block, wide = sq_ref.shape
    base = half // some * width
    depth = sp_ref.shape[0]
    vectors = jnp.concatenate([sq_ref[...].astype(jnp.float32), jnp.zeros((block, LANES - wide), jnp.float32)], axis=1)
    line = lax.broadcasted_iota(jnp.int32, (block, LANES), 0)
    lane = lax.broadcasted_iota(jnp.int32, (block, LANES), 1)
    place = jnp.zeros((block, LANES), jnp.int32)
    for q in range(block):
        place = jnp.where(line == q, pos_ref[q], place)
    high, low = lax.shift_right_logical(place, 6), place & 63
    vectors = jnp.where(lane == wide, high.astype(jnp.float32), vectors)
    vectors = jnp.where(lane == wide + 1, low.astype(jnp.float32), vectors).astype(jnp.bfloat16)
    sent_ref[base : base + depth] = sp_ref[...]
    sent_ref[base + depth :] = vectors


def prepare(tokens, lives, sq, sp, pos):
    block, slots, width = tokens.shape
    base = block // 2 * slots // LANES * width
    return pl.pallas_call(
        functools.partial(prepare_kernel, slots),
        out_shape=jax.ShapeDtypeStruct((base + sp.shape[0] + block, LANES), jnp.bfloat16),
        in_specs=[vmem(), smem(), vmem(), vmem(), smem()],
        out_specs=vmem(),
        compiler_params=params(56),
    )(tokens, lives, sq, sp, pos)


def blocks_kernel(per, lengths_ref, after_ref, blocks_ref):
    passages = lengths_ref.shape[0]

    def entries(p, at):
        length = lengths_ref[p]
        whole = p * TILE * TILE + TILE - 1
        for b in range(per):
            blocks_ref[at + b] = whole + b * TILE
        after = at + lax.shift_right_logical(length + TILE - 1, 4)
        blocks_ref[after - 1] = p * TILE * TILE + length - 1
        return after

    count = lax.fori_loop(0, passages, entries, 0)
    final = blocks_ref[count - 1]
    for i in range(GROUP):
        blocks_ref[count + i] = final
    blocks_ref[blocks_ref.shape[0] - 1] = count


def live_blocks(lengths, per, after):
    return pl.pallas_call(
        functools.partial(blocks_kernel, per),
        out_shape=jax.ShapeDtypeStruct((lengths.shape[0] * per + TILE + GROUP + 1,), jnp.int32),
        in_specs=[smem(), place()],
        out_specs=smem(),
        compiler_params=params(56),
    )(lengths, after)


def teacher_kernel(slots, tasks, shifts, sides, priors, *refs):
    query_refs = dict(zip(shifts, refs))
    refs = refs[len(shifts) :]
    token_refs = dict(zip(sides, refs))
    list_refs = dict(zip(sides, refs[len(sides) :]))
    prior_refs = refs[2 * len(sides) : 2 * len(sides) + priors]
    out_ref, best = refs[-2:]
    passages, lanes = out_ref.shape
    width = token_refs[sides[0]].shape[2]
    r, c = lax.axis_index("row"), lax.axis_index("col")
    rows = lanes // 2 // lax.axis_size("row") * slots
    total = sum([ref[...] for ref in prior_refs], jnp.zeros((passages, lanes), jnp.float32))
    line = lax.broadcasted_iota(jnp.int32, (TILE, width), 0)
    for side, used in tasks:
        tokens_ref, blocks_ref = token_refs[side], list_refs[side]
        per = tokens_ref.shape[0] // passages
        count = blocks_ref[blocks_ref.shape[0] - 1]
        cells = [(query_refs[k], j) for k in used for j in range(rows // LANES)]

        def step(i, carry, tokens_ref=tokens_ref, blocks_ref=blocks_ref, per=per, cells=cells):
            carry = list(carry)
            owner, fresh, values = [], [], []
            for g in range(GROUP):
                entry = blocks_ref[i * GROUP + g]
                p, b = lax.shift_right_logical(entry, 8), lax.shift_right_logical(entry, 4) & (TILE - 1)
                owner.append(pl.multiple_of(p * 8, 8))
                fresh.append(b == 0)
                value = tokens_ref[p * per + b].astype(jnp.float32)
                value = jnp.where(line <= (entry & (TILE - 1)), value, value[0:1, :])
                values.append(value.astype(jnp.bfloat16))
            block = jnp.concatenate(values, axis=0)
            for n in range(0, len(cells), 2):
                pair = [ref[j * width : (j + 1) * width, :] for ref, j in cells[n : n + 2]]
                sims = mxu(block, jnp.concatenate(pair, axis=1))
                for g in range(GROUP):
                    for l in range(2):
                        top = sims[g * TILE : g * TILE + 8, l * LANES : (l + 1) * LANES]
                        low = sims[g * TILE + 8 : g * TILE + 16, l * LANES : (l + 1) * LANES]
                        kept = jnp.where(fresh[g], NEG, carry[n + l])
                        carry[n + l] = jnp.maximum(kept, jnp.maximum(top, low))
                        best[n + l, pl.ds(owner[g], 8), :] = carry[n + l]
            return tuple(carry)

        steps = lax.shift_right_logical(count + GROUP - 1, GROUP.bit_length() - 1)
        twice = lax.shift_right_logical(steps, 1)
        begin = tuple(jnp.full((8, LANES), NEG, jnp.float32) for _ in cells)
        begin = lax.fori_loop(0, twice, lambda i, x, step=step: step(2 * i + 1, step(2 * i, x)), begin)
        lax.fori_loop(2 * twice, steps, step, begin)
        found = []
        for l in range(len(cells)):
            peak = best[l, pl.ds(0, passages, stride=8), :]
            for s in range(1, 8):
                peak = jnp.maximum(peak, best[l, pl.ds(s, passages, stride=8), :])
            found.append(peak)
        parity = c % 2 if side == 0 else 1 - c % 2
        for n, k in enumerate(used):
            some = rows // LANES
            peaks = jnp.concatenate(found[n * some : (n + 1) * some], axis=1)
            start = parity * (lanes // 2) + (r ^ k) * (rows // slots)
            owner = lax.broadcasted_iota(jnp.int32, (rows, lanes), 0) // slots + start
            member = (owner == lax.broadcasted_iota(jnp.int32, (rows, lanes), 1)).astype(jnp.bfloat16)
            for piece in split(peaks, 3):
                total = total + mxu(piece, member)
    out_ref[...] = total


def teacher(slots, tasks, near, tokens, lists, queries, passages, priors=(), after=(), megabytes=16):
    shifts = sorted({k for _, used in tasks for k in used})
    sides = sorted({side for side, _ in tasks})
    operands = [near[k] for k in shifts] + [tokens[i] for i in sides] + [lists[i] for i in sides]
    specs = [vmem()] * (len(shifts) + len(sides)) + [smem()] * len(sides)
    operands += list(priors) + list(after)
    specs += [vmem()] * len(priors)
    specs += [place()] * len(after)
    most = max(len(used) for _, used in tasks)
    size = tokens[0].size
    rows = queries // 2 // lax.axis_size("row") * slots
    return pl.pallas_call(
        functools.partial(teacher_kernel, slots, tasks, shifts, sides, len(priors)),
        out_shape=jax.ShapeDtypeStruct((passages, queries), jnp.float32),
        in_specs=specs,
        out_specs=vmem(),
        scratch_shapes=[pltpu.VMEM((most * rows // LANES, passages * 8, LANES), jnp.float32)],
        compiler_params=params(megabytes),
        cost_estimate=pl.CostEstimate(
            flops=sum(4 * rows * len(used) * size for _, used in tasks),
            bytes_accessed=2 * size * len(sides),
            transcendentals=0,
        ),
    )(*operands)


def pack_kernel(axis, first, count, pieces, *refs):
    out_ref, token_ref = refs[-2:]
    me = lax.axis_index("row") if axis == "row" else lax.axis_index("col") // 2
    for k, ref in enumerate(refs[:pieces]):
        out_ref[me ^ k] = ref[first : first + count]
    token_ref[...] = jnp.zeros(token_ref.shape, jnp.float32)


def pack(axis, pieces, first, count, after):
    shape = (len(pieces), count) + pieces[0].shape[1:]
    return pl.pallas_call(
        functools.partial(pack_kernel, axis, first, count, len(pieces)),
        out_shape=(jax.ShapeDtypeStruct(shape, pieces[0].dtype), jax.ShapeDtypeStruct((8, LANES), jnp.float32)),
        in_specs=[vmem()] * len(pieces) + [place()] * len(after),
        out_specs=(vmem(), vmem()),
        compiler_params=params(24),
    )(*pieces, *after)


def loop(count, body, init):
    if count > 4:
        return lax.fori_loop(0, count, body, init)
    for i in range(count):
        init = body(i, init)
    return init


def student_kernel(
    wide, mine_ref, other_ref, after_ref, score_ref, slope_ref, vectors_ref, stats_ref, held, flat
):
    pairs, R, rows, span = mine_ref.shape
    C = 2 * pairs
    r, c = lax.axis_index("row"), lax.axis_index("col")
    queries = score_ref.shape[2]
    block = queries // R
    half = block // 2
    depth = rows - block
    per = depth // wide
    sides = ((mine_ref, c % 2), (other_ref, 1 - c % 2))
    for j in range(pairs):
        for ref, odd in sides:
            for i in range(R):
                for x in range(2):
                    held[2 * j + odd, x, i] = ref[j, i, depth + x * half : depth + (x + 1) * half]

    def columns(index):
        return held[index].reshape(queries, span).astype(jnp.float32)

    for i in range(R):
        pieces = [columns(i * per + h)[:, :wide] for h in range(per)]
        flat[i] = jnp.concatenate(pieces, axis=1).astype(jnp.bfloat16)
    vectors_ref[...] = flat[r]
    meta = columns(c)
    where = meta[:, wide : wide + 1] * 64.0 + meta[:, wide + 1 : wide + 2]
    diag = lax.broadcasted_iota(jnp.int32, (queries, queries), 0) == lax.broadcasted_iota(
        jnp.int32, (queries, queries), 1
    )
    spot = jnp.sum(jnp.where(diag, where, 0.0), axis=0, keepdims=True).astype(jnp.int32)
    index = lax.broadcasted_iota(jnp.int32, (span, queries), 0)

    def scores(j, carry):
        peak, score = carry
        for ref, odd in sides:
            total = jnp.zeros((queries, span), jnp.float32)
            for k in range(R):
                total = total + mxu(flat[k], ref[j, k, :depth])
            s = (SCALE * total).T
            i = 2 * j + odd
            score_ref[i] = s
            hot = index + i * span == spot
            peak, score = jnp.maximum(peak, s), score + jnp.where(hot, s, 0.0)
        return peak, score

    low = jnp.full((span, queries), -jnp.inf, jnp.float32)
    zero = jnp.zeros((span, queries), jnp.float32)
    peak, score = loop(pairs, scores, (low, zero))
    peak = jnp.max(peak, axis=0, keepdims=True)
    score = jnp.sum(score, axis=0, keepdims=True)

    def powers(j, total):
        for i in (2 * j, 2 * j + 1):
            power = jnp.exp(score_ref[i] - peak)
            slope_ref[i] = power
            total = total + power
        return total

    total = jnp.sum(loop(pairs, powers, zero), axis=0, keepdims=True)
    stats_ref[0:1, :] = peak + jnp.log(total)
    stats_ref[1:2, :] = score
    stats_ref[2:8, :] = jnp.zeros((6, queries), jnp.float32)
    factor = SCALE / queries
    scale = 2.0 * factor / total

    def slopes(j, carry):
        for i in (2 * j, 2 * j + 1):
            hot = index + i * span == spot
            slope_ref[i] = slope_ref[i] * scale - jnp.where(hot, factor, 0.0)
        return carry

    loop(pairs, slopes, 0)


def student_scores(mine, other, after, queries, wide):
    pairs, R, rows, span = mine.shape
    depth = rows - queries // R
    C = 2 * pairs
    return pl.pallas_call(
        functools.partial(student_kernel, wide),
        out_shape=(
            jax.ShapeDtypeStruct((C, span, queries), jnp.float32),
            jax.ShapeDtypeStruct((C, span, queries), jnp.float32),
            jax.ShapeDtypeStruct((queries, depth), jnp.bfloat16),
            jax.ShapeDtypeStruct((8, queries), jnp.float32),
        ),
        in_specs=[vmem(), vmem(), place()],
        out_specs=(vmem(),) * 4,
        scratch_shapes=[
            pltpu.VMEM((C, 2, R, queries // R // 2, span), jnp.bfloat16),
            pltpu.VMEM((R, queries, depth), jnp.bfloat16),
        ],
        compiler_params=params(40),
    )(mine, other, after)


def finish_kernel(
    wide,
    t_mine,
    t_other,
    s_ref,
    slope_ref,
    mine_ref,
    other_ref,
    vectors_ref,
    stats_ref,
    query_ref,
    passage_ref,
    loss_ref,
    teach,
):
    pairs, R, rows, span = mine_ref.shape
    r, c = lax.axis_index("row"), lax.axis_index("col")
    queries = vectors_ref.shape[0]
    depth = vectors_ref.shape[1]
    per = depth // wide
    block = queries // R
    half = queries // 2
    shape = (span, queries)
    odd = c % 2
    s_lse, score = stats_ref[0:1, :], stats_ref[1:2, :]

    def peak(j, t_max):
        a, b = t_mine[j].reshape(shape), t_other[j].reshape(shape)
        pair = [jnp.where(odd == 0, a, b), jnp.where(odd == 0, b, a)]
        for x in range(2):
            t = jnp.concatenate([v[:, x * half : (x + 1) * half] for v in pair], axis=1)
            teach[2 * j + x] = t
            t_max = jnp.maximum(t_max, t)
        return t_max

    t_max = loop(pairs, peak, jnp.full(shape, -jnp.inf, jnp.float32))
    t_max = jnp.max(t_max, axis=0, keepdims=True)

    def totals(j, carry):
        t_sum, cross = carry
        for i in (2 * j, 2 * j + 1):
            t = teach[i]
            t_exp = jnp.exp(t - t_max)
            teach[i] = t_exp
            t_sum, cross = t_sum + t_exp, cross + t_exp * (t - s_ref[i])
        return t_sum, cross

    zero = jnp.zeros(shape, jnp.float32)
    t_sum, cross = loop(pairs, totals, (zero, zero))
    t_sum = jnp.sum(t_sum, axis=0, keepdims=True)
    cross = jnp.sum(cross, axis=0, keepdims=True)
    each = cross / t_sum - (t_max + jnp.log(t_sum)) + 2.0 * s_lse - score
    loss_ref[...] = jnp.sum(each, axis=1, keepdims=True) / queries
    t_factor = SCALE / queries / t_sum

    def slope(i):
        return split(slope_ref[i] - teach[i] * t_factor, 2)

    def gradient(j, total):
        for ref, side in ((mine_ref, odd), (other_ref, 1 - odd)):
            vectors = ref[j, c // per, :depth]
            for piece in slope(2 * j + side):
                total = total + mxu(vectors, piece)
        return total

    flat = loop(pairs, gradient, jnp.zeros((depth, queries), jnp.float32)).T
    sub = block // 2
    for h in range(2):
        lines = functools.reduce(
            jnp.add,
            [jnp.where(r == i, flat[h * half + i * sub : h * half + (i + 1) * sub], 0.0) for i in range(R)],
        )
        query_ref[h * sub : (h + 1) * sub, :] = functools.reduce(
            jnp.add, [jnp.where(c % per == i, lines[:, i * wide : (i + 1) * wide], 0.0) for i in range(per)]
        )
    grads = sum(mxu(piece, vectors_ref[...]) for piece in slope(c))
    passage_ref[...] = grads.T


def finish(t_mine, t_other, s, slope, mine, other, vectors, stats, wide):
    pairs, R, rows, span = mine.shape
    queries, depth = vectors.shape
    return pl.pallas_call(
        functools.partial(finish_kernel, wide),
        out_shape=(
            jax.ShapeDtypeStruct((queries // R, wide), jnp.float32),
            jax.ShapeDtypeStruct((depth, span), jnp.float32),
            jax.ShapeDtypeStruct((1, 1), jnp.float32),
        ),
        in_specs=[vmem()] * 8,
        out_specs=(vmem(),) * 3,
        scratch_shapes=[pltpu.VMEM((2 * pairs, span, queries), jnp.float32)],
        compiler_params=params(48),
    )(t_mine, t_other, s, slope, mine, other, vectors, stats)


def shards(query_tokens, query_lengths, passage_tokens, passage_lengths, student_queries, student_passages, positives):
    R, C = lax.axis_size("row"), lax.axis_size("col")
    block, slots, width = query_tokens.shape
    queries = block * R
    local, count = passage_tokens.shape[:2]
    wide = student_queries.shape[1]

    def over_row(x, k):
        return lax.ppermute(x, "row", [(i, i ^ k) for i in range(R)])

    def over_col(x, k):
        return lax.ppermute(x, "col", [(i, i ^ k) for i in range(C)])

    cells = passage_tokens.reshape(local * count // TILE, TILE, width)
    tokens = [cells, over_col(cells, 1)]
    sent = prepare(query_tokens, query_lengths, student_queries, student_passages.T, positives)
    near = [sent]
    for k in range(1, R):
        near.append(over_row(near[k & (k - 1)], k & -k))
    blocks = live_blocks(passage_lengths, count // TILE, sent)
    lists = [blocks, over_col(blocks, 1)]
    common = dict(tokens=tokens, lists=lists, queries=queries, passages=local)
    begun = teacher(slots, ((0, (0,)),), near=near, megabytes=56, **common)
    near[1], begun = lax.optimization_barrier((near[1], begun))
    common["near"] = near
    score = teacher(slots, ((1, (0, 1)), (0, (1,))), **common)
    base = sent.shape[0] - student_passages.shape[1] - block
    vectors, token = pack("row", near, base, sent.shape[0] - base, (score,))
    parts = {0: vectors}
    for k in range(2, C, 2):
        if k & (k - 1) == 0:
            parts[k] = over_col(vectors, k)
    priors = (score, begun)
    for k in range(2, R, 2):
        score = teacher(slots, ((0, (k, k + 1)), (1, (k, k + 1))), priors=priors, after=(token,), **common)
        priors = (score,)
    parts, score = lax.optimization_barrier((parts, score))
    for k in range(2, C, 2):
        if k not in parts:
            parts[k] = over_col(parts[k & (k - 1)], k & -k)
    stack, token = pack("row", [score] + [over_row(score, k) for k in range(1, R)], 0, local, ())
    mine, _ = pack("col", [parts[k] for k in range(0, C, 2)], 0, R, (token,))
    other = over_col(mine, 1)
    t_mine, token = pack("col", [stack] + [over_col(stack, k) for k in range(2, C, 2)], 0, R, ())
    t_other = over_col(t_mine, 1)
    s, slope, vectors, stats = student_scores(mine, other, token, queries, wide)
    query_grads, passage_grads, loss = finish(t_mine, t_other, s, slope, mine, other, vectors, stats, wide)
    return (query_grads, passage_grads.T, loss[0, 0])


def solution(mesh):
    return jax.shard_map(
        shards,
        mesh=mesh,
        in_specs=(
            P("row", None, None),
            P("row"),
            P(("col", "row"), None, None),
            P(("col", "row")),
            P("row", "col"),
            P("col", "row"),
            P("row"),
        ),
        out_specs=(P("row", "col"), P("col", "row"), P()),
        check_vma=False,
    )
```

```python
import functools

import jax
import jax.numpy as jnp
from jax import lax
from jax.experimental import pallas as pl
from jax.experimental.pallas import tpu as pltpu
from jax.sharding import PartitionSpec as P

NEG = -1e30
SCALE = 4.0
TILE = 16
GROUP = 32
LANES = 128


def params(megabytes):
    return pltpu.CompilerParams(vmem_limit_bytes=megabytes * 1024 * 1024)


def vmem():
    return pl.BlockSpec(memory_space=pltpu.VMEM)


def place():
    return pl.BlockSpec(memory_space=pl.ANY)


def smem():
    return pl.BlockSpec(memory_space=pltpu.SMEM)


def split(x, parts):
    out = []
    for _ in range(parts):
        piece = x.astype(jnp.bfloat16)
        out.append(piece)
        x = x - piece.astype(jnp.float32)
    return out


def mxu(a, b, dims=((1,), (0,))):
    return lax.dot_general(a, b, (dims, ((), ())), preferred_element_type=jnp.float32)


def prepare_kernel(
    slots, tokens_ref, lives_ref, sq_ref, sp_ref, pos_ref, sent_ref
):
    c = lax.axis_index("col")
    half = tokens_ref.shape[0] // 2
    width = tokens_ref.shape[2]
    slot = lax.broadcasted_iota(jnp.int32, (slots, width), 0)
    some = LANES // slots
    for j in range(half // some):
        values = []
        for q in range(some):
            at = (c % 2) * half + j * some + q
            value = tokens_ref[at].astype(jnp.float32)
            values.append(jnp.where(slot < lives_ref[at], value, 0.0))
        flipped = jnp.concatenate(values, axis=0).T
        sent_ref[j * width : (j + 1) * width, :] = flipped.astype(jnp.bfloat16)
    block, wide = sq_ref.shape
    base = half // some * width
    depth = sp_ref.shape[0]
    vectors = jnp.concatenate([sq_ref[...].astype(jnp.float32), jnp.zeros((block, LANES - wide), jnp.float32)], axis=1)
    line = lax.broadcasted_iota(jnp.int32, (block, LANES), 0)
    lane = lax.broadcasted_iota(jnp.int32, (block, LANES), 1)
    place = jnp.zeros((block, LANES), jnp.int32)
    for q in range(block):
        place = jnp.where(line == q, pos_ref[q], place)
    high, low = lax.shift_right_logical(place, 6), place & 63
    vectors = jnp.where(lane == wide, high.astype(jnp.float32), vectors)
    vectors = jnp.where(lane == wide + 1, low.astype(jnp.float32), vectors).astype(jnp.bfloat16)
    sent_ref[base : base + depth] = sp_ref[...]
    sent_ref[base + depth :] = vectors


def prepare(tokens, lives, sq, sp, pos):
    block, slots, width = tokens.shape
    base = block // 2 * slots // LANES * width
    return pl.pallas_call(
        functools.partial(prepare_kernel, slots),
        out_shape=jax.ShapeDtypeStruct((base + sp.shape[0] + block, LANES), jnp.bfloat16),
        in_specs=[vmem(), smem(), vmem(), vmem(), smem()],
        out_specs=vmem(),
        compiler_params=params(56),
    )(tokens, lives, sq, sp, pos)


def blocks_kernel(per, lengths_ref, after_ref, blocks_ref):
    passages = lengths_ref.shape[0]

    def entries(p, at):
        length = lengths_ref[p]
        whole = p * TILE * TILE + TILE - 1
        for b in range(per):
            blocks_ref[at + b] = whole + b * TILE
        after = at + lax.shift_right_logical(length + TILE - 1, 4)
        blocks_ref[after - 1] = p * TILE * TILE + length - 1
        return after

    count = lax.fori_loop(0, passages, entries, 0)
    final = blocks_ref[count - 1]
    for i in range(GROUP):
        blocks_ref[count + i] = final
    blocks_ref[blocks_ref.shape[0] - 1] = count


def live_blocks(lengths, per, after):
    return pl.pallas_call(
        functools.partial(blocks_kernel, per),
        out_shape=jax.ShapeDtypeStruct((lengths.shape[0] * per + TILE + GROUP + 1,), jnp.int32),
        in_specs=[smem(), place()],
        out_specs=smem(),
        compiler_params=params(56),
    )(lengths, after)


def teacher_kernel(slots, tasks, shifts, sides, priors, *refs):
    query_refs = dict(zip(shifts, refs))
    refs = refs[len(shifts) :]
    token_refs = dict(zip(sides, refs))
    list_refs = dict(zip(sides, refs[len(sides) :]))
    prior_refs = refs[2 * len(sides) : 2 * len(sides) + priors]
    out_ref, best = refs[-2:]
    passages, lanes = out_ref.shape
    width = token_refs[sides[0]].shape[2]
    r, c = lax.axis_index("row"), lax.axis_index("col")
    rows = lanes // 2 // lax.axis_size("row") * slots
    total = sum([ref[...] for ref in prior_refs], jnp.zeros((passages, lanes), jnp.float32))
    line = lax.broadcasted_iota(jnp.int32, (TILE, width), 0)
    for side, used in tasks:
        tokens_ref, blocks_ref = token_refs[side], list_refs[side]
        per = tokens_ref.shape[0] // passages
        count = blocks_ref[blocks_ref.shape[0] - 1]
        cells = [(query_refs[k], j) for k in used for j in range(rows // LANES)]

        def step(i, carry, tokens_ref=tokens_ref, blocks_ref=blocks_ref, per=per, cells=cells):
            carry = list(carry)
            owner, fresh, values = [], [], []
            for g in range(GROUP):
                entry = blocks_ref[i * GROUP + g]
                p, b = lax.shift_right_logical(entry, 8), lax.shift_right_logical(entry, 4) & (TILE - 1)
                owner.append(pl.multiple_of(p * 8, 8))
                fresh.append(b == 0)
                value = tokens_ref[p * per + b].astype(jnp.float32)
                value = jnp.where(line <= (entry & (TILE - 1)), value, value[0:1, :])
                values.append(value.astype(jnp.bfloat16))
            block = jnp.concatenate(values, axis=0)
            for n in range(0, len(cells), 2):
                pair = [ref[j * width : (j + 1) * width, :] for ref, j in cells[n : n + 2]]
                sims = mxu(block, jnp.concatenate(pair, axis=1))
                for g in range(GROUP):
                    for l in range(2):
                        top = sims[g * TILE : g * TILE + 8, l * LANES : (l + 1) * LANES]
                        low = sims[g * TILE + 8 : g * TILE + 16, l * LANES : (l + 1) * LANES]
                        kept = jnp.where(fresh[g], NEG, carry[n + l])
                        carry[n + l] = jnp.maximum(kept, jnp.maximum(top, low))
                        best[n + l, pl.ds(owner[g], 8), :] = carry[n + l]
            return tuple(carry)

        steps = lax.shift_right_logical(count + GROUP - 1, GROUP.bit_length() - 1)
        twice = lax.shift_right_logical(steps, 1)
        begin = tuple(jnp.full((8, LANES), NEG, jnp.float32) for _ in cells)
        begin = lax.fori_loop(0, twice, lambda i, x, step=step: step(2 * i + 1, step(2 * i, x)), begin)
        lax.fori_loop(2 * twice, steps, step, begin)
        found = []
        for l in range(len(cells)):
            peak = best[l, pl.ds(0, passages, stride=8), :]
            for s in range(1, 8):
                peak = jnp.maximum(peak, best[l, pl.ds(s, passages, stride=8), :])
            found.append(peak)
        parity = c % 2 if side == 0 else 1 - c % 2
        for n, k in enumerate(used):
            some = rows // LANES
            peaks = jnp.concatenate(found[n * some : (n + 1) * some], axis=1)
            start = parity * (lanes // 2) + (r ^ k) * (rows // slots)
            owner = lax.broadcasted_iota(jnp.int32, (rows, lanes), 0) // slots + start
            member = (owner == lax.broadcasted_iota(jnp.int32, (rows, lanes), 1)).astype(jnp.bfloat16)
            for piece in split(peaks, 3):
                total = total + mxu(piece, member)
    out_ref[...] = total


def teacher(slots, tasks, near, tokens, lists, queries, passages, priors=(), after=(), megabytes=16):
    shifts = sorted({k for _, used in tasks for k in used})
    sides = sorted({side for side, _ in tasks})
    operands = [near[k] for k in shifts] + [tokens[i] for i in sides] + [lists[i] for i in sides]
    specs = [vmem()] * (len(shifts) + len(sides)) + [smem()] * len(sides)
    operands += list(priors) + list(after)
    specs += [vmem()] * len(priors)
    specs += [place()] * len(after)
    most = max(len(used) for _, used in tasks)
    size = tokens[0].size
    rows = queries // 2 // lax.axis_size("row") * slots
    return pl.pallas_call(
        functools.partial(teacher_kernel, slots, tasks, shifts, sides, len(priors)),
        out_shape=jax.ShapeDtypeStruct((passages, queries), jnp.float32),
        in_specs=specs,
        out_specs=vmem(),
        scratch_shapes=[pltpu.VMEM((most * rows // LANES, passages * 8, LANES), jnp.float32)],
        compiler_params=params(megabytes),
        cost_estimate=pl.CostEstimate(
            flops=sum(4 * rows * len(used) * size for _, used in tasks),
            bytes_accessed=2 * size * len(sides),
            transcendentals=0,
        ),
    )(*operands)


def pack_kernel(axis, first, count, pieces, *refs):
    out_ref, token_ref = refs[-2:]
    me = lax.axis_index("row") if axis == "row" else lax.axis_index("col") // 2
    for k, ref in enumerate(refs[:pieces]):
        out_ref[me ^ k] = ref[first : first + count]
    token_ref[...] = jnp.zeros(token_ref.shape, jnp.float32)


def pack(axis, pieces, first, count, after):
    shape = (len(pieces), count) + pieces[0].shape[1:]
    return pl.pallas_call(
        functools.partial(pack_kernel, axis, first, count, len(pieces)),
        out_shape=(jax.ShapeDtypeStruct(shape, pieces[0].dtype), jax.ShapeDtypeStruct((8, LANES), jnp.float32)),
        in_specs=[vmem()] * len(pieces) + [place()] * len(after),
        out_specs=(vmem(), vmem()),
        compiler_params=params(24),
    )(*pieces, *after)


def join_kernel(placed, first_ref, second_ref, out_ref, token_ref):
    me = lax.axis_index("row") if placed else 0
    count = first_ref.shape[0]
    for i in range(count):
        out_ref[me ^ i] = first_ref[i]
        out_ref[me ^ (count + i)] = second_ref[i]
    token_ref[...] = jnp.zeros(token_ref.shape, jnp.float32)


def join(first, second, placed):
    shape = (2 * first.shape[0],) + first.shape[1:]
    return pl.pallas_call(
        functools.partial(join_kernel, placed),
        out_shape=(jax.ShapeDtypeStruct(shape, first.dtype), jax.ShapeDtypeStruct((8, LANES), jnp.float32)),
        in_specs=[vmem()] * 2,
        out_specs=(vmem(), vmem()),
        compiler_params=params(24),
    )(first, second)


def loop(count, body, init):
    if count > 4:
        return lax.fori_loop(0, count, body, init)
    for i in range(count):
        init = body(i, init)
    return init


def student_kernel(
    wide, mine_ref, other_ref, after_ref, score_ref, slope_ref, vectors_ref, stats_ref, held, flat
):
    pairs, R, rows, span = mine_ref.shape
    C = 2 * pairs
    r, c = lax.axis_index("row"), lax.axis_index("col")
    queries = score_ref.shape[2]
    block = queries // R
    half = block // 2
    depth = rows - block
    per = depth // wide
    sides = ((mine_ref, c % 2), (other_ref, 1 - c % 2))
    for j in range(pairs):
        for ref, odd in sides:
            for i in range(R):
                for x in range(2):
                    held[2 * j + odd, x, i] = ref[j, i, depth + x * half : depth + (x + 1) * half]

    def columns(index):
        return held[index].reshape(queries, span).astype(jnp.float32)

    for i in range(R):
        pieces = [columns(i * per + h)[:, :wide] for h in range(per)]
        flat[i] = jnp.concatenate(pieces, axis=1).astype(jnp.bfloat16)
    vectors_ref[...] = flat[r]
    meta = columns(c)
    where = meta[:, wide : wide + 1] * 64.0 + meta[:, wide + 1 : wide + 2]
    diag = lax.broadcasted_iota(jnp.int32, (queries, queries), 0) == lax.broadcasted_iota(
        jnp.int32, (queries, queries), 1
    )
    spot = jnp.sum(jnp.where(diag, where, 0.0), axis=0, keepdims=True).astype(jnp.int32)
    index = lax.broadcasted_iota(jnp.int32, (span, queries), 0)

    def scores(j, carry):
        peak, score = carry
        for ref, odd in sides:
            total = jnp.zeros((queries, span), jnp.float32)
            for k in range(R):
                total = total + mxu(flat[k], ref[j, k, :depth])
            s = (SCALE * total).T
            i = 2 * j + odd
            score_ref[i] = s
            hot = index + i * span == spot
            peak, score = jnp.maximum(peak, s), score + jnp.where(hot, s, 0.0)
        return peak, score

    low = jnp.full((span, queries), -jnp.inf, jnp.float32)
    zero = jnp.zeros((span, queries), jnp.float32)
    peak, score = loop(pairs, scores, (low, zero))
    peak = jnp.max(peak, axis=0, keepdims=True)
    score = jnp.sum(score, axis=0, keepdims=True)

    def powers(j, total):
        for i in (2 * j, 2 * j + 1):
            power = jnp.exp(score_ref[i] - peak)
            slope_ref[i] = power
            total = total + power
        return total

    total = jnp.sum(loop(pairs, powers, zero), axis=0, keepdims=True)
    stats_ref[0:1, :] = peak + jnp.log(total)
    stats_ref[1:2, :] = score
    stats_ref[2:8, :] = jnp.zeros((6, queries), jnp.float32)
    factor = SCALE / queries
    scale = 2.0 * factor / total

    def slopes(j, carry):
        for i in (2 * j, 2 * j + 1):
            hot = index + i * span == spot
            slope_ref[i] = slope_ref[i] * scale - jnp.where(hot, factor, 0.0)
        return carry

    loop(pairs, slopes, 0)


def student_scores(mine, other, after, queries, wide):
    pairs, R, rows, span = mine.shape
    depth = rows - queries // R
    C = 2 * pairs
    return pl.pallas_call(
        functools.partial(student_kernel, wide),
        out_shape=(
            jax.ShapeDtypeStruct((C, span, queries), jnp.float32),
            jax.ShapeDtypeStruct((C, span, queries), jnp.float32),
            jax.ShapeDtypeStruct((queries, depth), jnp.bfloat16),
            jax.ShapeDtypeStruct((8, queries), jnp.float32),
        ),
        in_specs=[vmem(), vmem(), place()],
        out_specs=(vmem(),) * 4,
        scratch_shapes=[
            pltpu.VMEM((C, 2, R, queries // R // 2, span), jnp.bfloat16),
            pltpu.VMEM((R, queries, depth), jnp.bfloat16),
        ],
        compiler_params=params(40),
    )(mine, other, after)


def finish_kernel(
    wide,
    t_mine,
    t_other,
    s_ref,
    slope_ref,
    mine_ref,
    other_ref,
    vectors_ref,
    stats_ref,
    query_ref,
    passage_ref,
    loss_ref,
    teach,
):
    pairs, R, rows, span = mine_ref.shape
    r, c = lax.axis_index("row"), lax.axis_index("col")
    queries = vectors_ref.shape[0]
    depth = vectors_ref.shape[1]
    per = depth // wide
    block = queries // R
    half = queries // 2
    shape = (span, queries)
    odd = c % 2
    s_lse, score = stats_ref[0:1, :], stats_ref[1:2, :]

    def peak(j, t_max):
        a, b = t_mine[j].reshape(shape), t_other[j].reshape(shape)
        pair = [jnp.where(odd == 0, a, b), jnp.where(odd == 0, b, a)]
        for x in range(2):
            t = jnp.concatenate([v[:, x * half : (x + 1) * half] for v in pair], axis=1)
            teach[2 * j + x] = t
            t_max = jnp.maximum(t_max, t)
        return t_max

    t_max = loop(pairs, peak, jnp.full(shape, -jnp.inf, jnp.float32))
    t_max = jnp.max(t_max, axis=0, keepdims=True)

    def totals(j, carry):
        t_sum, cross = carry
        for i in (2 * j, 2 * j + 1):
            t = teach[i]
            t_exp = jnp.exp(t - t_max)
            teach[i] = t_exp
            t_sum, cross = t_sum + t_exp, cross + t_exp * (t - s_ref[i])
        return t_sum, cross

    zero = jnp.zeros(shape, jnp.float32)
    t_sum, cross = loop(pairs, totals, (zero, zero))
    t_sum = jnp.sum(t_sum, axis=0, keepdims=True)
    cross = jnp.sum(cross, axis=0, keepdims=True)
    each = cross / t_sum - (t_max + jnp.log(t_sum)) + 2.0 * s_lse - score
    loss_ref[...] = jnp.sum(each, axis=1, keepdims=True) / queries
    t_factor = SCALE / queries / t_sum

    def slope(i):
        return split(slope_ref[i] - teach[i] * t_factor, 2)

    def gradient(j, total):
        for ref, side in ((mine_ref, odd), (other_ref, 1 - odd)):
            vectors = ref[j, c // per, :depth]
            for piece in slope(2 * j + side):
                total = total + mxu(vectors, piece)
        return total

    flat = loop(pairs, gradient, jnp.zeros((depth, queries), jnp.float32)).T
    sub = block // 2
    for h in range(2):
        lines = functools.reduce(
            jnp.add,
            [jnp.where(r == i, flat[h * half + i * sub : h * half + (i + 1) * sub], 0.0) for i in range(R)],
        )
        query_ref[h * sub : (h + 1) * sub, :] = functools.reduce(
            jnp.add, [jnp.where(c % per == i, lines[:, i * wide : (i + 1) * wide], 0.0) for i in range(per)]
        )
    grads = sum(mxu(piece, vectors_ref[...]) for piece in slope(c))
    passage_ref[...] = grads.T


def finish(t_mine, t_other, s, slope, mine, other, vectors, stats, wide):
    pairs, R, rows, span = mine.shape
    queries, depth = vectors.shape
    return pl.pallas_call(
        functools.partial(finish_kernel, wide),
        out_shape=(
            jax.ShapeDtypeStruct((queries // R, wide), jnp.float32),
            jax.ShapeDtypeStruct((depth, span), jnp.float32),
            jax.ShapeDtypeStruct((1, 1), jnp.float32),
        ),
        in_specs=[vmem()] * 8,
        out_specs=(vmem(),) * 3,
        scratch_shapes=[pltpu.VMEM((2 * pairs, span, queries), jnp.float32)],
        compiler_params=params(48),
    )(t_mine, t_other, s, slope, mine, other, vectors, stats)


def shards(query_tokens, query_lengths, passage_tokens, passage_lengths, student_queries, student_passages, positives):
    R, C = lax.axis_size("row"), lax.axis_size("col")
    block, slots, width = query_tokens.shape
    queries = block * R
    local, count = passage_tokens.shape[:2]
    wide = student_queries.shape[1]

    def over_row(x, k):
        return lax.ppermute(x, "row", [(i, i ^ k) for i in range(R)])

    def over_col(x, k):
        return lax.ppermute(x, "col", [(i, i ^ k) for i in range(C)])

    cells = passage_tokens.reshape(local * count // TILE, TILE, width)
    tokens = [cells, over_col(cells, 1)]
    sent = prepare(query_tokens, query_lengths, student_queries, student_passages.T, positives)
    near = [sent]
    for k in range(1, R):
        near.append(over_row(near[k & (k - 1)], k & -k))
    blocks = live_blocks(passage_lengths, count // TILE, sent)
    lists = [blocks, over_col(blocks, 1)]
    common = dict(tokens=tokens, lists=lists, queries=queries, passages=local)
    begun = teacher(slots, ((0, (0,)),), near=near, megabytes=56, **common)
    tokens[1], begun = lax.optimization_barrier((tokens[1], begun))
    common["near"] = near
    more = teacher(slots, ((1, (0,)),), **common)
    near[1], more = lax.optimization_barrier((near[1], more))
    score = teacher(slots, ((1, (1,)), (0, (1,))), priors=(more,), **common)
    base = sent.shape[0] - student_passages.shape[1] - block
    vectors, token = pack("row", near, base, sent.shape[0] - base, (score,))
    parts = {0: vectors}
    for k in range(2, C, 2):
        if k & (k - 1) == 0:
            parts[k] = over_col(vectors, k)
    priors = (score, begun)
    for k in range(2, R, 2):
        score = teacher(slots, ((0, (k, k + 1)), (1, (k, k + 1))), priors=priors, after=(token,), **common)
        priors = (score,)
    parts, score = lax.optimization_barrier((parts, score))
    for k in range(2, C, 2):
        if k not in parts:
            parts[k] = over_col(parts[k & (k - 1)], k & -k)
    stack, bit = score[None], 1
    while bit < R:
        stack, token = join(stack, over_row(stack, bit), 2 * bit == R)
        bit *= 2
    mine, _ = pack("col", [parts[k] for k in range(0, C, 2)], 0, R, (token,))
    other = over_col(mine, 1)
    t_mine, token = pack("col", [stack] + [over_col(stack, k) for k in range(2, C, 2)], 0, R, ())
    t_other = over_col(t_mine, 1)
    s, slope, vectors, stats = student_scores(mine, other, token, queries, wide)
    query_grads, passage_grads, loss = finish(t_mine, t_other, s, slope, mine, other, vectors, stats, wide)
    return (query_grads, passage_grads.T, loss[0, 0])


def solution(mesh):
    return jax.shard_map(
        shards,
        mesh=mesh,
        in_specs=(
            P("row", None, None),
            P("row"),
            P(("col", "row"), None, None),
            P(("col", "row")),
            P("row", "col"),
            P("col", "row"),
            P("row"),
        ),
        out_specs=(P("row", "col"), P("col", "row"), P()),
        check_vma=False,
    )
```
